32 devices in a mesh: rep: 2 (over y), fsdp: 16 (over z, x, core).
Axes of the slice: x: 2, y: 2, z: 4, core: 2. Of those that a mesh axis runs over, the one named last changes fastest.
Arguments:
- tokens: bfloat16 [16384, 768], P(('rep', 'fsdp')), may hold values from -6 to 6
- qkv_weight: bfloat16 [768, 2304], P(None, 'fsdp'), may hold values from -0.21875 to 0.21875
- qv_bias: bfloat16 [1536], P('fsdp'), may hold values from -1.796875 to 1.796875
- out_weight: bfloat16 [768, 768], P('fsdp'), may hold values from -0.875 to 0.875
- out_bias: bfloat16 [768], P('fsdp'), may hold values from -1.796875 to 1.796875
- norm1_gain: bfloat16 [768], P('fsdp'), may hold values from 0.5 to 1.5
- norm1_shift: bfloat16 [768], P('fsdp'), may hold values from -1.796875 to 1.796875
- ff_weight: bfloat16 [768, 6144], P(None, 'fsdp'), may hold values from -0.21875 to 0.21875
- ff_bias: bfloat16 [6144], P('fsdp'), may hold values from -1.796875 to 1.796875
- down_weight: bfloat16 [3072, 768], P('fsdp'), may hold values from -0.21875 to 0.21875
- down_bias: bfloat16 [768], P('fsdp'), may hold values from -1.796875 to 1.796875
- norm2_gain: bfloat16 [768], P('fsdp'), may hold values from 0.5 to 1.5
- norm2_shift: bfloat16 [768], P('fsdp'), may hold values from -1.796875 to 1.796875
- pair_length: int32 [32], P(('rep', 'fsdp')), may hold values from 256 to 512, as said below
- cotangent: bfloat16 [16384, 768], P(('rep', 'fsdp')), may hold values from -6 to 6
Outputs:
- output: bfloat16 [16384, 768], P(('rep', 'fsdp'))
- d_tokens: bfloat16 [16384, 768], P(('rep', 'fsdp'))
- d_qkv_weight: float32 [768, 2304], P(None, 'fsdp')
- d_qv_bias: float32 [1536], P('fsdp')
- d_out_weight: float32 [768, 768], P('fsdp')
- d_out_bias: float32 [768], P('fsdp')
- d_norm1_gain: float32 [768], P('fsdp')
- d_norm1_shift: float32 [768], P('fsdp')
- d_ff_weight: float32 [768, 6144], P(None, 'fsdp')
- d_ff_bias: float32 [6144], P('fsdp')
- d_down_weight: float32 [3072, 768], P('fsdp')
- d_down_bias: float32 [768], P('fsdp')
- d_norm2_gain: float32 [768], P('fsdp')
- d_norm2_shift: float32 [768], P('fsdp')
The draws below stay inside these ranges and needn't reach their ends.
Inputs may be any that keep to these rules, and one draw needn't show every extreme that they name: `pair_length`: sequence 0 always has all 512 slots real.
All inputs are finite; a program needn't handle non-finite values.
Results may differ from the reference program's by a relative error of at most 0.018.
Values may be sent and summed in bfloat16 or wider, within the bound.
A program may use at most 192 MiB of HBM per device.

```python
import jax
import jax.numpy as jnp
from jax import lax

D = 768
HEADS = 12
FF = 3072
SEQ = 512
SEQS = 32
TOKENS = 16384


def draw_pair_length(key, part):
    key = jax.random.fold_in(key, 7)
    lengths = jax.random.randint(key, (SEQS,), SEQ // 2, SEQ + 1)
    return lengths.at[0].set(SEQ)


def strengthened(array, stream_key, source, target, blocks, factor):
    owner, partner = [(jnp.arange(array.shape[axis_at]) // (array.shape[axis_at] // blocks)).reshape([-1 if axis == axis_at else 1 for axis in range(array.ndim)]) for axis_at in (source, target)]
    chosen = jax.random.permutation(stream_key, blocks)[partner]
    strong = (owner == chosen) | (owner == (partner + blocks // 2) % blocks)
    return jnp.where(strong, factor * array, array)


def levels(rng, extent, pieces, least, top_value):
    level, own = 1.0, jax.random.fold_in(rng, 6)
    for axis_at, blocks in pieces:
        heights = jnp.exp(jax.random.uniform(jax.random.fold_in(own, axis_at), (blocks,), jnp.float32, least / len(pieces), top_value / len(pieces)))
        level = level * jnp.repeat(heights, extent[axis_at] // blocks).reshape([-1 if axis == axis_at else 1 for axis in range(len(extent))])
    return level


def noise(key, shape, scale, limit, cuts=(), kind=jnp.bfloat16):
    array = jax.random.normal(key, shape, jnp.float32) * scale
    if len(cuts) > 0:
        array = levels(key, shape, cuts, -0.22, 0.18) * array
    return jnp.clip(array, min=-limit, max=limit).astype(kind)


def noise_with(own_key, dims, scale, most, split, heavy, kind=jnp.bfloat16):
    array = scale * jax.random.normal(own_key, dims, jnp.float32)
    if split:
        array = array * levels(own_key, dims, split, -0.22, 0.18)
    return jnp.clip(strengthened(array, jax.random.fold_in(own_key, 3), *heavy), -most, most).astype(kind)


def setup_inputs(seed: int = 0) -> dict:
    key_of = jax.random.split(jax.random.key(seed), 16)
    return {
        "tokens": noise(key_of[0], (TOKENS, D), 1.0, 6.0, ((0, 32),)),
        "qkv_weight": noise(key_of[1], (D, 3 * D), D ** -0.5, 0.21875, ((1, 16),)),
        "qv_bias": noise(key_of[2], (2 * D,), 0.3, 1.796875, ((0, 16),)),
        "out_weight": noise(key_of[3], (D, D), (D // 16) ** -0.5, 0.875, ((0, 16),)),
        "out_bias": noise(key_of[4], (D,), 0.3, 1.796875, ((0, 16),)),
        "norm1_gain": jnp.clip(1.0 + 0.1 * jax.random.normal(key_of[5], (D,), jnp.float32), 0.5, 1.5).astype(jnp.bfloat16),
        "norm1_shift": noise(key_of[6], (D,), 0.3, 1.796875, ((0, 16),)),
        "ff_weight": noise(key_of[7], (D, 2 * FF), D ** -0.5, 0.21875, ((1, 16),)),
        "ff_bias": noise(key_of[8], (2 * FF,), 0.3, 1.796875, ((0, 16),)),
        "down_weight": noise(key_of[9], (FF, D), (FF // 4) ** -0.5, 0.21875, ((0, 16),)),
        "down_bias": noise(key_of[10], (D,), 0.3, 1.796875, ((0, 16),)),
        "norm2_gain": jnp.clip(1.0 + 0.1 * jax.random.normal(key_of[11], (D,), jnp.float32), 0.5, 1.5).astype(jnp.bfloat16),
        "norm2_shift": noise(key_of[12], (D,), 0.3, 1.796875, ((0, 16),)),
        "pair_length": draw_pair_length(jax.random.fold_in(key_of[15], 71), 0),
        "cotangent": noise_with(key_of[14], (TOKENS, D), 1.0, 6.0, ((0, 32),), (0, 1, 32, 2.75)),
    }


@jax.custom_vjp
def low(v):
    return lax.optimization_barrier(v.astype(jnp.bfloat16)).astype(jnp.float32)

@jax.custom_vjp
def low_back(v):
    return v

def low_keep(v):
    return (low(v), None)

def low_pass(kept, grad):
    return (grad,)

def back_keep(v):
    return (v, None)

def back_low(kept, grad):
    return (low(grad),)
low.defvjp(low_keep, low_pass)
low_back.defvjp(back_keep, back_low)

def layer_norm(h, gain, shift):
    mean = lax.optimization_barrier(jnp.mean(h, -1, keepdims=True))
    centered = h - mean
    spread = lax.optimization_barrier(jnp.mean(centered * centered, -1, keepdims=True))
    return centered * lax.rsqrt(spread + 1e-05) * gain + shift

def project(left, weight):
    return jnp.einsum('gsd,de->gse', left, weight, precision=lax.Precision.HIGHEST)

def block(x, qkv_weight, qv_bias, out_weight, out_bias, gain1, shift1, ff_weight, ff_bias, down_weight, down_bias, gain2, shift2, valid):
    groups, length, width = x.shape
    heads = HEADS
    size = width // heads
    full_bias = jnp.concatenate([qv_bias[:width], jnp.zeros((width,), jnp.float32), qv_bias[width:]])
    qkv = low(low_back(project(x, qkv_weight) + full_bias))
    qkv = qkv.reshape(groups, length, 3, heads, size)
    query, keys, values = (qkv[:, :, 0], qkv[:, :, 1], qkv[:, :, 2])
    scores = jnp.einsum('gqhd,gkhd->ghqk', query, keys, precision=lax.Precision.HIGHEST) * 0.125
    place = jnp.arange(length, dtype=jnp.float32)
    slopes = 2.0 ** (-8.0 * jnp.arange(1, heads + 1, dtype=jnp.float32) / heads)
    distance = jnp.abs(place[:, None] - place[None, :])
    scores = low_back(scores - slopes[:, None, None] * distance)
    allowed = jnp.arange(length, dtype=jnp.int32)[None, :] < valid[:, None]
    scores = jnp.where(allowed[:, None, None, :], scores, -1e+30)
    probs = low(jax.nn.softmax(scores, axis=-1))
    context = jnp.einsum('ghqk,gkhd->gqhd', probs, values, precision=lax.Precision.HIGHEST)
    context = low(low_back(context.reshape(groups, length, width)))
    attended = low_back(project(context, out_weight) + out_bias)
    normed = layer_norm(x + attended, gain1, shift1)
    gate_up = low_back(project(low(normed), ff_weight) + ff_bias)
    half = ff_weight.shape[1] // 2
    hidden = low(low_back(jax.nn.gelu(gate_up[..., :half], approximate=False) * gate_up[..., half:]))
    branch = low_back(project(hidden, down_weight) + down_bias)
    return layer_norm(normed + branch, gain2, shift2)

def reference(tokens, qkv_weight, qv_bias, out_weight, out_bias, norm1_gain, norm1_shift, ff_weight, ff_bias, down_weight, down_bias, norm2_gain, norm2_shift, pair_length, cotangent):
    group = max(1, min(SEQS, 4096 // SEQ))
    count = SEQS // group
    params = tuple((p.astype(jnp.float32) for p in (qkv_weight, qv_bias, out_weight, out_bias, norm1_gain, norm1_shift, ff_weight, ff_bias, down_weight, down_bias, norm2_gain, norm2_shift)))
    inputs = tokens.astype(jnp.float32).reshape(count, group, SEQ, D)
    grads_in = cotangent.astype(jnp.float32).reshape(count, group, SEQ, D)
    lengths = pair_length.reshape(count, group)

    def step(carry, item):
        x, grad_out, valid = item

        def apply(x, *weights):
            return block(x, *weights, valid)
        out, back = jax.vjp(apply, x, *params)
        grads = back(grad_out)
        carry = tuple((c + g for c, g in zip(carry, grads[1:])))
        return (carry, (out.astype(jnp.bfloat16), grads[0].astype(jnp.bfloat16)))
    start = tuple((jnp.zeros_like(p) for p in params))
    sums, (outs, d_inputs) = lax.scan(step, start, (inputs, grads_in, lengths))
    return (outs.reshape(TOKENS, D), d_inputs.reshape(TOKENS, D), sums[0], sums[1], sums[2], sums[3], sums[4], sums[5], sums[6], sums[7], sums[8], sums[9], sums[10], sums[11])
```

```python
import functools

import jax
import jax.numpy as jnp
from jax import lax
from jax.experimental import pallas as pl
from jax.experimental.pallas import tpu as pltpu
from jax.sharding import PartitionSpec as P

HEADS = 12
MESH = pl.DeviceIdType.MESH
BF = jnp.bfloat16
F32 = jnp.float32


def layer_norm(h, gain, shift):
    mean = jnp.mean(h, -1, keepdims=True)
    centered = h - mean
    spread = jnp.mean(centered * centered, -1, keepdims=True)
    return centered * lax.rsqrt(spread + 1e-05) * gain + shift


def inner_rows(left, right):
    return lax.dot_general(
        left, right, (((0,), (0,)), ((), ())), preferred_element_type=jnp.float32
    )


def times_transposed(left, right):
    return lax.dot_general(
        left, right, (((1,), (1,)), ((), ())), preferred_element_type=jnp.float32
    )


def score_block(query, keys, slope, valid):
    length = query.shape[0]
    place = jnp.arange(length, dtype=jnp.float32)
    scores = times_transposed(query, keys) * 0.125 - slope * jnp.abs(
        place[:, None] - place[None, :]
    )
    allowed = jnp.arange(length, dtype=jnp.int32) < valid
    return jnp.where(allowed[None, :], scores, -1e30)


def head_slopes():
    return 2.0 ** (-8.0 * jnp.arange(1, HEADS + 1, dtype=jnp.float32) / HEADS)


def forward(tokens, attention, feedforward, valid):
    qkv_weight, qv_bias, out_weight, out_bias, gain1, shift1 = attention
    ff_weight, ff_bias, down_weight, down_bias, gain2, shift2 = feedforward
    length, width = tokens.shape
    bias_f = qv_bias.astype(jnp.float32)
    full_bias = jnp.concatenate([bias_f[:width], jnp.zeros((width,), jnp.float32), bias_f[width:]])
    qkv = (jnp.dot(tokens, qkv_weight, preferred_element_type=jnp.float32) + full_bias).astype(
        jnp.bfloat16
    )
    per_head = qkv.reshape(length, 3, HEADS, width // HEADS).transpose(1, 2, 0, 3)

    def attend(item):
        query, keys, values, slope = item
        scores = score_block(query, keys, slope, valid)
        top = jnp.max(scores, -1, keepdims=True)
        expo = jnp.exp(scores - top)
        total = jnp.sum(expo, -1, keepdims=True)
        probs = (expo / total).astype(jnp.bfloat16)
        return (
            jnp.dot(probs, values, preferred_element_type=jnp.float32),
            top[:, 0] + jnp.log(total[:, 0]),
        )

    context, log_total = lax.map(attend, (per_head[0], per_head[1], per_head[2], head_slopes()))
    context = context.transpose(1, 0, 2).reshape(length, width).astype(jnp.bfloat16)
    attended = jnp.dot(context, out_weight, preferred_element_type=jnp.float32) + out_bias.astype(
        jnp.float32
    )
    residual1 = tokens.astype(jnp.float32) + attended
    normed = layer_norm(residual1, gain1.astype(jnp.float32), shift1.astype(jnp.float32))
    normed_low = normed.astype(jnp.bfloat16)
    gate_up = jnp.dot(normed_low, ff_weight, preferred_element_type=jnp.float32) + ff_bias.astype(
        jnp.float32
    )
    half = gate_up.shape[1] // 2
    hidden = (jax.nn.gelu(gate_up[:, :half], approximate=False) * gate_up[:, half:]).astype(
        jnp.bfloat16
    )
    residual2 = (
        normed
        + jnp.dot(hidden, down_weight, preferred_element_type=jnp.float32)
        + down_bias.astype(jnp.float32)
    )
    return (per_head, log_total, context, residual1, normed_low, gate_up, hidden, residual2)


def gelu_product(gate, up):
    return jax.nn.gelu(gate, approximate=False) * up


def plain_on_device(
    tokens,
    qkv_weight,
    qv_bias,
    out_weight,
    out_bias,
    norm1_gain,
    norm1_shift,
    ff_weight,
    ff_bias,
    down_weight,
    down_bias,
    norm2_gain,
    norm2_shift,
    pair_length,
    cotangent,
):
    valid = pair_length[0]
    attention = (
        lax.all_gather(qkv_weight, "fsdp", axis=1, tiled=True),
        lax.all_gather(qv_bias, "fsdp", axis=0, tiled=True),
        lax.all_gather(out_weight, "fsdp", axis=0, tiled=True),
        lax.all_gather(out_bias, "fsdp", axis=0, tiled=True),
        lax.all_gather(norm1_gain, "fsdp", axis=0, tiled=True),
        lax.all_gather(norm1_shift, "fsdp", axis=0, tiled=True),
    )
    feedforward = (
        lax.all_gather(ff_weight, "fsdp", axis=1, tiled=True),
        lax.all_gather(ff_bias, "fsdp", axis=0, tiled=True),
        lax.all_gather(down_weight, "fsdp", axis=0, tiled=True),
        lax.all_gather(down_bias, "fsdp", axis=0, tiled=True),
        lax.all_gather(norm2_gain, "fsdp", axis=0, tiled=True),
        lax.all_gather(norm2_shift, "fsdp", axis=0, tiled=True),
    )
    stored = forward(tokens, attention, feedforward, valid)
    gain2 = feedforward[4].astype(jnp.float32)
    shift2 = feedforward[5].astype(jnp.float32)
    output = layer_norm(stored[7], gain2, shift2).astype(jnp.bfloat16)
    per_head, log_total, context, residual1, normed_low, gate_up, hidden, residual2 = stored
    full_qkv, bias_unused, full_out, out_unused, gain1, shift1 = attention
    full_ff, ff_unused, full_down, down_unused, gain_unused, shift_unused = feedforward
    length, width = tokens.shape
    unused_out, back_second = jax.vjp(layer_norm, residual2, gain2, shift2)
    d_res2, d_gain2, d_shift2 = back_second(cotangent.astype(jnp.float32))
    d_branch = d_res2.astype(jnp.bfloat16)
    d_down = inner_rows(hidden, d_branch)
    d_down_bias = jnp.sum(d_branch.astype(jnp.float32), 0)
    d_hidden = times_transposed(d_branch, full_down).astype(jnp.bfloat16)
    half = gate_up.shape[1] // 2
    unused_prod, back_gelu = jax.vjp(gelu_product, gate_up[:, :half], gate_up[:, half:])
    d_gate, d_up = back_gelu(d_hidden.astype(jnp.float32))
    d_gate_up = jnp.concatenate([d_gate, d_up], 1).astype(jnp.bfloat16)
    d_ff = inner_rows(normed_low, d_gate_up)
    d_ff_bias = jnp.sum(d_gate_up.astype(jnp.float32), 0)
    d_normed = times_transposed(d_gate_up, full_ff) + d_res2
    unused_norm, back_first = jax.vjp(
        layer_norm, residual1, gain1.astype(jnp.float32), shift1.astype(jnp.float32)
    )
    d_res1, d_gain1, d_shift1 = back_first(d_normed)
    ff_terms = (d_ff, d_ff_bias, d_down, d_down_bias, d_gain2, d_shift2)
    ff_grads = (
        lax.psum_scatter(ff_terms[0], "fsdp", scatter_dimension=1, tiled=True),
        lax.psum_scatter(ff_terms[1], "fsdp", scatter_dimension=0, tiled=True),
        lax.psum_scatter(ff_terms[2], "fsdp", scatter_dimension=0, tiled=True),
        lax.psum_scatter(ff_terms[3], "fsdp", scatter_dimension=0, tiled=True),
        lax.psum_scatter(ff_terms[4], "fsdp", scatter_dimension=0, tiled=True),
        lax.psum_scatter(ff_terms[5], "fsdp", scatter_dimension=0, tiled=True),
    )
    ff_grads = (
        lax.psum(ff_grads[0].astype(jnp.bfloat16), "rep").astype(jnp.float32),
        lax.psum(ff_grads[1].astype(jnp.bfloat16), "rep").astype(jnp.float32),
        lax.psum(ff_grads[2].astype(jnp.bfloat16), "rep").astype(jnp.float32),
        lax.psum(ff_grads[3].astype(jnp.bfloat16), "rep").astype(jnp.float32),
        lax.psum(ff_grads[4].astype(jnp.bfloat16), "rep").astype(jnp.float32),
        lax.psum(ff_grads[5].astype(jnp.bfloat16), "rep").astype(jnp.float32),
    )
    d_attended = d_res1.astype(jnp.bfloat16)
    d_out = inner_rows(context, d_attended)
    d_out_bias = jnp.sum(d_attended.astype(jnp.float32), 0)
    d_context = times_transposed(d_attended, full_out).astype(jnp.bfloat16)
    d_context = d_context.reshape(length, HEADS, width // HEADS).transpose(1, 0, 2)

    def attend_back(item):
        query, keys, values, grad_context, total_log, slope = item
        scores = score_block(query, keys, slope, valid)
        probs = jnp.exp(scores - total_log[:, None])
        probs_low = probs.astype(jnp.bfloat16)
        d_probs = times_transposed(grad_context, values)
        d_scores = (probs * (d_probs - jnp.sum(probs * d_probs, -1, keepdims=True))).astype(
            jnp.bfloat16
        )
        d_query = jnp.dot(d_scores, keys, preferred_element_type=jnp.float32) * 0.125
        d_keys = inner_rows(d_scores, query) * 0.125
        d_values = inner_rows(probs_low, grad_context)
        return (d_query, d_keys, d_values)

    d_query, d_keys, d_values = lax.map(
        attend_back, (per_head[0], per_head[1], per_head[2], d_context, log_total, head_slopes())
    )
    d_qkv = (
        jnp.stack([d_query, d_keys, d_values])
        .transpose(2, 0, 1, 3)
        .reshape(length, 3 * width)
        .astype(jnp.bfloat16)
    )
    d_qkv_w = inner_rows(tokens, d_qkv)
    column_sums = jnp.sum(d_qkv.astype(jnp.float32), 0)
    d_qv = jnp.concatenate([column_sums[:width], column_sums[2 * width :]])
    d_tokens = (times_transposed(d_qkv, full_qkv) + d_res1).astype(jnp.bfloat16)
    at_terms = (d_qkv_w, d_qv, d_out, d_out_bias, d_gain1, d_shift1)
    at_grads = (
        lax.psum_scatter(at_terms[0], "fsdp", scatter_dimension=1, tiled=True),
        lax.psum_scatter(at_terms[1], "fsdp", scatter_dimension=0, tiled=True),
        lax.psum_scatter(at_terms[2], "fsdp", scatter_dimension=0, tiled=True),
        lax.psum_scatter(at_terms[3], "fsdp", scatter_dimension=0, tiled=True),
        lax.psum_scatter(at_terms[4], "fsdp", scatter_dimension=0, tiled=True),
        lax.psum_scatter(at_terms[5], "fsdp", scatter_dimension=0, tiled=True),
    )
    at_grads = (
        lax.psum(at_grads[0].astype(jnp.bfloat16), "rep").astype(jnp.float32),
        lax.psum(at_grads[1].astype(jnp.bfloat16), "rep").astype(jnp.float32),
        lax.psum(at_grads[2].astype(jnp.bfloat16), "rep").astype(jnp.float32),
        lax.psum(at_grads[3].astype(jnp.bfloat16), "rep").astype(jnp.float32),
        lax.psum(at_grads[4].astype(jnp.bfloat16), "rep").astype(jnp.float32),
        lax.psum(at_grads[5].astype(jnp.bfloat16), "rep").astype(jnp.float32),
    )
    return (
        output,
        d_tokens,
        at_grads[0],
        at_grads[1],
        at_grads[2],
        at_grads[3],
        at_grads[4],
        at_grads[5],
        ff_grads[0],
        ff_grads[1],
        ff_grads[2],
        ff_grads[3],
        ff_grads[4],
        ff_grads[5],
    )


def dot(left, right, left_dim, right_dim):
    return lax.dot_general(
        left, right, (((left_dim,), (right_dim,)), ((), ())), preferred_element_type=F32
    )


def whereabouts():
    y = lax.axis_index("rep")
    k = lax.axis_index("fsdp")
    return y, k // 4, (k // 2) % 2, k % 2


def index(z, x, c):
    return z * 4 + x * 2 + c


def greet():
    y, z, x, c = whereabouts()
    friends = [(y, index(z, x, 1 - c)), (y, index(z, 1 - x, c)), (1 - y, index(z, x, c))]
    friends += [(y, index((z + d) % 4, x, c)) for d in (1, 2, 3)]
    barrier = pltpu.get_barrier_semaphore()
    for friend in friends:
        pl.semaphore_signal(barrier, inc=1, device_id=friend, device_id_type=MESH)
    pl.semaphore_wait(barrier, len(friends))


class Gather:
    Z, X, Y, D, C = 0, 3, 7, 10, 14
    SLOTS = 22

    def __init__(self, t, src, dst, rows, by_row, sends, recvs, locals_):
        self.t, self.src, self.dst, self.rows, self.by_row = t, src, dst, rows, by_row
        self.sends, self.recvs, self.locals_ = sends, recvs, locals_
        self.y, self.z, self.x, self.c = whereabouts()

    def plane(self, i):
        return (self.z + i) % 4

    def half(self, ref, base, h):
        if self.by_row:
            n = self.rows // 2
            return ref.at[pl.ds(pl.multiple_of(base + h * n, 16), n), :]
        n = ref.shape[1] // 2
        return ref.at[pl.ds(base, self.rows), pl.ds(pl.multiple_of(h * n, 128), n)]

    def part(self, k, h):
        return self.half(self.dst, pl.multiple_of(k * self.rows, 16), h)

    def shard(self, k):
        return self.dst.at[pl.ds(pl.multiple_of(k * self.rows, 16), self.rows), :]

    def copy(self, slot, src, dst, device):
        return pltpu.make_async_remote_copy(
            src_ref=src,
            dst_ref=dst,
            send_sem=self.sends.at[self.t, slot],
            recv_sem=self.recvs.at[self.t, slot],
            device_id=device,
            device_id_type=MESH,
        )

    def to_plane(self, d):
        k = index(self.z, self.x, self.c)
        device = (self.y, index((self.z + d) % 4, self.x, self.c))
        return self.copy(self.Z + d - 1, self.half(self.src, 0, self.y), self.part(k, self.y), device)

    def to_x(self, i):
        k = index(self.plane(i), self.x, self.c)
        src = self.half(self.src, 0, self.y) if i == 0 else self.part(k, self.y)
        return self.copy(
            self.X + i, src, self.part(k, self.y), (self.y, index(self.z, 1 - self.x, self.c))
        )

    def to_y(self, i):
        k = index(self.plane(i), self.x, self.c)
        part = self.part(k, self.y)
        return self.copy(self.Y + i - 1, part, part, (1 - self.y, index(self.z, self.x, self.c)))

    def onward(self, i):
        c = 0 if i == 0 else self.c
        k = index(self.plane(i), (1 - self.x) * (1 - c) + self.x * c, self.c)
        part = self.part(k, self.y * (1 - c) + (1 - self.y) * c)
        x = self.x * (1 - c) + (1 - self.x) * c
        y = self.y * c + (1 - self.y) * (1 - c)
        return self.copy(self.D + i, part, part, (y, index(self.z, x, self.c)))

    def to_core(self, i, home):
        k = index(self.plane(i), self.x if home else 1 - self.x, self.c)
        src = self.src if home and i == 0 else self.shard(k)
        device = (self.y, index(self.z, self.x, 1 - self.c))
        return self.copy(self.C + i + (0 if home else 4), src, self.shard(k), device)

    def own(self):
        return pltpu.make_async_copy(
            self.src, self.shard(index(self.z, self.x, self.c)), self.locals_.at[self.t]
        )

    def begin(self):
        for d in (1, 3, 2):
            self.to_plane(d).start()
        self.to_x(0).start()
        self.to_core(0, True).start()
        self.own().start()

    def second(self, i):
        if i:
            self.to_plane(4 - i).wait_recv()
            self.to_x(i).start()
            self.to_y(i).start()

    def third(self, i):
        if i:
            self.to_y(i).wait_recv()
            self.to_core(i, True).start()
        self.to_x(i).wait_recv()
        self.onward(i).start()

    def fourth(self, i):
        self.onward(i).wait_recv()
        self.to_core(i, False).start()

    def arrived(self, i):
        self.to_core(i, True).wait_recv()
        self.to_core(i, False).wait_recv()
        if i == 0:
            self.own().wait()

    def finish(self):
        for d in (1, 2, 3):
            self.to_plane(d).wait_send()
        for i in range(4):
            self.to_x(i).wait_send()
            if i:
                self.to_y(i).wait_send()
            self.onward(i).wait_send()
            self.to_core(i, True).wait_send()
            self.to_core(i, False).wait_send()


def slope_of(head):
    return jnp.exp2(jnp.full((1, 1), head + 1, jnp.int32).astype(F32) * (-8.0 / HEADS))


def normalise(h):
    centered = h - jnp.mean(h, -1, keepdims=True)
    inverse = lax.rsqrt(jnp.mean(centered * centered, -1, keepdims=True) + 1e-05)
    return centered * inverse, inverse


def norm_back(d_scaled, scaled, inverse):
    mean1 = jnp.mean(d_scaled, -1, keepdims=True)
    mean2 = jnp.mean(d_scaled * scaled, -1, keepdims=True)
    return inverse * (d_scaled - mean1 - scaled * mean2)


def column_sum(v):
    return jnp.sum(v, axis=0, keepdims=True)


def cdf(gate):
    return 0.5 * (1.0 + lax.erf(gate * 0.7071067811865476))


def bias_at(j):
    return pl.ds(8 + j // 2, 1), pl.ds(pl.multiple_of((j % 2) * 384, 128), 384)


def forward_kernel(
    tok, cot, valid, s_bias, s_qkv, s_out, s_ff, s_down,
    o_out, o_qkvw, o_outw, o_ffw, o_downw, o_rows, o_sums, o_qkv, o_ctx, o_probs, o_nlt, o_scaled1,
    o_inv1, o_gu, o_hid, o_dh2, o_db,
    w_bias, w_qkv, w_out, w_ff, w_down, v_dist, v_qkv, v_ctx, v_probs, v_scaled1, v_nl, v_gu,
    v_hid, v_acc, v_nlt, sends, recvs, locals_, outs,
):
    places = [w_bias, w_qkv, w_out, w_ff, w_down]
    shards = [s_bias, s_qkv, s_out, s_ff, s_down]
    g = [
        Gather(t, shards[t], places[t], shards[t].shape[0], t == 3, sends, recvs, locals_)
        for t in range(5)
    ]
    y, z, x, c = whereabouts()
    greet()
    for t in range(5):
        g[t].begin()
    items = [(t, 0) for t in range(5)] + [(t, i) for t in range(5) for i in (3, 1, 2)]

    def service(s):
        if s < len(items):
            g[items[s][0]].second(items[s][1])
        if 0 <= s - 2 < len(items):
            g[items[s - 2][0]].third(items[s - 2][1])
        if 0 <= s - 4 < len(items):
            g[items[s - 4][0]].fourth(items[s - 4][1])

    pending = []

    def save(src, dst):
        copy = pltpu.make_async_copy(src, dst, outs.at[len(pending)])
        copy.start()
        pending.append(copy)

    length = tok.shape[0]
    j = lax.broadcasted_iota(jnp.int32, (length, length), 0)
    i = lax.broadcasted_iota(jnp.int32, (length, length), 1)
    v_dist[...] = jnp.where(j < valid[0], jnp.abs(i - j).astype(F32), 1e33)

    for s in range(15):
        service(s)
    for i in range(4):
        g[0].arrived(i)
        g[1].arrived(i)

    rows = w_bias[0:16, :].astype(F32)
    for k in range(1, 16):
        rows = rows + w_bias[16 * k : 16 * k + 16, :].astype(F32)
    o_rows[...] = rows

    for n in range(3):
        part = dot(tok[...], w_qkv[768 * n : 768 * n + 768, :], 1, 1)
        if n == 0:
            part = (part + rows[0:1, :]).astype(BF).astype(F32) * 0.125
        if n == 2:
            part = part + rows[1:2, :]
        v_qkv[:, 768 * n : 768 * n + 768] = part.astype(BF)
    save(v_qkv, o_qkv)
    save(w_qkv, o_qkvw)

    lane = lax.broadcasted_iota(jnp.int32, (1, 128), 1)

    def attend(pair):
        col = 128 * pair
        k_pair = v_qkv[:, 768 + col : 768 + col + 128]
        v_pair = v_qkv[:, 1536 + col : 1536 + col + 128]

        def one(chunk, carry):
            at = pl.multiple_of(chunk * 256, 256)
            results = []
            for hh in range(2):
                mine = (lane < 64) if hh == 0 else (lane >= 64)
                q_head = jnp.where(mine, v_qkv[pl.ds(at, 256), col : col + 128], jnp.zeros((), BF))
                scores = dot(k_pair, q_head, 1, 1)
                scores = scores - slope_of(2 * pair + hh) * v_dist[:, pl.ds(at, 256)]
                expo = jnp.exp(scores - jnp.max(scores, axis=0, keepdims=True))
                probs = (expo * (1.0 / jnp.sum(expo, axis=0, keepdims=True))).astype(BF)
                v_probs[2 * pair + hh, :, pl.ds(at, 256)] = probs
                results.append(dot(probs, v_pair, 0, 0))
            v_ctx[pl.ds(at, 256), col : col + 128] = jnp.where(
                lane < 64, results[0], results[1]
            ).astype(BF)
            return carry

        lax.fori_loop(0, length // 256, one, 0)

    for pair in range(6):
        service(15 + pair)
        attend(pair)
        save(v_probs.at[pl.ds(2 * pair, 2)], o_probs.at[pl.ds(2 * pair, 2)])
    service(21)
    save(v_ctx, o_ctx)

    for i in range(4):
        g[2].arrived(i)
    save(w_out, o_outw)
    h1 = dot(v_ctx[...], w_out[...], 1, 0) + rows[2:3, :] + tok[...].astype(F32)
    scaled1, inverse1 = normalise(h1)
    v_scaled1[...] = scaled1
    o_inv1[...] = jnp.broadcast_to(inverse1, o_inv1.shape)
    normed = scaled1 * rows[3:4, :] + rows[4:5, :]
    v_acc[...] = normed + rows[5:6, :]
    v_nl[...] = normed.astype(BF)
    v_nlt[...] = normed.astype(BF).T
    save(v_scaled1, o_scaled1)
    save(v_nlt, o_nlt)

    def feed(j):
        gate = dot(v_nl[...], w_ff[pl.ds(pl.multiple_of(j * 768, 768), 768), :], 1, 0)
        up = dot(v_nl[...], w_ff[pl.ds(pl.multiple_of((8 + j) * 768, 768), 768), :], 1, 0)
        gate = gate + o_rows[bias_at(j)]
        up = up + o_rows[bias_at(8 + j)]
        v_gu[0, j] = gate.astype(BF)
        v_gu[1, j] = up.astype(BF)
        v_hid[j] = (gate * cdf(gate) * up).astype(BF)

    def feed_four(first):
        def one(s, carry):
            feed(first + s)
            return carry

        lax.fori_loop(0, 4, one, 0)

    for i in (1, 3):
        g[3].arrived(i)
    feed_four(4 * ((z + 1) % 2))
    service(22)
    for i in (0, 2):
        g[3].arrived(i)
    feed_four(4 * (z % 2))
    service(23)
    save(w_ff, o_ffw)
    save(v_gu, o_gu)
    save(v_hid, o_hid)
    for i in range(4):
        g[4].arrived(i)
    save(w_down, o_downw)

    def down(j, carry):
        rows_j = pl.ds(pl.multiple_of(j * 384, 384), 384)
        v_acc[...] += dot(v_hid[j], w_down[rows_j, :], 1, 0)
        return carry

    lax.fori_loop(0, 8, down, 0)
    scaled2, inverse2 = normalise(v_acc[...])
    o_out[...] = (scaled2 * rows[6:7, :] + rows[7:8, :]).astype(BF)
    grad = cot[...].astype(F32)
    d_h2 = norm_back(grad * rows[6:7, :], scaled2, inverse2)
    o_dh2[...] = d_h2
    o_db[...] = d_h2.astype(BF)
    o_sums[...] = jnp.zeros_like(o_sums)
    o_sums[0:1, :] = column_sum(d_h2.astype(BF).astype(F32))
    o_sums[1:2, :] = column_sum(grad * scaled2)
    o_sums[2:3, :] = column_sum(grad)
    for t in range(5):
        g[t].finish()
    for copy in pending:
        copy.wait()


class Reduce:
    def __init__(self, t, base, rows, planes, at, full, both, across, sides, columns, sends, recvs):
        self.t, self.base, self.rows, self.planes, self.at = t, base, rows, planes, at
        self.full, self.both, self.across, self.sides, self.columns = full, both, across, sides, columns
        self.sends, self.recvs = sends, recvs
        self.y, self.z, self.x, self.c = whereabouts()

    def copy(self, slot, src, dst, device):
        return pltpu.make_async_remote_copy(
            src_ref=src,
            dst_ref=dst,
            send_sem=self.sends.at[self.t, slot],
            recv_sem=self.recvs.at[self.t, slot],
            device_id=device,
            device_id_type=MESH,
        )

    def unit(self, i, away_x, c, h):
        x = 1 - self.x if away_x else self.x
        row = self.at(self.z, (self.z + i) % 4, x, c, h)
        return self.full.at[pl.ds(pl.multiple_of(row, 16), self.rows), :]

    def mine(self, i, away_x, away_h):
        n = i * 4 + away_x * 2 + away_h
        return self.both.at[pl.ds(pl.multiple_of(self.base * 16 + n * self.rows, 16), self.rows), :]

    def side(self, i, s):
        return self.sides.at[pl.ds(self.base * 8 + (i * 2 + s) * self.rows, self.rows), :]

    def cross(self, i):
        return self.across.at[pl.ds(self.base * 4 + i * self.rows, self.rows), :]

    def column(self, n):
        return self.columns.at[pl.ds(self.base * 5 + n * self.rows, self.rows), :]

    def way(self, i):
        return 1 if i == 0 else self.c

    def neighbour(self, over_x):
        return (
            self.y * over_x + (1 - self.y) * (1 - over_x),
            index(self.z, (1 - self.x) * over_x + self.x * (1 - over_x), self.c),
        )

    def to_core(self, i, n):
        device = (self.y, index(self.z, self.x, 1 - self.c))
        away_x, away_h = n // 2, n % 2
        h = 1 - self.y if away_h else self.y
        src = self.unit(i, away_x, 1 - self.c, h)
        return self.copy(i * 8 + n, src, self.mine(i, away_x, away_h), device)

    def diagonal(self, i):
        return self.copy(i * 8 + 4, self.mine(i, 1, 1), self.cross(i), self.neighbour(self.way(i)))

    def early(self, i):
        w = self.way(i)
        return self.copy(i * 8 + 5, self.mine(i, w, 1 - w), self.side(i, 0), self.neighbour(w))

    def late(self, i):
        w = self.way(i)
        return self.copy(i * 8 + 6, self.mine(i, 1 - w, w), self.side(i, 1), self.neighbour(1 - w))

    def to_plane(self, i):
        device = (self.y, index((self.z + i) % 4, self.x, self.c))
        return self.copy(i * 8 + 7, self.mine(i, 0, 0), self.column(i - 1), device)

    def to_y(self):
        device = (1 - self.y, index(self.z, self.x, self.c))
        return self.copy(7, self.column(3), self.column(4), device)

    def first(self, i):
        for n in (3, 2, 1, 0):
            self.to_core(i, n).start()

    def second(self, i):
        for n in (3, 2, 1, 0):
            self.to_core(i, n).wait()
            h = 1 - self.y if n % 2 else self.y
            part = self.mine(i, n // 2, n % 2)
            part[...] = part[...] + self.unit(i, n // 2, self.c, h)[...]
            if n == 3:
                self.diagonal(i).start()
        self.early(i).start()

    def third(self, i):
        w = self.way(i)
        self.diagonal(i).wait_recv()
        part = self.mine(i, 1 - w, w)
        part[...] = part[...] + self.cross(i)[...]
        self.late(i).start()

    def fourth(self, i):
        self.early(i).wait_recv()
        self.late(i).wait_recv()
        part = self.mine(i, 0, 0)
        total = part[...].astype(F32) + self.side(i, 0)[...].astype(F32)
        part[...] = (total + self.side(i, 1)[...].astype(F32)).astype(BF)
        if i:
            self.to_plane(i).start()

    def arrive(self, i):
        if i:
            self.to_plane(i).wait_recv()

    def fifth(self):
        total = self.mine(0, 0, 0)[...].astype(F32)
        for n in range(3):
            total = total + self.column(n)[...].astype(F32)
        self.column(3)[...] = total.astype(BF)
        self.to_y().start()

    def finish(self):
        for i in self.planes:
            self.diagonal(i).wait_send()
            self.early(i).wait_send()
            self.late(i).wait_send()
            if i:
                self.to_plane(i).wait_send()


def backward_kernel(
    tok, qkv, ctx, nlt, db, rows, sums, inv1, w_qkv, w_out, w_ff, w_down, scaled1, dh2, probs, gu, hid,
    o_tok, o_qkv, o_out, o_ff, o_down, o_rows,
    v_qkvw, v_outw, v_ffw, v_downw, v_scaled1, v_dn, v_probs, v_gu, v_hid, full_a, full_b, both, across,
    sides, columns, v_dctx, v_dqkv, v_sum, v_sums, sends, recvs, row_sends, row_recvs, loads, stages,
):
    y, z, x, c = whereabouts()
    length = tok.shape[0]
    one_load = [
        (w_out, v_outw), (w_qkv, v_qkvw), (scaled1, v_scaled1), (dh2, v_dn),
    ]

    def load(n):
        return pltpu.make_async_copy(one_load[n][0], one_load[n][1], loads.at[n])

    def stage(kind, src, dst, slot):
        return pltpu.make_async_copy(src, dst, stages.at[kind, slot])

    def hid_stage(n):
        return stage(0, hid.at[(2 * z + n) % 8], v_hid.at[n % 2], n % 2)

    def chunk_of(n):
        half = (z + 1) % 2 if n < 4 else z % 2
        return 4 * half + n % 4

    def ff_stages(n):
        j = chunk_of(n)
        s = n % 2
        rows_g = pl.ds(pl.multiple_of(j * 768, 768), 768)
        rows_u = pl.ds(pl.multiple_of((8 + j) * 768, 768), 768)
        rows_d = pl.ds(pl.multiple_of(j * 384, 384), 384)
        return [
            stage(1, w_ff.at[rows_g, :], v_ffw.at[s, 0], s),
            stage(2, w_ff.at[rows_u, :], v_ffw.at[s, 1], s),
            stage(3, w_down.at[rows_d, :], v_downw.at[s], s),
            stage(4, gu.at[0, j], v_gu.at[s, 0], s),
            stage(5, gu.at[1, j], v_gu.at[s, 1], s),
        ]

    def probs_stage(pair):
        return stage(6, probs.at[pl.ds(2 * pair, 2)], v_probs.at[pair % 2], pair % 2)

    hid_stage(0).start()
    hid_stage(1).start()
    for copy in ff_stages(0) + ff_stages(1):
        copy.start()
    load(3).start()

    def at_down(z_, plane, x_, c_, h):
        return h * 3072 + index(plane, x_, c_) * 192

    def at_ff(z_, plane, x_, c_, h):
        return (plane // 2) * 3072 + index(0, x_, c_) * 768 + h * 384

    def at_out(z_, plane, x_, c_, h):
        return h * 768 + index(plane, x_, c_) * 48

    def at_qkv(z_, plane, x_, c_, h):
        return 1536 + h * 2304 + index(plane, x_, c_) * 144

    every = (0, 1, 2, 3)
    shared = (both, across, sides, columns, sends, recvs)
    r_down = Reduce(0, 0, 192, every, at_down, full_a, *shared)
    r_ff1 = Reduce(1, 192, 384, (1, 3), at_ff, full_b, *shared)
    r_ff2 = Reduce(1, 192, 384, (0, 2), at_ff, full_a, *shared)
    r_out = Reduce(2, 576, 48, every, at_out, full_b, *shared)
    r_qkv = Reduce(3, 624, 144, every, at_qkv, full_b, *shared)
    greet()

    items = [(r_down, i) for i in (1, 3, 2, 0)] + [(r_ff1, 1), (r_ff1, 3), (r_ff2, 2), (r_ff2, 0)]
    items += [(r_out, i) for i in (1, 3, 2, 0)] + [(r_qkv, i) for i in (1, 3, 2, 0)]

    def first(r):
        for i in r.planes:
            r.first(i)

    def second(*ns):
        for n in ns:
            items[n][0].second(items[n][1])

    def third(*ns):
        for n in ns:
            items[n][0].third(items[n][1])

    def fourth(*ns):
        for n in ns:
            items[n][0].fourth(items[n][1])

    def fifth(r):
        for i in (1, 2, 3):
            r.arrive(i)
        r.fifth()

    d_branch = db[...]
    for n in range(8):
        hid_stage(n).wait()
        part = dot(v_hid[n % 2], d_branch, 0, 0)
        row = pl.multiple_of(((2 * z + n) % 8) * 384, 384)
        full_a[pl.ds(row, 384), :] = part[:, :384].astype(BF)
        full_a[pl.ds(3072 + row, 384), :] = part[:, 384:].astype(BF)
        if n < 6:
            hid_stage(n + 2).start()
        if n % 2:
            r_down.first(n // 2)

    def chunk(n):
        s = n % 2
        j = chunk_of(n)
        for copy in ff_stages(n):
            copy.wait()
        d_hid = dot(db[...], v_downw[s], 1, 1).astype(BF).astype(F32)
        gate = v_gu[s, 0].astype(F32)
        up = v_gu[s, 1].astype(F32)
        below = cdf(gate)
        density = jnp.exp(-0.5 * gate * gate) * 0.3989422804014327
        d_gate = (d_hid * up * (below + gate * density)).astype(BF)
        d_up = (d_hid * (gate * below)).astype(BF)
        full = full_b if n < 4 else full_a
        full[pl.ds(768 * (n % 4), 768), :] = dot(nlt[...], d_gate, 1, 0).astype(BF)
        full[pl.ds(3072 + 768 * (n % 4), 768), :] = dot(nlt[...], d_up, 1, 0).astype(BF)
        v_sum[bias_at(j)] = column_sum(d_gate.astype(F32))
        v_sum[bias_at(8 + j)] = column_sum(d_up.astype(F32))
        v_dn[...] += dot(d_gate, v_ffw[s, 0], 1, 1) + dot(d_up, v_ffw[s, 1], 1, 1)
        if n < 6:
            for copy in ff_stages(n + 2):
                copy.start()

    load(3).wait()
    load(2).start()
    load(0).start()
    load(1).start()
    chunk(0)
    second(0)
    chunk(1)
    second(1)
    chunk(2)
    second(2)
    third(0)
    chunk(3)
    second(3)
    third(1)
    first(r_ff1)
    probs_stage(0).start()
    probs_stage(1).start()
    chunk(4)
    second(4)
    third(2)
    fourth(0)
    chunk(5)
    second(5)
    third(3)
    fourth(1)
    chunk(6)
    fourth(2)
    chunk(7)
    first(r_ff2)
    fourth(3)
    third(4)

    d_normed = v_dn[...]
    load(2).wait()
    scaled = v_scaled1[...]
    v_sum[2:3, :] = jnp.zeros((1, v_sum.shape[1]), F32)
    v_sum[3:4, :] = column_sum(d_normed * scaled)
    v_sum[4:5, :] = column_sum(d_normed)
    v_sum[5:8, :] = sums[0:3, :]
    d_h1 = norm_back(d_normed * rows[3:4, :], scaled, inv1[:, 0:1])
    v_dn[...] = d_h1
    d_att = d_h1.astype(BF)
    v_sum[2:3, :] = column_sum(d_att.astype(F32))
    part = dot(ctx[...], d_att, 0, 0)
    full_b[0:768, :] = part[:, :384].astype(BF)
    full_b[768:1536, :] = part[:, 384:].astype(BF)
    first(r_out)
    second(6)
    third(5)
    load(0).wait()
    v_dctx[...] = dot(d_att, v_outw[...], 1, 1).astype(BF)
    second(7)
    fourth(4)

    lane = lax.broadcasted_iota(jnp.int32, (1, 128), 1)

    def attend_back(pair):
        col = 128 * pair
        probs_stage(pair).wait()
        q_pair = qkv[:, col : col + 128]
        k_pair = qkv[:, 768 + col : 768 + col + 128]
        v_pair = qkv[:, 1536 + col : 1536 + col + 128]
        d_pair = v_dctx[:, col : col + 128]
        product = d_pair.astype(F32) * ctx[:, col : col + 128].astype(F32)
        d_q, d_k, d_v = [], [], []
        for hh in range(2):
            mine = (lane < 64) if hh == 0 else (lane >= 64)
            inner = lax.dot_general(
                jnp.broadcast_to(mine.astype(F32), (8, 128)),
                product,
                (((1,), (1,)), ((), ())),
                preferred_element_type=F32,
                precision=lax.Precision.HIGHEST,
            )[0:1, :]
            d_probs = dot(v_pair, jnp.where(mine, d_pair, jnp.zeros((), BF)), 1, 1)
            probs_t = v_probs[pair % 2, hh]
            d_scores = (probs_t.astype(F32) * (d_probs - inner)).astype(BF)
            d_v.append(dot(probs_t, d_pair, 1, 0))
            d_k.append(dot(d_scores, q_pair, 1, 0))
            d_q.append(dot(d_scores, k_pair, 0, 0))
        v_dqkv[:, col : col + 128] = (jnp.where(lane < 64, d_q[0], d_q[1]) * 0.125).astype(BF)
        v_dqkv[:, 768 + col : 768 + col + 128] = jnp.where(lane < 64, d_k[0], d_k[1]).astype(BF)
        v_dqkv[:, 1536 + col : 1536 + col + 128] = jnp.where(lane < 64, d_v[0], d_v[1]).astype(BF)
        if pair < 4:
            probs_stage(pair + 2).start()

    attend_back(0)
    fourth(5)
    fifth(r_down)
    attend_back(1)
    third(6)
    attend_back(2)
    third(7)
    attend_back(3)
    second(8, 9)
    attend_back(4)
    fourth(6)
    second(10, 11)
    attend_back(5)
    fourth(7)
    third(8, 9, 10, 11)

    v_sum[0:1, :] = column_sum(v_dqkv[:, 0:768].astype(F32))
    v_sum[1:2, :] = column_sum(v_dqkv[:, 1536:2304].astype(F32))

    def row_copy(n, device):
        return pltpu.make_async_remote_copy(
            src_ref=v_sum,
            dst_ref=v_sums.at[n],
            send_sem=row_sends.at[n],
            recv_sem=row_recvs.at[n],
            device_id=device,
            device_id_type=MESH,
        )

    row_copies = [
        row_copy(0, (y, index(z, x, 1 - c))),
        row_copy(1, (y, index(z, 1 - x, c))),
        row_copy(2, (1 - y, index(z, x, c))),
    ] + [row_copy(2 + d, (y, index((z + d) % 4, x, c))) for d in (1, 2, 3)]

    def row_add(n):
        row_copies[n].wait()
        v_sum[...] = v_sum[...] + v_sums[n]

    row_copies[0].start()
    for n in range(3):
        part = dot(v_dqkv[:, 768 * n : 768 * n + 768], tok[...], 0, 0)
        full_b[1536 + 768 * n : 2304 + 768 * n, :] = part[:, :384].astype(BF)
        full_b[3840 + 768 * n : 4608 + 768 * n, :] = part[:, 384:].astype(BF)
    first(r_qkv)
    row_add(0)
    row_copies[1].start()
    fifth(r_ff2)
    second(12, 13, 14, 15)
    row_add(1)
    row_copies[2].start()
    load(1).wait()
    o_tok[...] = (dot(v_dqkv[...], v_qkvw[...], 1, 0) + v_dn[...]).astype(BF)
    fourth(8, 9, 10, 11)
    row_add(2)
    for n in (3, 4, 5):
        row_copies[n].start()
    third(12, 13, 14, 15)
    fifth(r_out)
    fourth(12, 13, 14, 15)
    for n in (3, 4, 5):
        row_copies[n].wait()
    o_rows[...] = v_sum[...] + v_sums[3] + v_sums[4] + v_sums[5]
    fifth(r_qkv)

    def put(r, o, by_row):
        r.to_y().wait()
        if by_row:
            o[pl.ds(pl.multiple_of(y * r.rows, 16), r.rows), :] = r.column(3)[...]
            o[pl.ds(pl.multiple_of((1 - y) * r.rows, 16), r.rows), :] = r.column(4)[...]
        else:
            o[:, pl.ds(pl.multiple_of(y * 384, 128), 384)] = r.column(3)[...]
            o[:, pl.ds(pl.multiple_of((1 - y) * 384, 128), 384)] = r.column(4)[...]

    put(r_down, o_down, False)
    put(r_ff2, o_ff, True)
    put(r_out, o_out, False)
    put(r_qkv, o_qkv, False)
    for r in (r_down, r_ff1, r_ff2, r_out, r_qkv):
        r.finish()


def bias_rows(parts, k):
    qv_bias, out_bias, gain1, shift1, ff_bias, down_bias, gain2, shift2 = parts

    def spread(shard, rows):
        n = shard.shape[0]
        whole = jnp.tile(shard, rows * 768 // n).reshape(rows, 768)
        at = lax.broadcasted_iota(jnp.int32, (rows, 768), 0) * 768
        at = at + lax.broadcasted_iota(jnp.int32, (rows, 768), 1)
        return jnp.where(at // n == k, whole, jnp.zeros((), BF))

    return jnp.concatenate(
        [
            spread(qv_bias, 2), spread(out_bias, 1), spread(gain1, 1), spread(shift1, 1),
            spread(down_bias, 1), spread(gain2, 1), spread(shift2, 1), spread(ff_bias, 8),
        ],
        0,
    )


def fused_on_device(
    tokens,
    qkv_weight,
    qv_bias,
    out_weight,
    out_bias,
    norm1_gain,
    norm1_shift,
    ff_weight,
    ff_bias,
    down_weight,
    down_bias,
    norm2_gain,
    norm2_shift,
    pair_length,
    cotangent,
):
    length, width = tokens.shape
    k = lax.axis_index("fsdp")
    vectors = (qv_bias, out_bias, norm1_gain, norm1_shift, ff_bias, down_bias, norm2_gain, norm2_shift)
    shards = (bias_rows(vectors, k), qkv_weight.T, out_weight, ff_weight, down_weight)
    in_vmem = pl.BlockSpec(memory_space=pltpu.VMEM)
    in_smem = pl.BlockSpec(memory_space=pltpu.SMEM)
    anywhere = pl.BlockSpec(memory_space=pl.ANY)
    struct = jax.ShapeDtypeStruct
    dma = pltpu.SemaphoreType.DMA
    whole = [(256, 768), (2304, 768), (768, 768), (12288, 384), (3072, 768)]
    (
        output, w_qkv, w_out, w_ff, w_down, rows, sums, qkv, ctx, probs, nlt, scaled1, inv1, gu, hid, dh2, db,
    ) = pl.pallas_call(
        forward_kernel,
        name="forward",
        out_shape=[
            struct((length, width), BF),
            struct(whole[1], BF),
            struct(whole[2], BF),
            struct(whole[3], BF),
            struct(whole[4], BF),
            struct((16, width), F32),
            struct((8, width), F32),
            struct((length, 2304), BF),
            struct((length, width), BF),
            struct((HEADS, length, length), BF),
            struct((width, length), BF),
            struct((length, width), F32),
            struct((length, 128), F32),
            struct((2, 8, length, 384), BF),
            struct((8, length, 384), BF),
            struct((length, width), F32),
            struct((length, width), BF),
        ],
        in_specs=[in_vmem, in_vmem, in_smem] + [anywhere] * 5,
        out_specs=[in_vmem] + [anywhere] * 4 + [in_vmem] * 2 + [anywhere] * 5 + [in_vmem] + [anywhere] * 2
        + [in_vmem] * 2,
        scratch_shapes=[pltpu.VMEM(s, BF) for s in whole]
        + [
            pltpu.VMEM((length, length), F32),
            pltpu.VMEM((length, 2304), BF),
            pltpu.VMEM((length, width), BF),
            pltpu.VMEM((HEADS, length, length), BF),
            pltpu.VMEM((length, width), F32),
            pltpu.VMEM((length, width), BF),
            pltpu.VMEM((2, 8, length, 384), BF),
            pltpu.VMEM((8, length, 384), BF),
            pltpu.VMEM((length, width), F32),
            pltpu.VMEM((width, length), BF),
            dma((5, Gather.SLOTS)),
            dma((5, Gather.SLOTS)),
            dma((5,)),
            dma((24,)),
        ],
        compiler_params=pltpu.CompilerParams(
            collective_id=0, has_side_effects=True, vmem_limit_bytes=60 * 2**20
        ),
    )(tokens, cotangent, pair_length, *shards)
    d_tokens, d_qkv, d_out, d_ff, d_down, d_rows = pl.pallas_call(
        backward_kernel,
        name="backward",
        out_shape=[
            struct((length, width), BF),
            struct((144, width), BF),
            struct((48, width), BF),
            struct((768, 384), BF),
            struct((192, width), BF),
            struct((16, width), F32),
        ],
        in_specs=[in_vmem] * 8 + [anywhere] * 9,
        out_specs=[in_vmem] * 6,
        scratch_shapes=[
            pltpu.VMEM((2304, width), BF),
            pltpu.VMEM((width, width), BF),
            pltpu.VMEM((2, 2, 768, 384), BF),
            pltpu.VMEM((2, 384, width), BF),
            pltpu.VMEM((length, width), F32),
            pltpu.VMEM((length, width), F32),
            pltpu.VMEM((2, 2, length, length), BF),
            pltpu.VMEM((2, 2, length, 384), BF),
            pltpu.VMEM((2, length, 384), BF),
            pltpu.VMEM((6144, 384), BF),
            pltpu.VMEM((6144, 384), BF),
            pltpu.VMEM((768 * 16, 384), BF),
            pltpu.VMEM((768 * 4, 384), BF),
            pltpu.VMEM((768 * 8, 384), BF),
            pltpu.VMEM((768 * 5, 384), BF),
            pltpu.VMEM((length, width), BF),
            pltpu.VMEM((length, 2304), BF),
            pltpu.VMEM((16, width), F32),
            pltpu.VMEM((6, 16, width), F32),
            dma((4, 32)),
            dma((4, 32)),
            dma((6,)),
            dma((6,)),
            dma((4,)),
            dma((7, 2)),
        ],
        compiler_params=pltpu.CompilerParams(
            collective_id=1, has_side_effects=True, vmem_limit_bytes=63 * 2**20
        ),
    )(tokens, qkv, ctx, nlt, db, rows, sums, inv1, w_qkv, w_out, w_ff, w_down, scaled1, dh2, probs, gu, hid)

    def own(row, n):
        return lax.dynamic_slice(d_rows[row : row + max(1, n * 16 // 768)].reshape(-1), (k * n,), (n,))

    return (
        output,
        d_tokens,
        d_qkv.T.astype(F32),
        own(0, 96),
        d_out.astype(F32),
        own(2, 48),
        own(3, 48),
        own(4, 48),
        d_ff.astype(F32),
        own(8, 384),
        d_down.astype(F32),
        own(5, 48),
        own(6, 48),
        own(7, 48),
    )


def solution(mesh):
    in_specs = (
        P(("rep", "fsdp"), None),
        P(None, "fsdp"),
        P("fsdp"),
        P("fsdp", None),
        P("fsdp"),
        P("fsdp"),
        P("fsdp"),
        P(None, "fsdp"),
        P("fsdp"),
        P("fsdp", None),
        P("fsdp"),
        P("fsdp"),
        P("fsdp"),
        P(("rep", "fsdp")),
        P(("rep", "fsdp"), None),
    )
    out_specs = (
        P(("rep", "fsdp"), None),
        P(("rep", "fsdp"), None),
        P(None, "fsdp"),
        P("fsdp"),
        P("fsdp", None),
        P("fsdp"),
        P("fsdp"),
        P("fsdp"),
        P(None, "fsdp"),
        P("fsdp"),
        P("fsdp", None),
        P("fsdp"),
        P("fsdp"),
        P("fsdp"),
    )
    planes = mesh.shape["rep"] == 2 and mesh.shape["fsdp"] == 16
    return jax.shard_map(
        fused_on_device if planes else plain_on_device, mesh=mesh, in_specs=in_specs, out_specs=out_specs, check_vma=False
    )
```

```python
import jax
import jax.numpy as jnp
from jax import lax
from jax.experimental import pallas as pl
from jax.experimental.pallas import tpu as pltpu
from jax.sharding import PartitionSpec as P

HEADS = 12
MESH = pl.DeviceIdType.MESH
BF = jnp.bfloat16
F32 = jnp.float32


def layer_norm(h, gain, shift):
    mean = jnp.mean(h, -1, keepdims=True)
    centered = h - mean
    spread = jnp.mean(centered * centered, -1, keepdims=True)
    return centered * lax.rsqrt(spread + 1e-05) * gain + shift


def inner_rows(left, right):
    return lax.dot_general(
        left, right, (((0,), (0,)), ((), ())), preferred_element_type=jnp.float32
    )


def times_transposed(left, right):
    return lax.dot_general(
        left, right, (((1,), (1,)), ((), ())), preferred_element_type=jnp.float32
    )


def score_block(query, keys, slope, valid):
    length = query.shape[0]
    place = jnp.arange(length, dtype=jnp.float32)
    scores = times_transposed(query, keys) * 0.125 - slope * jnp.abs(
        place[:, None] - place[None, :]
    )
    allowed = jnp.arange(length, dtype=jnp.int32) < valid
    return jnp.where(allowed[None, :], scores, -1e30)


def head_slopes():
    return 2.0 ** (-8.0 * jnp.arange(1, HEADS + 1, dtype=jnp.float32) / HEADS)


def forward(tokens, attention, feedforward, valid):
    qkv_weight, qv_bias, out_weight, out_bias, gain1, shift1 = attention
    ff_weight, ff_bias, down_weight, down_bias, gain2, shift2 = feedforward
    length, width = tokens.shape
    bias_f = qv_bias.astype(jnp.float32)
    full_bias = jnp.concatenate([bias_f[:width], jnp.zeros((width,), jnp.float32), bias_f[width:]])
    qkv = (jnp.dot(tokens, qkv_weight, preferred_element_type=jnp.float32) + full_bias).astype(
        jnp.bfloat16
    )
    per_head = qkv.reshape(length, 3, HEADS, width // HEADS).transpose(1, 2, 0, 3)

    def attend(item):
        query, keys, values, slope = item
        scores = score_block(query, keys, slope, valid)
        top = jnp.max(scores, -1, keepdims=True)
        expo = jnp.exp(scores - top)
        total = jnp.sum(expo, -1, keepdims=True)
        probs = (expo / total).astype(jnp.bfloat16)
        return (
            jnp.dot(probs, values, preferred_element_type=jnp.float32),
            top[:, 0] + jnp.log(total[:, 0]),
        )

    context, log_total = lax.map(attend, (per_head[0], per_head[1], per_head[2], head_slopes()))
    context = context.transpose(1, 0, 2).reshape(length, width).astype(jnp.bfloat16)
    attended = jnp.dot(context, out_weight, preferred_element_type=jnp.float32) + out_bias.astype(
        jnp.float32
    )
    residual1 = tokens.astype(jnp.float32) + attended
    normed = layer_norm(residual1, gain1.astype(jnp.float32), shift1.astype(jnp.float32))
    normed_low = normed.astype(jnp.bfloat16)
    gate_up = jnp.dot(normed_low, ff_weight, preferred_element_type=jnp.float32) + ff_bias.astype(
        jnp.float32
    )
    half = gate_up.shape[1] // 2
    hidden = (jax.nn.gelu(gate_up[:, :half], approximate=False) * gate_up[:, half:]).astype(
        jnp.bfloat16
    )
    residual2 = (
        normed
        + jnp.dot(hidden, down_weight, preferred_element_type=jnp.float32)
        + down_bias.astype(jnp.float32)
    )
    return (per_head, log_total, context, residual1, normed_low, gate_up, hidden, residual2)


def gelu_product(gate, up):
    return jax.nn.gelu(gate, approximate=False) * up


def plain_on_device(
    tokens,
    qkv_weight,
    qv_bias,
    out_weight,
    out_bias,
    norm1_gain,
    norm1_shift,
    ff_weight,
    ff_bias,
    down_weight,
    down_bias,
    norm2_gain,
    norm2_shift,
    pair_length,
    cotangent,
):
    valid = pair_length[0]
    attention = (
        lax.all_gather(qkv_weight, "fsdp", axis=1, tiled=True),
        lax.all_gather(qv_bias, "fsdp", axis=0, tiled=True),
        lax.all_gather(out_weight, "fsdp", axis=0, tiled=True),
        lax.all_gather(out_bias, "fsdp", axis=0, tiled=True),
        lax.all_gather(norm1_gain, "fsdp", axis=0, tiled=True),
        lax.all_gather(norm1_shift, "fsdp", axis=0, tiled=True),
    )
    feedforward = (
        lax.all_gather(ff_weight, "fsdp", axis=1, tiled=True),
        lax.all_gather(ff_bias, "fsdp", axis=0, tiled=True),
        lax.all_gather(down_weight, "fsdp", axis=0, tiled=True),
        lax.all_gather(down_bias, "fsdp", axis=0, tiled=True),
        lax.all_gather(norm2_gain, "fsdp", axis=0, tiled=True),
        lax.all_gather(norm2_shift, "fsdp", axis=0, tiled=True),
    )
    stored = forward(tokens, attention, feedforward, valid)
    gain2 = feedforward[4].astype(jnp.float32)
    shift2 = feedforward[5].astype(jnp.float32)
    output = layer_norm(stored[7], gain2, shift2).astype(jnp.bfloat16)
    per_head, log_total, context, residual1, normed_low, gate_up, hidden, residual2 = stored
    full_qkv, bias_unused, full_out, out_unused, gain1, shift1 = attention
    full_ff, ff_unused, full_down, down_unused, gain_unused, shift_unused = feedforward
    length, width = tokens.shape
    unused_out, back_second = jax.vjp(layer_norm, residual2, gain2, shift2)
    d_res2, d_gain2, d_shift2 = back_second(cotangent.astype(jnp.float32))
    d_branch = d_res2.astype(jnp.bfloat16)
    d_down = inner_rows(hidden, d_branch)
    d_down_bias = jnp.sum(d_branch.astype(jnp.float32), 0)
    d_hidden = times_transposed(d_branch, full_down).astype(jnp.bfloat16)
    half = gate_up.shape[1] // 2
    unused_prod, back_gelu = jax.vjp(gelu_product, gate_up[:, :half], gate_up[:, half:])
    d_gate, d_up = back_gelu(d_hidden.astype(jnp.float32))
    d_gate_up = jnp.concatenate([d_gate, d_up], 1).astype(jnp.bfloat16)
    d_ff = inner_rows(normed_low, d_gate_up)
    d_ff_bias = jnp.sum(d_gate_up.astype(jnp.float32), 0)
    d_normed = times_transposed(d_gate_up, full_ff) + d_res2
    unused_norm, back_first = jax.vjp(
        layer_norm, residual1, gain1.astype(jnp.float32), shift1.astype(jnp.float32)
    )
    d_res1, d_gain1, d_shift1 = back_first(d_normed)
    ff_terms = (d_ff, d_ff_bias, d_down, d_down_bias, d_gain2, d_shift2)
    ff_grads = (
        lax.psum_scatter(ff_terms[0], "fsdp", scatter_dimension=1, tiled=True),
        lax.psum_scatter(ff_terms[1], "fsdp", scatter_dimension=0, tiled=True),
        lax.psum_scatter(ff_terms[2], "fsdp", scatter_dimension=0, tiled=True),
        lax.psum_scatter(ff_terms[3], "fsdp", scatter_dimension=0, tiled=True),
        lax.psum_scatter(ff_terms[4], "fsdp", scatter_dimension=0, tiled=True),
        lax.psum_scatter(ff_terms[5], "fsdp", scatter_dimension=0, tiled=True),
    )
    ff_grads = (
        lax.psum(ff_grads[0].astype(jnp.bfloat16), "rep").astype(jnp.float32),
        lax.psum(ff_grads[1].astype(jnp.bfloat16), "rep").astype(jnp.float32),
        lax.psum(ff_grads[2].astype(jnp.bfloat16), "rep").astype(jnp.float32),
        lax.psum(ff_grads[3].astype(jnp.bfloat16), "rep").astype(jnp.float32),
        lax.psum(ff_grads[4].astype(jnp.bfloat16), "rep").astype(jnp.float32),
        lax.psum(ff_grads[5].astype(jnp.bfloat16), "rep").astype(jnp.float32),
    )
    d_attended = d_res1.astype(jnp.bfloat16)
    d_out = inner_rows(context, d_attended)
    d_out_bias = jnp.sum(d_attended.astype(jnp.float32), 0)
    d_context = times_transposed(d_attended, full_out).astype(jnp.bfloat16)
    d_context = d_context.reshape(length, HEADS, width // HEADS).transpose(1, 0, 2)

    def attend_back(item):
        query, keys, values, grad_context, total_log, slope = item
        scores = score_block(query, keys, slope, valid)
        probs = jnp.exp(scores - total_log[:, None])
        probs_low = probs.astype(jnp.bfloat16)
        d_probs = times_transposed(grad_context, values)
        d_scores = (probs * (d_probs - jnp.sum(probs * d_probs, -1, keepdims=True))).astype(
            jnp.bfloat16
        )
        d_query = jnp.dot(d_scores, keys, preferred_element_type=jnp.float32) * 0.125
        d_keys = inner_rows(d_scores, query) * 0.125
        d_values = inner_rows(probs_low, grad_context)
        return (d_query, d_keys, d_values)

    d_query, d_keys, d_values = lax.map(
        attend_back, (per_head[0], per_head[1], per_head[2], d_context, log_total, head_slopes())
    )
    d_qkv = (
        jnp.stack([d_query, d_keys, d_values])
        .transpose(2, 0, 1, 3)
        .reshape(length, 3 * width)
        .astype(jnp.bfloat16)
    )
    d_qkv_w = inner_rows(tokens, d_qkv)
    column_sums = jnp.sum(d_qkv.astype(jnp.float32), 0)
    d_qv = jnp.concatenate([column_sums[:width], column_sums[2 * width :]])
    d_tokens = (times_transposed(d_qkv, full_qkv) + d_res1).astype(jnp.bfloat16)
    at_terms = (d_qkv_w, d_qv, d_out, d_out_bias, d_gain1, d_shift1)
    at_grads = (
        lax.psum_scatter(at_terms[0], "fsdp", scatter_dimension=1, tiled=True),
        lax.psum_scatter(at_terms[1], "fsdp", scatter_dimension=0, tiled=True),
        lax.psum_scatter(at_terms[2], "fsdp", scatter_dimension=0, tiled=True),
        lax.psum_scatter(at_terms[3], "fsdp", scatter_dimension=0, tiled=True),
        lax.psum_scatter(at_terms[4], "fsdp", scatter_dimension=0, tiled=True),
        lax.psum_scatter(at_terms[5], "fsdp", scatter_dimension=0, tiled=True),
    )
    at_grads = (
        lax.psum(at_grads[0].astype(jnp.bfloat16), "rep").astype(jnp.float32),
        lax.psum(at_grads[1].astype(jnp.bfloat16), "rep").astype(jnp.float32),
        lax.psum(at_grads[2].astype(jnp.bfloat16), "rep").astype(jnp.float32),
        lax.psum(at_grads[3].astype(jnp.bfloat16), "rep").astype(jnp.float32),
        lax.psum(at_grads[4].astype(jnp.bfloat16), "rep").astype(jnp.float32),
        lax.psum(at_grads[5].astype(jnp.bfloat16), "rep").astype(jnp.float32),
    )
    return (
        output,
        d_tokens,
        at_grads[0],
        at_grads[1],
        at_grads[2],
        at_grads[3],
        at_grads[4],
        at_grads[5],
        ff_grads[0],
        ff_grads[1],
        ff_grads[2],
        ff_grads[3],
        ff_grads[4],
        ff_grads[5],
    )


def dot(left, right, left_dim, right_dim):
    return lax.dot_general(
        left, right, (((left_dim,), (right_dim,)), ((), ())), preferred_element_type=F32
    )


def whereabouts():
    y = lax.axis_index("rep")
    k = lax.axis_index("fsdp")
    return y, k // 4, (k // 2) % 2, k % 2


def index(z, x, c):
    return z * 4 + x * 2 + c


def plane_at(z, i):
    return (z, z + 1 - 2 * (z % 2), (z + 2) % 4, 3 - z)[i]


def in_middle(z):
    return (z == 1) | (z == 2)


def greet():
    y, z, x, c = whereabouts()
    friends = [(y, index(z, x, 1 - c)), (y, index(z, 1 - x, c)), (1 - y, index(z, x, c))]
    friends += [(y, index(plane_at(z, i), x, c)) for i in (1, 2, 3)]
    barrier = pltpu.get_barrier_semaphore()
    for friend in friends:
        pl.semaphore_signal(barrier, inc=1, device_id=friend, device_id_type=MESH)
    pl.semaphore_wait(barrier, len(friends))


class Gather:
    Z, X, Y, D, C = 0, 8, 12, 16, 20
    SLOTS = 28

    def __init__(self, t, src, dst, rows, by_row, deep, sends, recvs, locals_):
        self.t, self.src, self.dst, self.rows, self.by_row, self.deep = t, src, dst, rows, by_row, deep
        self.sends, self.recvs, self.locals_ = sends, recvs, locals_
        self.y, self.z, self.x, self.c = whereabouts()

    def plane(self, i):
        return plane_at(self.z, i)

    def half(self, ref, base, h):
        if self.by_row:
            n = self.rows // 2
            return ref.at[pl.ds(pl.multiple_of(base + h * n, 16), n), :]
        n = ref.shape[1] // 2
        return ref.at[pl.ds(base, self.rows), pl.ds(pl.multiple_of(h * n, 128), n)]

    def part(self, k, h):
        return self.half(self.dst, pl.multiple_of(k * self.rows, 16), h)

    def shard(self, k):
        return self.dst.at[pl.ds(pl.multiple_of(k * self.rows, 16), self.rows), :]

    def copy(self, slot, src, dst, device, arrival=None):
        return pltpu.make_async_remote_copy(
            src_ref=src,
            dst_ref=dst,
            send_sem=self.sends.at[self.t, slot],
            recv_sem=self.recvs.at[self.t, slot if arrival is None else arrival],
            device_id=device,
            device_id_type=MESH,
        )

    def halves(self):
        return (0, 1) if self.deep else (0,)

    def to_plane(self, i, a):
        h = 1 - self.y if a else self.y
        k = index(self.z, self.x, self.c)
        device = (self.y, index(self.plane(i), self.x, self.c))
        return self.copy(self.Z + 2 * i + a, self.half(self.src, 0, h), self.part(k, h), device)

    def relay(self, a):
        h = 1 - self.y if a else self.y
        k = index(self.plane(2), self.x, self.c)
        device = (self.y, index(self.plane(1), self.x, self.c))
        return self.copy(self.Z + a, self.part(k, h), self.part(k, h), device, self.Z + 6 + a)

    def to_x(self, i):
        k = index(self.plane(i), self.x, self.c)
        src = self.half(self.src, 0, self.y) if i == 0 else self.part(k, self.y)
        return self.copy(
            self.X + i, src, self.part(k, self.y), (self.y, index(self.z, 1 - self.x, self.c))
        )

    def to_y(self, i):
        k = index(self.plane(i), self.x, self.c)
        part = self.part(k, self.y)
        return self.copy(self.Y + i, part, part, (1 - self.y, index(self.z, self.x, self.c)))

    def onward(self, i):
        c = 0 if i == 0 or self.deep else self.c
        k = index(self.plane(i), (1 - self.x) * (1 - c) + self.x * c, self.c)
        part = self.part(k, self.y * (1 - c) + (1 - self.y) * c)
        x = self.x * (1 - c) + (1 - self.x) * c
        y = self.y * c + (1 - self.y) * (1 - c)
        return self.copy(self.D + i, part, part, (y, index(self.z, x, self.c)))

    def to_core(self, i, home):
        k = index(self.plane(i), self.x if home else 1 - self.x, self.c)
        src = self.src if home and i == 0 else self.shard(k)
        device = (self.y, index(self.z, self.x, 1 - self.c))
        return self.copy(self.C + i + (0 if home else 4), src, self.shard(k), device)

    def own(self):
        return pltpu.make_async_copy(
            self.src, self.shard(index(self.z, self.x, self.c)), self.locals_.at[self.t]
        )

    def begin(self):
        for a in self.halves():
            for i in (2, 1):
                self.to_plane(i, a).start()

            @pl.when(in_middle(self.z))
            def _():
                self.to_plane(3, a).start()

    def begin_plane(self):
        self.to_x(0).start()
        self.to_core(0, True).start()
        self.own().start()

    def second(self, i):
        if i == 0:
            return
        for a in self.halves():
            self.to_plane(i, a).wait_recv()
            if i == 2:

                @pl.when(in_middle(self.z))
                def _():
                    self.relay(a).start()

            if a == 0:
                self.to_x(i).start()
                if not self.deep:
                    self.to_y(i).start()
        if self.deep:
            self.to_core(i, True).start()

    def third(self, i):
        if i and not self.deep:
            self.to_y(i).wait_recv()
            self.to_core(i, True).start()
        self.to_x(i).wait_recv()
        self.onward(i).start()

    def fourth(self, i):
        self.onward(i).wait_recv()
        self.to_core(i, False).start()

    def arrived(self, i):
        self.to_core(i, True).wait_recv()
        self.to_core(i, False).wait_recv()
        if i == 0:
            self.own().wait()

    def finish(self):
        for a in self.halves():
            for i in (1, 2):
                self.to_plane(i, a).wait_send()

            @pl.when(in_middle(self.z))
            def _():
                self.to_plane(3, a).wait_send()
                self.relay(a).wait_send()

        for i in range(4):
            self.to_x(i).wait_send()
            if i and not self.deep:
                self.to_y(i).wait_send()
            self.onward(i).wait_send()
            self.to_core(i, True).wait_send()
            self.to_core(i, False).wait_send()


class Reduce:
    CORE, DIAGONAL, EARLY, LATE, PLANE, ARRIVE, LAST, SLOTS = 0, 4, 5, 6, 7, 36, 38, 40

    def __init__(self, t, base, rows, deep, at, full, both, across, sides, columns, sends, recvs):
        self.t, self.base, self.rows, self.deep, self.at = t, base, rows, deep, at
        self.full, self.both, self.across, self.sides, self.columns = full, both, across, sides, columns
        self.sends, self.recvs = sends, recvs
        self.y, self.z, self.x, self.c = whereabouts()

    def copy(self, slot, src, dst, device, arrival=None):
        return pltpu.make_async_remote_copy(
            src_ref=src,
            dst_ref=dst,
            send_sem=self.sends.at[self.t, slot],
            recv_sem=self.recvs.at[self.t, slot if arrival is None else arrival],
            device_id=device,
            device_id_type=MESH,
        )

    def rows_of(self, ref, row):
        return ref.at[pl.ds(pl.multiple_of(row, 16), self.rows), :]

    def unit(self, i, away_x, c, h):
        x = 1 - self.x if away_x else self.x
        return self.rows_of(self.full, self.at(plane_at(self.z, i), x, c, h))

    def mine(self, i, away_x, away_h):
        n = i * 4 + away_x * 2 + away_h
        return self.rows_of(self.both, self.base * 16 + n * self.rows)

    def side(self, i, s):
        return self.rows_of(self.sides, self.base * 8 + (i * 2 + s) * self.rows)

    def cross(self, i):
        return self.rows_of(self.across, self.base * 4 + i * self.rows)

    def column(self, n, a):
        return self.rows_of(self.columns, self.base * 12 + (2 * n + a) * self.rows)

    def halves(self):
        return (0, 1) if self.deep else (0,)

    def way(self, i):
        return 0 if self.deep else (1 if i == 0 else self.c)

    def neighbour(self, over_x):
        return (
            self.y * over_x + (1 - self.y) * (1 - over_x),
            index(self.z, (1 - self.x) * over_x + self.x * (1 - over_x), self.c),
        )

    def to_core(self, i, n):
        device = (self.y, index(self.z, self.x, 1 - self.c))
        h = 1 - self.y if n % 2 else self.y
        src = self.unit(i, n // 2, 1 - self.c, h)
        return self.copy(i * 9 + n, src, self.mine(i, n // 2, n % 2), device)

    def diagonal(self, i):
        device = self.neighbour(self.way(i))
        return self.copy(i * 9 + self.DIAGONAL, self.mine(i, 1, 1), self.cross(i), device)

    def early(self, i):
        w = self.way(i)
        return self.copy(i * 9 + self.EARLY, self.mine(i, w, 1 - w), self.side(i, 0), self.neighbour(w))

    def late(self, i):
        w = self.way(i)
        return self.copy(i * 9 + self.LATE, self.mine(i, 1 - w, w), self.side(i, 1), self.neighbour(1 - w))

    def over_x(self, i, a):
        slot = i * 9 + (self.LATE if a else self.EARLY)
        return self.copy(slot, self.mine(i, 1, a), self.side(i, a), self.neighbour(1))

    def to_plane(self, i, a):
        slot = i * 9 + self.PLANE + a
        src = self.mine(i, 0, a)
        if i < 3:
            device = (self.y, index(plane_at(self.z, i), self.x, self.c))
            return self.copy(slot, src, self.column(i - 1, a), device)
        near, far = plane_at(self.z, 1), plane_at(self.z, 3)
        middle = (self.z % 3 + 1) // 2
        plane = far * middle + near * (1 - middle)
        arrival = slot * middle + (self.ARRIVE + a) * (1 - middle)
        return self.copy(
            slot, src, self.column(3 - middle, a), (self.y, index(plane, self.x, self.c)), arrival
        )

    def handed(self, a):
        slot = 3 * 9 + self.PLANE + a
        device = (self.y, index(plane_at(self.z, 1), self.x, self.c))
        return self.copy(slot, self.mine(3, 0, a), self.column(3, a), device, self.ARRIVE + a)

    def mirrored(self, a):
        slot = 3 * 9 + self.PLANE + a
        device = (self.y, index(plane_at(self.z, 3), self.x, self.c))
        return self.copy(slot, self.mine(3, 0, a), self.column(2, a), device)

    def last(self, a):
        device = (1 - self.y, index(self.z, self.x, self.c))
        b = 1 - a if self.deep else a
        return self.copy(self.LAST + a, self.column(4, a), self.column(5, b), device, self.LAST + b)

    def first(self, i):
        for n in (3, 2, 1, 0):
            self.to_core(i, n).start()

    def second(self, i):
        for n in (3, 2, 1, 0):
            self.to_core(i, n).wait()
            h = 1 - self.y if n % 2 else self.y
            part = self.mine(i, n // 2, n % 2)
            part[...] = part[...] + self.unit(i, n // 2, self.c, h)[...]
            if self.deep and i == 0:
                if n > 1:
                    self.over_x(i, n - 2).start()
            elif n == 3:
                self.diagonal(i).start()
        if not self.deep:
            self.early(i).start()

    def third(self, i):
        if self.deep and i == 0:
            return
        w = self.way(i)
        self.diagonal(i).wait_recv()
        part = self.mine(i, 1 - w, w)
        part[...] = part[...] + self.cross(i)[...]
        if self.deep:
            self.over_x(i, 0).start()
        else:
            self.late(i).start()

    def fourth(self, i):
        if self.deep:
            for a in (0, 1) if i == 0 else (0,):
                self.over_x(i, a).wait_recv()
                part = self.mine(i, 0, a)
                part[...] = part[...] + self.side(i, a)[...]
            return
        self.early(i).wait_recv()
        self.late(i).wait_recv()
        part = self.mine(i, 0, 0)
        total = part[...].astype(F32) + self.side(i, 0)[...].astype(F32)
        part[...] = (total + self.side(i, 1)[...].astype(F32)).astype(BF)

    def along(self, i, a):
        if i == 2:

            @pl.when(in_middle(self.z))
            def _():
                self.handed(a).wait_recv()
                part = self.mine(2, 0, a)
                part[...] = part[...] + self.column(3, a)[...]

        self.to_plane(i, a).start()

    def fifth(self, a):
        for i in (1, 2):
            self.to_plane(i, a).wait_recv()
        total = self.mine(0, 0, a)[...].astype(F32)
        total = total + self.column(0, a)[...].astype(F32) + self.column(1, a)[...].astype(F32)

        @pl.when(in_middle(self.z))
        def _():
            self.mirrored(a).wait_recv()
            self.column(4, a)[...] = (total + self.column(2, a)[...].astype(F32)).astype(BF)

        @pl.when(jnp.logical_not(in_middle(self.z)))
        def _():
            self.column(4, a)[...] = total.astype(BF)

        self.last(a).start()

    def put(self, a, out, by_row):
        self.last(a).wait_send()
        self.last(1 - a if self.deep else a).wait_recv()
        own, other = self.column(4, a)[...].astype(F32), self.column(5, a)[...].astype(F32)
        here, there = self.y, 1 - self.y
        if self.deep:
            pairs = [((there if a else here), own + other)]
        else:
            pairs = [(here, own), (there, other)]
        for h, value in pairs:
            if by_row:
                out[pl.ds(pl.multiple_of(h * self.rows, 16), self.rows), :] = value
            else:
                out[:, pl.ds(pl.multiple_of(h * 384, 128), 384)] = value

    def finish(self):
        for i in range(4):
            if self.deep:
                if i:
                    self.diagonal(i).wait_send()
                self.over_x(i, 0).wait_send()
                if i == 0:
                    self.over_x(i, 1).wait_send()
            else:
                self.diagonal(i).wait_send()
                self.early(i).wait_send()
                self.late(i).wait_send()
            if i:
                for a in self.halves():
                    self.to_plane(i, a).wait_send()


def slope_of(head):
    return jnp.exp2(jnp.full((1, 1), head + 1, jnp.int32).astype(F32) * (-8.0 / HEADS))


def normalise(h):
    centered = h - jnp.mean(h, -1, keepdims=True)
    inverse = lax.rsqrt(jnp.mean(centered * centered, -1, keepdims=True) + 1e-05)
    return centered * inverse, inverse


def norm_back(d_scaled, scaled, inverse):
    mean1 = jnp.mean(d_scaled, -1, keepdims=True)
    mean2 = jnp.mean(d_scaled * scaled, -1, keepdims=True)
    return inverse * (d_scaled - mean1 - scaled * mean2)


def column_sum(v):
    return jnp.sum(v, axis=0, keepdims=True)


def cdf(gate):
    return 0.5 * (1.0 + lax.erf(gate * 0.7071067811865476))


def bias_at(j):
    return pl.ds(8 + j // 2, 1), pl.ds(pl.multiple_of((j % 2) * 384, 128), 384)


VECTORS = (
    (0, 96, 0), (96, 48, 2), (144, 48, 3), (192, 48, 4), (240, 384, 8), (624, 48, 5), (672, 48, 6), (720, 48, 7),
)


def spread_vectors(shards, k):
    lane = lax.broadcasted_iota(jnp.int32, (16, 768), 1)
    line = lax.broadcasted_iota(jnp.int32, (16, 768), 0)
    wide = jnp.broadcast_to(shards, (16, 768))
    rows = jnp.zeros((16, 768), F32)
    for start, n, row in VECTORS:
        per = 768 // n
        shift = ((k % per) * n - start + 768) % 768
        here = (lane // n == k % per) & (line == row + k // per)
        rows = jnp.where(here, pltpu.roll(wide, shift, 1), rows)
    return rows


(
    OWN, ALONG, SECOND, THIRD, FOURTH, ARRIVED, DIST, ROWS, QKV, ATTEND, NORM, FEED, DOWN, END, START,
    D_DOWN, CHUNK, D_NORM, D_OUT, D_CTX, D_QKV, D_TOK, ROW, FIRST, FIFTH, PUT,
) = range(26)

FORWARD_ORDER = (
    (OWN, 2), (ALONG, 0, 3), (ALONG, 1, 3), (OWN, 1), (THIRD, 2, 0), (ALONG, 2, 2), (OWN, 0), (ALONG, 1, 1),
    (ALONG, 0, 2), (THIRD, 1, 0), (OWN, 4), (ALONG, 1, 2), (ALONG, 2, 1), (ALONG, 2, 3), (THIRD, 4, 0),
    (SECOND, 2, 2), (ALONG, 4, 3), (THIRD, 0, 0), (OWN, 3), (ALONG, 0, 1), (FOURTH, 1, 0), (SECOND, 0, 3),
    (SECOND, 2, 1), (SECOND, 0, 1), (ALONG, 3, 2), (SECOND, 0, 2), (SECOND, 1, 2), (FOURTH, 2, 0), (FOURTH, 4, 0),
    (SECOND, 2, 3), (THIRD, 0, 1), (THIRD, 0, 3), (FOURTH, 0, 0), (THIRD, 2, 2), (SECOND, 1, 3), (SECOND, 1, 1),
    (FOURTH, 0, 3), (ALONG, 3, 1), (ARRIVED, 1, 0), (ARRIVED, 0, 0), (THIRD, 2, 1), (THIRD, 1, 3), (THIRD, 1, 1),
    (ARRIVED, 2, 0), (FOURTH, 0, 1), (THIRD, 0, 2), (THIRD, 1, 2), (ALONG, 3, 3), (SECOND, 3, 1), (FOURTH, 1, 3),
    (FOURTH, 1, 1), (ARRIVED, 0, 3), (ARRIVED, 1, 3), (FOURTH, 2, 2), (ARRIVED, 0, 1), (THIRD, 2, 3), (DIST,),
    (FOURTH, 0, 2), (SECOND, 3, 2), (ARRIVED, 0, 2), (ARRIVED, 1, 1), (ROWS,), (FOURTH, 1, 2), (ARRIVED, 1, 2),
    (ALONG, 4, 2), (QKV, 0), (SECOND, 3, 3), (FOURTH, 2, 3), (FOURTH, 2, 1), (ALONG, 4, 1), (QKV, 1), (QKV, 2),
    (ATTEND, 0), (ATTEND, 1), (THIRD, 3, 1), (ATTEND, 2), (THIRD, 3, 3), (ARRIVED, 2, 1), (THIRD, 3, 2),
    (ARRIVED, 2, 2), (ARRIVED, 2, 3), (ATTEND, 3), (ATTEND, 4), (FOURTH, 3, 1), (SECOND, 4, 2), (ATTEND, 5),
    (FOURTH, 3, 3), (THIRD, 3, 0), (NORM,), (ARRIVED, 3, 3), (FOURTH, 3, 2), (ARRIVED, 3, 1), (FEED, 0),
    (SECOND, 4, 3), (FEED, 1), (ARRIVED, 4, 0), (THIRD, 4, 2), (FOURTH, 3, 0), (SECOND, 4, 1), (FEED, 2),
    (FEED, 3), (ARRIVED, 3, 0), (THIRD, 4, 3), (ARRIVED, 3, 2), (FOURTH, 4, 2), (FEED, 4), (FEED, 5),
    (THIRD, 4, 1), (ARRIVED, 4, 2), (FEED, 6), (FOURTH, 4, 3), (FEED, 7), (DOWN, 2), (ARRIVED, 4, 3),
    (FOURTH, 4, 1), (DOWN, 3), (DOWN, 0), (ARRIVED, 4, 1), (DOWN, 1), (END,),
)

BACKWARD_ORDER = (
    (START,), (D_DOWN, 3), (D_DOWN, 0), (FIRST, 0, 3), (D_DOWN, 2), (FIRST, 0, 2), (SECOND, 0, 3), (D_DOWN, 1),
    (SECOND, 0, 2), (FIRST, 0, 0), (CHUNK, 0), (THIRD, 0, 3), (CHUNK, 1), (CHUNK, 2), (FOURTH, 0, 3),
    (FIRST, 0, 1), (ALONG, 0, 3, 1), (SECOND, 0, 0), (CHUNK, 3), (SECOND, 0, 1), (ALONG, 0, 3, 0), (THIRD, 0, 2),
    (ALONG, 0, 2, 1), (FIRST, 1, 3), (CHUNK, 4), (ALONG, 0, 1, 1), (SECOND, 1, 3), (FIRST, 1, 1), (CHUNK, 5),
    (SECOND, 1, 1), (THIRD, 0, 1), (FOURTH, 0, 2), (ALONG, 1, 3, 1), (CHUNK, 6), (THIRD, 1, 3), (CHUNK, 7),
    (FIRST, 1, 2), (D_NORM,), (FOURTH, 0, 1), (ALONG, 0, 2, 0), (ALONG, 0, 1, 0), (THIRD, 1, 1), (FIRST, 1, 0),
    (D_OUT,), (D_CTX,), (SECOND, 1, 2), (FOURTH, 0, 0), (SECOND, 1, 0), (ALONG, 1, 2, 1), (ATTEND, 0),
    (ALONG, 1, 1, 1), (ATTEND, 1), (FIFTH, 0, 0), (FIRST, 2, 0), (FIRST, 2, 1), (FIRST, 2, 3), (ATTEND, 2),
    (THIRD, 1, 2), (FOURTH, 1, 3), (SECOND, 2, 3), (FOURTH, 1, 1), (ATTEND, 3), (SECOND, 2, 1), (ALONG, 1, 3, 0),
    (FIFTH, 0, 1), (SECOND, 2, 0), (ATTEND, 4), (ALONG, 1, 1, 0), (FOURTH, 1, 0), (ATTEND, 5), (FIFTH, 1, 1),
    (ROW, 0), (D_QKV, 0), (D_QKV, 1), (FOURTH, 1, 2), (ALONG, 1, 2, 0), (D_QKV, 2), (FIRST, 3, 3), (THIRD, 2, 0),
    (ROW, 1), (THIRD, 2, 3), (FIRST, 3, 2), (SECOND, 3, 3), (FIRST, 2, 2), (FIRST, 3, 0), (ROW, 2), (FIRST, 3, 1),
    (SECOND, 2, 2), (THIRD, 2, 1), (FOURTH, 2, 3), (SECOND, 3, 2), (THIRD, 3, 2), (SECOND, 3, 1), (ROW, 3),
    (D_TOK,), (FOURTH, 3, 2), (THIRD, 3, 3), (FOURTH, 2, 1), (THIRD, 3, 1), (SECOND, 3, 0), (ALONG, 2, 1, 0),
    (THIRD, 2, 2), (FOURTH, 2, 0), (ALONG, 2, 3, 0), (PUT, 0, 1), (FIFTH, 1, 0), (FOURTH, 3, 3), (ALONG, 3, 3, 0),
    (FOURTH, 3, 1), (FOURTH, 2, 2), (THIRD, 3, 0), (ALONG, 2, 2, 0), (ALONG, 3, 2, 0), (ALONG, 3, 1, 0),
    (FIFTH, 2, 0), (FOURTH, 3, 0), (ROW, 4), (PUT, 1, 0), (FIFTH, 3, 0), (PUT, 2, 0), (PUT, 0, 0), (PUT, 1, 1),
    (PUT, 3, 0),
)

FORWARD_DEEP = (False, False, False, False, True)
BACKWARD_DEEP = (True, True, False, False)
DOWN_ORDER = tuple(step[1] for step in BACKWARD_ORDER if step[0] == D_DOWN)


def run_in_order(order, steps):
    for name, *place in order:
        steps[name](*place)


def forward_kernel(
    tok, cot, valid, vectors, s_qkv, s_out, s_ff, s_down,
    o_out, o_qkvw, o_outw, o_ffw, o_downw, o_rows, o_sums, o_qkv, o_ctx, o_probs, o_nlt, o_scaled1,
    o_inv1, o_gu, o_hid, o_dh2, o_db,
    w_bias, w_qkv, w_out, w_ff, w_down, s_bias, v_dist, v_qkv, v_ctx, v_probs, v_scaled1, v_nl, v_gu,
    v_hid, v_acc, v_nlt, sends, recvs, locals_, outs,
):
    y, z, x, c = whereabouts()
    places = [w_bias, w_qkv, w_out, w_ff, w_down]
    shards = [s_bias, s_qkv, s_out, s_ff, s_down]
    g = [
        Gather(t, shards[t], places[t], shards[t].shape[0], t == 3, FORWARD_DEEP[t], sends, recvs, locals_)
        for t in range(5)
    ]
    length = tok.shape[0]
    lane = lax.broadcasted_iota(jnp.int32, (1, 128), 1)
    pending = []

    def save(src, dst):
        copy = pltpu.make_async_copy(src, dst, outs.at[len(pending)])
        copy.start()
        pending.append(copy)

    def dist():
        j = lax.broadcasted_iota(jnp.int32, (length, length), 0)
        i = lax.broadcasted_iota(jnp.int32, (length, length), 1)
        v_dist[...] = jnp.where(j < valid[0], jnp.abs(i - j).astype(F32), 1e33)

    def rows():
        total = w_bias[0:16, :].astype(F32)
        for k in range(1, 16):
            total = total + w_bias[16 * k : 16 * k + 16, :].astype(F32)
        o_rows[...] = total

    def project(n):
        part = dot(tok[...], w_qkv[768 * n : 768 * n + 768, :], 1, 1)
        if n == 0:
            part = (part + o_rows[0:1, :]).astype(BF).astype(F32) * 0.125
        if n == 2:
            part = part + o_rows[1:2, :]
        v_qkv[:, 768 * n : 768 * n + 768] = part.astype(BF)
        if n == 2:
            save(v_qkv, o_qkv)
            save(w_qkv, o_qkvw)

    def attend(pair):
        col = 128 * pair
        k_pair = v_qkv[:, 768 + col : 768 + col + 128]
        v_pair = v_qkv[:, 1536 + col : 1536 + col + 128]

        def one(chunk, carry):
            at = pl.multiple_of(chunk * 256, 256)
            results = []
            for hh in range(2):
                mine = (lane < 64) if hh == 0 else (lane >= 64)
                q_head = jnp.where(mine, v_qkv[pl.ds(at, 256), col : col + 128], jnp.zeros((), BF))
                scores = dot(k_pair, q_head, 1, 1)
                scores = scores - slope_of(2 * pair + hh) * v_dist[:, pl.ds(at, 256)]
                expo = jnp.exp(scores - jnp.max(scores, axis=0, keepdims=True))
                probs = (expo * (1.0 / jnp.sum(expo, axis=0, keepdims=True))).astype(BF)
                v_probs[2 * pair + hh, :, pl.ds(at, 256)] = probs
                results.append(dot(probs, v_pair, 0, 0))
            v_ctx[pl.ds(at, 256), col : col + 128] = jnp.where(
                lane < 64, results[0], results[1]
            ).astype(BF)
            return carry

        lax.fori_loop(0, length // 256, one, 0)
        save(v_probs.at[pl.ds(2 * pair, 2)], o_probs.at[pl.ds(2 * pair, 2)])
        if pair == 5:
            save(v_ctx, o_ctx)

    def first_norm():
        save(w_out, o_outw)
        h1 = dot(v_ctx[...], w_out[...], 1, 0) + o_rows[2:3, :] + tok[...].astype(F32)
        scaled1, inverse1 = normalise(h1)
        v_scaled1[...] = scaled1
        o_inv1[...] = jnp.broadcast_to(inverse1, o_inv1.shape)
        normed = scaled1 * o_rows[3:4, :] + o_rows[4:5, :]
        v_acc[...] = normed + o_rows[5:6, :]
        v_nl[...] = normed.astype(BF)
        v_nlt[...] = normed.astype(BF).T
        save(v_scaled1, o_scaled1)
        save(v_nlt, o_nlt)

    def feed(n):
        j = 4 * ((z + 1) % 2 if n < 4 else z % 2) + n % 4
        gate = dot(v_nl[...], w_ff[pl.ds(pl.multiple_of(j * 768, 768), 768), :], 1, 0)
        up = dot(v_nl[...], w_ff[pl.ds(pl.multiple_of((8 + j) * 768, 768), 768), :], 1, 0)
        gate = gate + o_rows[bias_at(j)]
        up = up + o_rows[bias_at(8 + j)]
        v_gu[0, j] = gate.astype(BF)
        v_gu[1, j] = up.astype(BF)
        v_hid[j] = (gate * cdf(gate) * up).astype(BF)
        if n == 7:
            save(w_ff, o_ffw)
            save(v_gu, o_gu)
            save(v_hid, o_hid)

    def down(i):
        plane = plane_at(z, i)
        for s in range(2):
            j = 2 * plane + s
            rows_j = pl.ds(pl.multiple_of(j * 384, 384), 384)
            v_acc[...] += dot(v_hid[j], w_down[rows_j, :], 1, 0)

    def second_norm():
        save(w_down, o_downw)
        scaled2, inverse2 = normalise(v_acc[...])
        o_out[...] = (scaled2 * o_rows[6:7, :] + o_rows[7:8, :]).astype(BF)
        grad = cot[...].astype(F32)
        d_h2 = norm_back(grad * o_rows[6:7, :], scaled2, inverse2)
        o_dh2[...] = d_h2
        o_db[...] = d_h2.astype(BF)
        o_sums[...] = jnp.zeros_like(o_sums)
        o_sums[0:1, :] = column_sum(d_h2.astype(BF).astype(F32))
        o_sums[1:2, :] = column_sum(grad * scaled2)
        o_sums[2:3, :] = column_sum(grad)

    def begin_along(t, i):
        for a in g[t].halves():
            if i < 3:
                g[t].to_plane(i, a).start()
            else:

                @pl.when(in_middle(z))
                def _():
                    g[t].to_plane(3, a).start()

    s_bias[...] = spread_vectors(vectors[...], index(z, x, c)).astype(BF)
    greet()
    run_in_order(
        FORWARD_ORDER,
        {
            OWN: lambda t: g[t].begin_plane(),
            ALONG: begin_along,
            SECOND: lambda t, i: g[t].second(i),
            THIRD: lambda t, i: g[t].third(i),
            FOURTH: lambda t, i: g[t].fourth(i),
            ARRIVED: lambda t, i: g[t].arrived(i),
            DIST: dist,
            ROWS: rows,
            QKV: project,
            ATTEND: attend,
            NORM: first_norm,
            FEED: feed,
            DOWN: down,
            END: second_norm,
        },
    )
    for t in range(5):
        g[t].finish()
    for copy in pending:
        copy.wait()


def backward_kernel(
    db, rows, sums, inv1, w_qkv, w_out, w_ff, w_down, scaled1, dh2, probs, gu, hid, tok_, qkv_, ctx_, nlt_,
    o_tok, o_qkv, o_out, o_ff, o_down, o_rows,
    v_qkvw, v_outw, v_ffw, v_downw, v_scaled1, v_dn, v_probs, v_gu, v_hid, tok, qkv, ctx, nlt, full_a, full_b,
    both, across, sides, columns, v_dctx, v_dqkv, v_sum, v_sums, sends, recvs, row_sends, row_recvs, loads, stages,
):
    y, z, x, c = whereabouts()
    lane = lax.broadcasted_iota(jnp.int32, (1, 128), 1)
    one_load = (
        (dh2, v_dn), (nlt_, nlt), (scaled1, v_scaled1), (ctx_, ctx),
        (w_out, v_outw), (qkv_, qkv), (tok_, tok), (w_qkv, v_qkvw),
    )

    def load(n):
        return pltpu.make_async_copy(*one_load[n], loads.at[n])

    def stage(kind, src, dst, slot):
        return pltpu.make_async_copy(src, dst, stages.at[kind, slot])

    hid_order = [2 * n + s for n in DOWN_ORDER for s in (0, 1)]

    def hid_stage(m):
        n = hid_order[m]
        return stage(0, hid.at[2 * plane_at(z, n // 2) + n % 2], v_hid.at[m % 2], m % 2)

    def chunk_of(n):
        return 4 * ((z + 1) % 2 if n < 4 else z % 2) + n % 4

    def ff_stages(n):
        j = chunk_of(n)
        s = n % 2
        rows_g = pl.ds(pl.multiple_of(j * 768, 768), 768)
        rows_u = pl.ds(pl.multiple_of((8 + j) * 768, 768), 768)
        rows_d = pl.ds(pl.multiple_of(j * 384, 384), 384)
        return [
            stage(1, w_ff.at[rows_g, :], v_ffw.at[s, 0], s),
            stage(2, w_ff.at[rows_u, :], v_ffw.at[s, 1], s),
            stage(3, w_down.at[rows_d, :], v_downw.at[s], s),
            stage(4, gu.at[0, j], v_gu.at[s, 0], s),
            stage(5, gu.at[1, j], v_gu.at[s, 1], s),
        ]

    def probs_stage(pair):
        return stage(6, probs.at[pl.ds(2 * pair, 2)], v_probs.at[pair % 2], pair % 2)

    def at_down(plane, x_, c_, h):
        return h * 3072 + index(plane, x_, c_) * 192

    def at_ff(plane, x_, c_, h):
        return (plane // 2) * 3072 + index(0, x_, c_) * 768 + h * 384

    def at_out(plane, x_, c_, h):
        return h * 768 + index(plane, x_, c_) * 48

    def at_qkv(plane, x_, c_, h):
        return 1536 + h * 2304 + index(plane, x_, c_) * 144

    shared = (both, across, sides, columns, sends, recvs)
    r_down = Reduce(0, 0, 192, BACKWARD_DEEP[0], at_down, full_a, *shared)
    r_ff1 = Reduce(1, 192, 384, BACKWARD_DEEP[1], at_ff, full_b, *shared)
    r_ff2 = Reduce(1, 192, 384, BACKWARD_DEEP[1], at_ff, full_a, *shared)
    r_out = Reduce(2, 576, 48, BACKWARD_DEEP[2], at_out, full_b, *shared)
    r_qkv = Reduce(3, 624, 144, BACKWARD_DEEP[3], at_qkv, full_b, *shared)

    def reducer(t, i):
        return (r_down, r_ff1 if i % 2 else r_ff2, r_out, r_qkv)[t]

    def start():
        load(0).wait()

    def d_down(i):
        for s in range(2):
            m = hid_order.index(2 * i + s)
            hid_stage(m).wait()
            part = dot(v_hid[m % 2], db[...], 0, 0)
            row = pl.multiple_of((2 * plane_at(z, i) + s) * 384, 384)
            full_a[pl.ds(row, 384), :] = part[:, :384].astype(BF)
            full_a[pl.ds(3072 + row, 384), :] = part[:, 384:].astype(BF)
            if m < 6:
                hid_stage(m + 2).start()

    def chunk(n):
        s = n % 2
        j = chunk_of(n)
        if n == 0:
            load(1).wait()
        for copy in ff_stages(n):
            copy.wait()
        d_hid = dot(db[...], v_downw[s], 1, 1).astype(BF).astype(F32)
        gate = v_gu[s, 0].astype(F32)
        up = v_gu[s, 1].astype(F32)
        below = cdf(gate)
        density = jnp.exp(-0.5 * gate * gate) * 0.3989422804014327
        d_gate = (d_hid * up * (below + gate * density)).astype(BF)
        d_up = (d_hid * (gate * below)).astype(BF)
        full = full_b if n < 4 else full_a
        full[pl.ds(768 * (n % 4), 768), :] = dot(nlt[...], d_gate, 1, 0).astype(BF)
        full[pl.ds(3072 + 768 * (n % 4), 768), :] = dot(nlt[...], d_up, 1, 0).astype(BF)
        v_sum[bias_at(j)] = column_sum(d_gate.astype(F32))
        v_sum[bias_at(8 + j)] = column_sum(d_up.astype(F32))
        v_dn[...] += dot(d_gate, v_ffw[s, 0], 1, 1) + dot(d_up, v_ffw[s, 1], 1, 1)
        if n < 6:
            for copy in ff_stages(n + 2):
                copy.start()

    def first_norm():
        d_normed = v_dn[...]
        load(2).wait()
        scaled = v_scaled1[...]
        v_sum[3:4, :] = column_sum(d_normed * scaled)
        v_sum[4:5, :] = column_sum(d_normed)
        v_sum[5:8, :] = sums[0:3, :]
        d_h1 = norm_back(d_normed * rows[3:4, :], scaled, inv1[:, 0:1])
        v_dn[...] = d_h1
        v_sum[2:3, :] = column_sum(d_h1.astype(BF).astype(F32))

    def d_out():
        load(3).wait()
        part = dot(ctx[...], v_dn[...].astype(BF), 0, 0)
        full_b[0:768, :] = part[:, :384].astype(BF)
        full_b[768:1536, :] = part[:, 384:].astype(BF)

    def d_context():
        load(4).wait()
        v_dctx[...] = dot(v_dn[...].astype(BF), v_outw[...], 1, 1).astype(BF)

    def attend_back(pair):
        col = 128 * pair
        if pair == 0:
            load(5).wait()
        probs_stage(pair).wait()
        q_pair = qkv[:, col : col + 128]
        k_pair = qkv[:, 768 + col : 768 + col + 128]
        v_pair = qkv[:, 1536 + col : 1536 + col + 128]
        d_pair = v_dctx[:, col : col + 128]
        product = d_pair.astype(F32) * ctx[:, col : col + 128].astype(F32)
        d_q, d_k, d_v = [], [], []
        for hh in range(2):
            mine = (lane < 64) if hh == 0 else (lane >= 64)
            inner = lax.dot_general(
                jnp.broadcast_to(mine.astype(F32), (8, 128)),
                product,
                (((1,), (1,)), ((), ())),
                preferred_element_type=F32,
                precision=lax.Precision.HIGHEST,
            )[0:1, :]
            d_probs = dot(v_pair, jnp.where(mine, d_pair, jnp.zeros((), BF)), 1, 1)
            probs_t = v_probs[pair % 2, hh]
            d_scores = (probs_t.astype(F32) * (d_probs - inner)).astype(BF)
            d_v.append(dot(probs_t, d_pair, 1, 0))
            d_k.append(dot(d_scores, q_pair, 1, 0))
            d_q.append(dot(d_scores, k_pair, 0, 0))
        v_dqkv[:, col : col + 128] = (jnp.where(lane < 64, d_q[0], d_q[1]) * 0.125).astype(BF)
        v_dqkv[:, 768 + col : 768 + col + 128] = jnp.where(lane < 64, d_k[0], d_k[1]).astype(BF)
        v_dqkv[:, 1536 + col : 1536 + col + 128] = jnp.where(lane < 64, d_v[0], d_v[1]).astype(BF)
        if pair < 4:
            probs_stage(pair + 2).start()
        if pair == 5:
            v_sum[0:1, :] = column_sum(v_dqkv[:, 0:768].astype(F32))
            v_sum[1:2, :] = column_sum(v_dqkv[:, 1536:2304].astype(F32))

    def d_qkv_weight(n):
        if n == 0:
            load(6).wait()
        part = dot(v_dqkv[:, 768 * n : 768 * n + 768], tok[...], 0, 0)
        full_b[1536 + 768 * n : 2304 + 768 * n, :] = part[:, :384].astype(BF)
        full_b[3840 + 768 * n : 4608 + 768 * n, :] = part[:, 384:].astype(BF)

    def d_tokens():
        load(7).wait()
        o_tok[...] = (dot(v_dqkv[...], v_qkvw[...], 1, 0) + v_dn[...]).astype(BF)

    def row_copy(n):
        device = (
            (y, index(z, x, 1 - c)), (y, index(z, 1 - x, c)), (1 - y, index(z, x, c)),
            *[(y, index(plane_at(z, i), x, c)) for i in (1, 2, 3)],
        )[n]
        return pltpu.make_async_remote_copy(
            src_ref=v_sum,
            dst_ref=v_sums.at[n],
            send_sem=row_sends.at[n],
            recv_sem=row_recvs.at[n],
            device_id=device,
            device_id_type=MESH,
        )

    def row_step(n):
        if 1 <= n <= 3:
            row_copy(n - 1).wait()
            v_sum[...] = v_sum[...] + v_sums[n - 1]
        if n < 3:
            row_copy(n).start()
        if n == 3:
            for m in (3, 4, 5):
                row_copy(m).start()
        if n == 4:
            for m in (3, 4, 5):
                row_copy(m).wait()
            o_rows[...] = v_sum[...] + v_sums[3] + v_sums[4] + v_sums[5]

    outs = (o_down, o_ff, o_out, o_qkv)
    hid_stage(0).start()
    hid_stage(1).start()
    load(0).start()
    load(1).start()
    for n in (0, 1):
        for copy in ff_stages(n):
            copy.start()
    for n in range(2, 8):
        load(n).start()
    probs_stage(0).start()
    probs_stage(1).start()
    greet()
    run_in_order(
        BACKWARD_ORDER,
        {
            START: start,
            D_DOWN: d_down,
            CHUNK: chunk,
            D_NORM: first_norm,
            D_OUT: d_out,
            D_CTX: d_context,
            ATTEND: attend_back,
            D_QKV: d_qkv_weight,
            D_TOK: d_tokens,
            ROW: row_step,
            FIRST: lambda t, i: reducer(t, i).first(i),
            SECOND: lambda t, i: reducer(t, i).second(i),
            THIRD: lambda t, i: reducer(t, i).third(i),
            FOURTH: lambda t, i: reducer(t, i).fourth(i),
            ALONG: lambda t, i, a: reducer(t, i).along(i, a),
            FIFTH: lambda t, a: reducer(t, 0).fifth(a),
            PUT: lambda t, a: reducer(t, 0).put(a, outs[t], t == 1),
        },
    )
    for t in range(4):
        reducer(t, 0).finish()


def finish_kernel(tok, qkv, out, ff, down, rows, fwd, *outs):
    o_fwd, o_tok, o_qkv, o_qv, o_out, o_outb, o_g1, o_s1, o_ff, o_ffb, o_down, o_downb, o_g2, o_s2 = outs
    k = lax.axis_index("fsdp")
    o_fwd[...] = fwd[...]
    o_tok[...] = tok[...]
    o_qkv[...] = qkv[...]
    o_out[...] = out[...]
    o_ff[...] = ff[...]
    o_down[...] = down[...]
    by_vector = (o_qv, o_outb, o_g1, o_s1, o_ffb, o_downb, o_g2, o_s2)
    for ref, (_, n, row) in zip(by_vector, VECTORS):
        per = 768 // n
        line = rows[pl.ds(row + k // per, 1), :]
        moved = pltpu.roll(jnp.broadcast_to(line, (8, 768)), ((768 - (k % per) * n) % 768), 1)
        ref[...] = moved[0:1, 0:n]


def fused_on_device(
    tokens,
    qkv_weight,
    qv_bias,
    out_weight,
    out_bias,
    norm1_gain,
    norm1_shift,
    ff_weight,
    ff_bias,
    down_weight,
    down_bias,
    norm2_gain,
    norm2_shift,
    pair_length,
    cotangent,
):
    length, width = tokens.shape
    vectors = jnp.concatenate(
        [qv_bias, out_bias, norm1_gain, norm1_shift, ff_bias, down_bias, norm2_gain, norm2_shift]
    )
    vectors = vectors.astype(F32).reshape(1, width)
    in_vmem = pl.BlockSpec(memory_space=pltpu.VMEM)
    in_smem = pl.BlockSpec(memory_space=pltpu.SMEM)
    anywhere = pl.BlockSpec(memory_space=pl.ANY)
    struct = jax.ShapeDtypeStruct
    dma = pltpu.SemaphoreType.DMA
    whole = [(256, 768), (2304, 768), (768, 768), (12288, 384), (3072, 768)]
    (
        output, w_qkv, w_out, w_ff, w_down, rows, sums, qkv, ctx, probs, nlt, scaled1, inv1, gu, hid, dh2, db,
    ) = pl.pallas_call(
        forward_kernel,
        name="forward",
        out_shape=[
            struct((length, width), BF),
            struct(whole[1], BF),
            struct(whole[2], BF),
            struct(whole[3], BF),
            struct(whole[4], BF),
            struct((16, width), F32),
            struct((8, width), F32),
            struct((length, 2304), BF),
            struct((length, width), BF),
            struct((HEADS, length, length), BF),
            struct((width, length), BF),
            struct((length, width), F32),
            struct((length, 128), F32),
            struct((2, 8, length, 384), BF),
            struct((8, length, 384), BF),
            struct((length, width), F32),
            struct((length, width), BF),
        ],
        in_specs=[in_vmem, in_vmem, in_smem, in_vmem] + [anywhere] * 4,
        out_specs=[in_vmem] + [anywhere] * 4 + [in_vmem] * 2 + [anywhere] * 5 + [in_vmem] + [anywhere] * 2
        + [in_vmem] * 2,
        scratch_shapes=[pltpu.VMEM(s, BF) for s in whole]
        + [
            pltpu.VMEM((16, width), BF),
            pltpu.VMEM((length, length), F32),
            pltpu.VMEM((length, 2304), BF),
            pltpu.VMEM((length, width), BF),
            pltpu.VMEM((HEADS, length, length), BF),
            pltpu.VMEM((length, width), F32),
            pltpu.VMEM((length, width), BF),
            pltpu.VMEM((2, 8, length, 384), BF),
            pltpu.VMEM((8, length, 384), BF),
            pltpu.VMEM((length, width), F32),
            pltpu.VMEM((width, length), BF),
            dma((5, Gather.SLOTS)),
            dma((5, Gather.SLOTS)),
            dma((5,)),
            dma((24,)),
        ],
        compiler_params=pltpu.CompilerParams(
            collective_id=0, has_side_effects=True, vmem_limit_bytes=60 * 2**20
        ),
    )(tokens, cotangent, pair_length, vectors, qkv_weight.T, out_weight, ff_weight, down_weight)
    grads = [struct((length, width), BF)] + [
        struct(s, F32) for s in ((144, width), (48, width), (768, 384), (192, width), (16, width))
    ]
    d_tokens, d_qkv, d_out, d_ff, d_down, d_rows = pl.pallas_call(
        backward_kernel,
        name="backward",
        out_shape=grads,
        in_specs=[in_vmem] * 4 + [anywhere] * 13,
        out_specs=[in_vmem] * 6,
        scratch_shapes=[
            pltpu.VMEM((2304, width), BF),
            pltpu.VMEM((width, width), BF),
            pltpu.VMEM((2, 2, 768, 384), BF),
            pltpu.VMEM((2, 384, width), BF),
            pltpu.VMEM((length, width), F32),
            pltpu.VMEM((length, width), F32),
            pltpu.VMEM((2, 2, length, length), BF),
            pltpu.VMEM((2, 2, length, 384), BF),
            pltpu.VMEM((2, length, 384), BF),
            pltpu.VMEM((length, width), BF),
            pltpu.VMEM((length, 2304), BF),
            pltpu.VMEM((length, width), BF),
            pltpu.VMEM((width, length), BF),
            pltpu.VMEM((6144, 384), BF),
            pltpu.VMEM((6144, 384), BF),
            pltpu.VMEM((768 * 16, 384), BF),
            pltpu.VMEM((768 * 4, 384), BF),
            pltpu.VMEM((768 * 8, 384), BF),
            pltpu.VMEM((768 * 12, 384), BF),
            pltpu.VMEM((length, width), BF),
            pltpu.VMEM((length, 2304), BF),
            pltpu.VMEM((16, width), F32),
            pltpu.VMEM((6, 16, width), F32),
            dma((4, Reduce.SLOTS)),
            dma((4, Reduce.SLOTS)),
            dma((6,)),
            dma((6,)),
            dma((8,)),
            dma((7, 2)),
        ],
        compiler_params=pltpu.CompilerParams(
            collective_id=1, has_side_effects=True, vmem_limit_bytes=63 * 2**20
        ),
    )(db, rows, sums, inv1, w_qkv, w_out, w_ff, w_down, scaled1, dh2, probs, gu, hid, tokens, qkv, ctx, nlt)

    def vector(n):
        return struct((1, n), F32)

    results = pl.pallas_call(
        finish_kernel,
        name="finish",
        out_shape=[
            struct((length, width), BF), grads[0], grads[1], vector(96), grads[2], vector(48), vector(48), vector(48),
            grads[3], vector(384), grads[4], vector(48), vector(48), vector(48),
        ],
        in_specs=[in_vmem] * 7,
        out_specs=[in_vmem] * 14,
    )(d_tokens, d_qkv, d_out, d_ff, d_down, d_rows, output)
    results = [r[0] if r.shape[0] == 1 else r for r in results]
    results[2] = results[2].T
    return tuple(results)


def solution(mesh):
    in_specs = (
        P(("rep", "fsdp"), None),
        P(None, "fsdp"),
        P("fsdp"),
        P("fsdp", None),
        P("fsdp"),
        P("fsdp"),
        P("fsdp"),
        P(None, "fsdp"),
        P("fsdp"),
        P("fsdp", None),
        P("fsdp"),
        P("fsdp"),
        P("fsdp"),
        P(("rep", "fsdp")),
        P(("rep", "fsdp"), None),
    )
    out_specs = (
        P(("rep", "fsdp"), None),
        P(("rep", "fsdp"), None),
        P(None, "fsdp"),
        P("fsdp"),
        P("fsdp", None),
        P("fsdp"),
        P("fsdp"),
        P("fsdp"),
        P(None, "fsdp"),
        P("fsdp"),
        P("fsdp", None),
        P("fsdp"),
        P("fsdp"),
        P("fsdp"),
    )
    planes = mesh.shape["rep"] == 2 and mesh.shape["fsdp"] == 16
    return jax.shard_map(
        fused_on_device if planes else plain_on_device, mesh=mesh, in_specs=in_specs, out_specs=out_specs, check_vma=False
    )
```

```python
import jax
import jax.numpy as jnp
from jax import lax
from jax.experimental import pallas as pl
from jax.experimental.pallas import tpu as pltpu
from jax.sharding import PartitionSpec as P

HEADS = 12
MESH = pl.DeviceIdType.MESH
BF = jnp.bfloat16
F32 = jnp.float32


def layer_norm(h, gain, shift):
    mean = jnp.mean(h, -1, keepdims=True)
    centered = h - mean
    spread = jnp.mean(centered * centered, -1, keepdims=True)
    return centered * lax.rsqrt(spread + 1e-05) * gain + shift


def inner_rows(left, right):
    return lax.dot_general(
        left, right, (((0,), (0,)), ((), ())), preferred_element_type=jnp.float32
    )


def times_transposed(left, right):
    return lax.dot_general(
        left, right, (((1,), (1,)), ((), ())), preferred_element_type=jnp.float32
    )


def score_block(query, keys, slope, valid):
    length = query.shape[0]
    place = jnp.arange(length, dtype=jnp.float32)
    scores = times_transposed(query, keys) * 0.125 - slope * jnp.abs(
        place[:, None] - place[None, :]
    )
    allowed = jnp.arange(length, dtype=jnp.int32) < valid
    return jnp.where(allowed[None, :], scores, -1e30)


def head_slopes():
    return 2.0 ** (-8.0 * jnp.arange(1, HEADS + 1, dtype=jnp.float32) / HEADS)


def forward(tokens, attention, feedforward, valid):
    qkv_weight, qv_bias, out_weight, out_bias, gain1, shift1 = attention
    ff_weight, ff_bias, down_weight, down_bias, gain2, shift2 = feedforward
    length, width = tokens.shape
    bias_f = qv_bias.astype(jnp.float32)
    full_bias = jnp.concatenate([bias_f[:width], jnp.zeros((width,), jnp.float32), bias_f[width:]])
    qkv = (jnp.dot(tokens, qkv_weight, preferred_element_type=jnp.float32) + full_bias).astype(
        jnp.bfloat16
    )
    per_head = qkv.reshape(length, 3, HEADS, width // HEADS).transpose(1, 2, 0, 3)

    def attend(item):
        query, keys, values, slope = item
        scores = score_block(query, keys, slope, valid)
        top = jnp.max(scores, -1, keepdims=True)
        expo = jnp.exp(scores - top)
        total = jnp.sum(expo, -1, keepdims=True)
        probs = (expo / total).astype(jnp.bfloat16)
        return (
            jnp.dot(probs, values, preferred_element_type=jnp.float32),
            top[:, 0] + jnp.log(total[:, 0]),
        )

    context, log_total = lax.map(attend, (per_head[0], per_head[1], per_head[2], head_slopes()))
    context = context.transpose(1, 0, 2).reshape(length, width).astype(jnp.bfloat16)
    attended = jnp.dot(context, out_weight, preferred_element_type=jnp.float32) + out_bias.astype(
        jnp.float32
    )
    residual1 = tokens.astype(jnp.float32) + attended
    normed = layer_norm(residual1, gain1.astype(jnp.float32), shift1.astype(jnp.float32))
    normed_low = normed.astype(jnp.bfloat16)
    gate_up = jnp.dot(normed_low, ff_weight, preferred_element_type=jnp.float32) + ff_bias.astype(
        jnp.float32
    )
    half = gate_up.shape[1] // 2
    hidden = (jax.nn.gelu(gate_up[:, :half], approximate=False) * gate_up[:, half:]).astype(
        jnp.bfloat16
    )
    residual2 = (
        normed
        + jnp.dot(hidden, down_weight, preferred_element_type=jnp.float32)
        + down_bias.astype(jnp.float32)
    )
    return (per_head, log_total, context, residual1, normed_low, gate_up, hidden, residual2)


def gelu_product(gate, up):
    return jax.nn.gelu(gate, approximate=False) * up


def plain_on_device(
    tokens,
    qkv_weight,
    qv_bias,
    out_weight,
    out_bias,
    norm1_gain,
    norm1_shift,
    ff_weight,
    ff_bias,
    down_weight,
    down_bias,
    norm2_gain,
    norm2_shift,
    pair_length,
    cotangent,
):
    valid = pair_length[0]
    attention = (
        lax.all_gather(qkv_weight, "fsdp", axis=1, tiled=True),
        lax.all_gather(qv_bias, "fsdp", axis=0, tiled=True),
        lax.all_gather(out_weight, "fsdp", axis=0, tiled=True),
        lax.all_gather(out_bias, "fsdp", axis=0, tiled=True),
        lax.all_gather(norm1_gain, "fsdp", axis=0, tiled=True),
        lax.all_gather(norm1_shift, "fsdp", axis=0, tiled=True),
    )
    feedforward = (
        lax.all_gather(ff_weight, "fsdp", axis=1, tiled=True),
        lax.all_gather(ff_bias, "fsdp", axis=0, tiled=True),
        lax.all_gather(down_weight, "fsdp", axis=0, tiled=True),
        lax.all_gather(down_bias, "fsdp", axis=0, tiled=True),
        lax.all_gather(norm2_gain, "fsdp", axis=0, tiled=True),
        lax.all_gather(norm2_shift, "fsdp", axis=0, tiled=True),
    )
    stored = forward(tokens, attention, feedforward, valid)
    gain2 = feedforward[4].astype(jnp.float32)
    shift2 = feedforward[5].astype(jnp.float32)
    output = layer_norm(stored[7], gain2, shift2).astype(jnp.bfloat16)
    per_head, log_total, context, residual1, normed_low, gate_up, hidden, residual2 = stored
    full_qkv, bias_unused, full_out, out_unused, gain1, shift1 = attention
    full_ff, ff_unused, full_down, down_unused, gain_unused, shift_unused = feedforward
    length, width = tokens.shape
    unused_out, back_second = jax.vjp(layer_norm, residual2, gain2, shift2)
    d_res2, d_gain2, d_shift2 = back_second(cotangent.astype(jnp.float32))
    d_branch = d_res2.astype(jnp.bfloat16)
    d_down = inner_rows(hidden, d_branch)
    d_down_bias = jnp.sum(d_branch.astype(jnp.float32), 0)
    d_hidden = times_transposed(d_branch, full_down).astype(jnp.bfloat16)
    half = gate_up.shape[1] // 2
    unused_prod, back_gelu = jax.vjp(gelu_product, gate_up[:, :half], gate_up[:, half:])
    d_gate, d_up = back_gelu(d_hidden.astype(jnp.float32))
    d_gate_up = jnp.concatenate([d_gate, d_up], 1).astype(jnp.bfloat16)
    d_ff = inner_rows(normed_low, d_gate_up)
    d_ff_bias = jnp.sum(d_gate_up.astype(jnp.float32), 0)
    d_normed = times_transposed(d_gate_up, full_ff) + d_res2
    unused_norm, back_first = jax.vjp(
        layer_norm, residual1, gain1.astype(jnp.float32), shift1.astype(jnp.float32)
    )
    d_res1, d_gain1, d_shift1 = back_first(d_normed)
    ff_terms = (d_ff, d_ff_bias, d_down, d_down_bias, d_gain2, d_shift2)
    ff_grads = (
        lax.psum_scatter(ff_terms[0], "fsdp", scatter_dimension=1, tiled=True),
        lax.psum_scatter(ff_terms[1], "fsdp", scatter_dimension=0, tiled=True),
        lax.psum_scatter(ff_terms[2], "fsdp", scatter_dimension=0, tiled=True),
        lax.psum_scatter(ff_terms[3], "fsdp", scatter_dimension=0, tiled=True),
        lax.psum_scatter(ff_terms[4], "fsdp", scatter_dimension=0, tiled=True),
        lax.psum_scatter(ff_terms[5], "fsdp", scatter_dimension=0, tiled=True),
    )
    ff_grads = (
        lax.psum(ff_grads[0].astype(jnp.bfloat16), "rep").astype(jnp.float32),
        lax.psum(ff_grads[1].astype(jnp.bfloat16), "rep").astype(jnp.float32),
        lax.psum(ff_grads[2].astype(jnp.bfloat16), "rep").astype(jnp.float32),
        lax.psum(ff_grads[3].astype(jnp.bfloat16), "rep").astype(jnp.float32),
        lax.psum(ff_grads[4].astype(jnp.bfloat16), "rep").astype(jnp.float32),
        lax.psum(ff_grads[5].astype(jnp.bfloat16), "rep").astype(jnp.float32),
    )
    d_attended = d_res1.astype(jnp.bfloat16)
    d_out = inner_rows(context, d_attended)
    d_out_bias = jnp.sum(d_attended.astype(jnp.float32), 0)
    d_context = times_transposed(d_attended, full_out).astype(jnp.bfloat16)
    d_context = d_context.reshape(length, HEADS, width // HEADS).transpose(1, 0, 2)

    def attend_back(item):
        query, keys, values, grad_context, total_log, slope = item
        scores = score_block(query, keys, slope, valid)
        probs = jnp.exp(scores - total_log[:, None])
        probs_low = probs.astype(jnp.bfloat16)
        d_probs = times_transposed(grad_context, values)
        d_scores = (probs * (d_probs - jnp.sum(probs * d_probs, -1, keepdims=True))).astype(
            jnp.bfloat16
        )
        d_query = jnp.dot(d_scores, keys, preferred_element_type=jnp.float32) * 0.125
        d_keys = inner_rows(d_scores, query) * 0.125
        d_values = inner_rows(probs_low, grad_context)
        return (d_query, d_keys, d_values)

    d_query, d_keys, d_values = lax.map(
        attend_back, (per_head[0], per_head[1], per_head[2], d_context, log_total, head_slopes())
    )
    d_qkv = (
        jnp.stack([d_query, d_keys, d_values])
        .transpose(2, 0, 1, 3)
        .reshape(length, 3 * width)
        .astype(jnp.bfloat16)
    )
    d_qkv_w = inner_rows(tokens, d_qkv)
    column_sums = jnp.sum(d_qkv.astype(jnp.float32), 0)
    d_qv = jnp.concatenate([column_sums[:width], column_sums[2 * width :]])
    d_tokens = (times_transposed(d_qkv, full_qkv) + d_res1).astype(jnp.bfloat16)
    at_terms = (d_qkv_w, d_qv, d_out, d_out_bias, d_gain1, d_shift1)
    at_grads = (
        lax.psum_scatter(at_terms[0], "fsdp", scatter_dimension=1, tiled=True),
        lax.psum_scatter(at_terms[1], "fsdp", scatter_dimension=0, tiled=True),
        lax.psum_scatter(at_terms[2], "fsdp", scatter_dimension=0, tiled=True),
        lax.psum_scatter(at_terms[3], "fsdp", scatter_dimension=0, tiled=True),
        lax.psum_scatter(at_terms[4], "fsdp", scatter_dimension=0, tiled=True),
        lax.psum_scatter(at_terms[5], "fsdp", scatter_dimension=0, tiled=True),
    )
    at_grads = (
        lax.psum(at_grads[0].astype(jnp.bfloat16), "rep").astype(jnp.float32),
        lax.psum(at_grads[1].astype(jnp.bfloat16), "rep").astype(jnp.float32),
        lax.psum(at_grads[2].astype(jnp.bfloat16), "rep").astype(jnp.float32),
        lax.psum(at_grads[3].astype(jnp.bfloat16), "rep").astype(jnp.float32),
        lax.psum(at_grads[4].astype(jnp.bfloat16), "rep").astype(jnp.float32),
        lax.psum(at_grads[5].astype(jnp.bfloat16), "rep").astype(jnp.float32),
    )
    return (
        output,
        d_tokens,
        at_grads[0],
        at_grads[1],
        at_grads[2],
        at_grads[3],
        at_grads[4],
        at_grads[5],
        ff_grads[0],
        ff_grads[1],
        ff_grads[2],
        ff_grads[3],
        ff_grads[4],
        ff_grads[5],
    )


def dot(left, right, left_dim, right_dim):
    return lax.dot_general(
        left, right, (((left_dim,), (right_dim,)), ((), ())), preferred_element_type=F32
    )


def whereabouts():
    y = lax.axis_index("rep")
    k = lax.axis_index("fsdp")
    return y, k // 4, (k // 2) % 2, k % 2


def index(z, x, c):
    return z * 4 + x * 2 + c


def plane_at(z, i):
    return (z, z + 1 - 2 * (z % 2), (z + 2) % 4, 3 - z)[i]


def in_middle(z):
    return (z == 1) | (z == 2)


def greet():
    y, z, x, c = whereabouts()
    friends = [(y, index(z, x, 1 - c)), (y, index(z, 1 - x, c)), (1 - y, index(z, x, c))]
    friends += [(y, index(plane_at(z, i), x, c)) for i in (1, 2, 3)]
    barrier = pltpu.get_barrier_semaphore()
    for friend in friends:
        pl.semaphore_signal(barrier, inc=1, device_id=friend, device_id_type=MESH)
    pl.semaphore_wait(barrier, len(friends))


class Gather:
    Z, X, Y, D, C = 0, 8, 12, 16, 20
    SLOTS = 28

    def __init__(self, t, src, dst, rows, pitch, start, by_row, deep, sends, recvs, locals_):
        self.t, self.src, self.dst, self.rows, self.by_row, self.deep = t, src, dst, rows, by_row, deep
        self.pitch, self.start = pitch, start
        self.sends, self.recvs, self.locals_ = sends, recvs, locals_
        self.y, self.z, self.x, self.c = whereabouts()

    def plane(self, i):
        return plane_at(self.z, i)

    def half(self, ref, base, h):
        if self.by_row:
            n = self.rows // 2
            return ref.at[pl.ds(pl.multiple_of(base + h * n, 16), n), :]
        n = ref.shape[1] // 2
        return ref.at[pl.ds(base, self.rows), pl.ds(pl.multiple_of(h * n, 128), n)]

    def part(self, k, h):
        return self.half(self.dst, pl.multiple_of(k * self.pitch + self.start, 16), h)

    def shard(self, k):
        return self.dst.at[pl.ds(pl.multiple_of(k * self.pitch + self.start, 16), self.rows), :]

    def whole(self):
        return self.src.at[pl.ds(self.start, self.rows), :]

    def copy(self, slot, src, dst, device, arrival=None):
        return pltpu.make_async_remote_copy(
            src_ref=src,
            dst_ref=dst,
            send_sem=self.sends.at[self.t, slot],
            recv_sem=self.recvs.at[self.t, slot if arrival is None else arrival],
            device_id=device,
            device_id_type=MESH,
        )

    def halves(self):
        return (0, 1) if self.deep else (0,)

    def to_plane(self, i, a):
        h = 1 - self.y if a else self.y
        k = index(self.z, self.x, self.c)
        device = (self.y, index(self.plane(i), self.x, self.c))
        return self.copy(self.Z + 2 * i + a, self.half(self.src, self.start, h), self.part(k, h), device)

    def relay(self, a):
        h = 1 - self.y if a else self.y
        k = index(self.plane(2), self.x, self.c)
        device = (self.y, index(self.plane(1), self.x, self.c))
        return self.copy(self.Z + a, self.part(k, h), self.part(k, h), device, self.Z + 6 + a)

    def to_x(self, i):
        k = index(self.plane(i), self.x, self.c)
        src = self.half(self.src, self.start, self.y) if i == 0 else self.part(k, self.y)
        return self.copy(
            self.X + i, src, self.part(k, self.y), (self.y, index(self.z, 1 - self.x, self.c))
        )

    def to_y(self, i):
        k = index(self.plane(i), self.x, self.c)
        part = self.part(k, self.y)
        return self.copy(self.Y + i, part, part, (1 - self.y, index(self.z, self.x, self.c)))

    def onward(self, i):
        c = 0 if i == 0 or self.deep else self.c
        k = index(self.plane(i), (1 - self.x) * (1 - c) + self.x * c, self.c)
        part = self.part(k, self.y * (1 - c) + (1 - self.y) * c)
        x = self.x * (1 - c) + (1 - self.x) * c
        y = self.y * c + (1 - self.y) * (1 - c)
        return self.copy(self.D + i, part, part, (y, index(self.z, x, self.c)))

    def to_core(self, i, home):
        k = index(self.plane(i), self.x if home else 1 - self.x, self.c)
        src = self.whole() if home and i == 0 else self.shard(k)
        device = (self.y, index(self.z, self.x, 1 - self.c))
        return self.copy(self.C + i + (0 if home else 4), src, self.shard(k), device)

    def own(self):
        return pltpu.make_async_copy(
            self.whole(), self.shard(index(self.z, self.x, self.c)), self.locals_.at[self.t]
        )

    def begin(self):
        for a in self.halves():
            for i in (2, 1):
                self.to_plane(i, a).start()

            @pl.when(in_middle(self.z))
            def _():
                self.to_plane(3, a).start()

    def begin_plane(self):
        self.to_x(0).start()
        self.to_core(0, True).start()
        self.own().start()

    def second(self, i):
        if i == 0:
            return
        for a in self.halves():
            self.to_plane(i, a).wait_recv()
            if i == 2:

                @pl.when(in_middle(self.z))
                def _():
                    self.relay(a).start()

            if a == 0:
                self.to_x(i).start()
                if not self.deep:
                    self.to_y(i).start()
        if self.deep:
            self.to_core(i, True).start()

    def third(self, i):
        if i and not self.deep:
            self.to_y(i).wait_recv()
            self.to_core(i, True).start()
        self.to_x(i).wait_recv()
        self.onward(i).start()

    def fourth(self, i):
        self.onward(i).wait_recv()
        self.to_core(i, False).start()

    def arrived(self, i):
        self.to_core(i, True).wait_recv()
        self.to_core(i, False).wait_recv()
        if i == 0:
            self.own().wait()

    def finish(self):
        for a in self.halves():
            for i in (1, 2):
                self.to_plane(i, a).wait_send()

            @pl.when(in_middle(self.z))
            def _():
                self.to_plane(3, a).wait_send()
                self.relay(a).wait_send()

        for i in range(4):
            self.to_x(i).wait_send()
            if i and not self.deep:
                self.to_y(i).wait_send()
            self.onward(i).wait_send()
            self.to_core(i, True).wait_send()
            self.to_core(i, False).wait_send()


class Reduce:
    CORE, DIAGONAL, EARLY, LATE, PLANE, ARRIVE, LAST, SLOTS = 0, 4, 5, 6, 7, 36, 38, 40

    def __init__(self, t, base, rows, deep, starts, at, full, both, across, sides, columns, sends, recvs):
        self.t, self.base, self.rows, self.deep, self.at = t, base, rows, deep, at
        self.full, self.both, self.across, self.sides, self.columns = full, both, across, sides, columns
        self.starts, self.sends, self.recvs = starts, sends, recvs
        self.y, self.z, self.x, self.c = whereabouts()

    def copy(self, slot, src, dst, device, arrival=None):
        return pltpu.make_async_remote_copy(
            src_ref=src,
            dst_ref=dst,
            send_sem=self.sends.at[self.t, slot],
            recv_sem=self.recvs.at[self.t, slot if arrival is None else arrival],
            device_id=device,
            device_id_type=MESH,
        )

    def rows_of(self, ref, row):
        return ref.at[pl.ds(pl.multiple_of(row, 16), self.rows), :]

    def unit(self, i, away_x, c, h):
        x = 1 - self.x if away_x else self.x
        return self.rows_of(self.full, self.at(plane_at(self.z, i), x, c, h))

    def mine(self, i, away_x, away_h):
        n = i * 4 + away_x * 2 + away_h
        return self.rows_of(self.both, self.base * 16 + n * self.rows)

    def side(self, i, s):
        n = (i + s if i == 0 else i + 1) if self.deep else i * 2 + s
        return self.rows_of(self.sides, self.starts[0] + n * self.rows)

    def cross(self, i):
        return self.rows_of(self.across, self.starts[1] + (i - 1 if self.deep else i) * self.rows)

    def column(self, n, a):
        return self.rows_of(self.columns, self.starts[2] + (2 * n + a if self.deep else n) * self.rows)

    def halves(self):
        return (0, 1) if self.deep else (0,)

    def way(self, i):
        return 0 if self.deep else (1 if i == 0 else self.c)

    def neighbour(self, over_x):
        return (
            self.y * over_x + (1 - self.y) * (1 - over_x),
            index(self.z, (1 - self.x) * over_x + self.x * (1 - over_x), self.c),
        )

    def to_core(self, i, n):
        device = (self.y, index(self.z, self.x, 1 - self.c))
        h = 1 - self.y if n % 2 else self.y
        src = self.unit(i, n // 2, 1 - self.c, h)
        return self.copy(i * 9 + n, src, self.mine(i, n // 2, n % 2), device)

    def diagonal(self, i):
        device = self.neighbour(self.way(i))
        return self.copy(i * 9 + self.DIAGONAL, self.mine(i, 1, 1), self.cross(i), device)

    def early(self, i):
        w = self.way(i)
        return self.copy(i * 9 + self.EARLY, self.mine(i, w, 1 - w), self.side(i, 0), self.neighbour(w))

    def late(self, i):
        w = self.way(i)
        return self.copy(i * 9 + self.LATE, self.mine(i, 1 - w, w), self.side(i, 1), self.neighbour(1 - w))

    def over_x(self, i, a):
        slot = i * 9 + (self.LATE if a else self.EARLY)
        return self.copy(slot, self.mine(i, 1, a), self.side(i, a), self.neighbour(1))

    def to_plane(self, i, a):
        slot = i * 9 + self.PLANE + a
        src = self.mine(i, 0, a)
        if i < 3:
            device = (self.y, index(plane_at(self.z, i), self.x, self.c))
            return self.copy(slot, src, self.column(i - 1, a), device)
        near, far = plane_at(self.z, 1), plane_at(self.z, 3)
        middle = (self.z % 3 + 1) // 2
        plane = far * middle + near * (1 - middle)
        arrival = slot * middle + (self.ARRIVE + a) * (1 - middle)
        return self.copy(
            slot, src, self.column(3 - middle, a), (self.y, index(plane, self.x, self.c)), arrival
        )

    def handed(self, a):
        slot = 3 * 9 + self.PLANE + a
        device = (self.y, index(plane_at(self.z, 1), self.x, self.c))
        return self.copy(slot, self.mine(3, 0, a), self.column(3, a), device, self.ARRIVE + a)

    def mirrored(self, a):
        slot = 3 * 9 + self.PLANE + a
        device = (self.y, index(plane_at(self.z, 3), self.x, self.c))
        return self.copy(slot, self.mine(3, 0, a), self.column(2, a), device)

    def last(self, a):
        device = (1 - self.y, index(self.z, self.x, self.c))
        b = 1 - a if self.deep else a
        return self.copy(self.LAST + a, self.column(4, a), self.column(5, b), device, self.LAST + b)

    def first(self, i):
        for n in (3, 2, 1, 0):
            self.to_core(i, n).start()

    def second(self, i):
        for n in (3, 2, 1, 0):
            self.to_core(i, n).wait()
            h = 1 - self.y if n % 2 else self.y
            part = self.mine(i, n // 2, n % 2)
            part[...] = part[...] + self.unit(i, n // 2, self.c, h)[...]
            if self.deep and i == 0:
                if n > 1:
                    self.over_x(i, n - 2).start()
            elif n == 3:
                self.diagonal(i).start()
        if not self.deep:
            self.early(i).start()

    def third(self, i):
        if self.deep and i == 0:
            return
        w = self.way(i)
        self.diagonal(i).wait_recv()
        part = self.mine(i, 1 - w, w)
        part[...] = part[...] + self.cross(i)[...]
        if self.deep:
            self.over_x(i, 0).start()
        else:
            self.late(i).start()

    def fourth(self, i):
        if self.deep:
            for a in (0, 1) if i == 0 else (0,):
                self.over_x(i, a).wait_recv()
                part = self.mine(i, 0, a)
                part[...] = part[...] + self.side(i, a)[...]
            return
        self.early(i).wait_recv()
        self.late(i).wait_recv()
        part = self.mine(i, 0, 0)
        total = part[...].astype(F32) + self.side(i, 0)[...].astype(F32)
        part[...] = (total + self.side(i, 1)[...].astype(F32)).astype(BF)

    def along(self, i, a):
        if i == 2:

            @pl.when(in_middle(self.z))
            def _():
                self.handed(a).wait_recv()
                part = self.mine(2, 0, a)
                part[...] = part[...] + self.column(3, a)[...]

        self.to_plane(i, a).start()

    def fifth(self, a):
        for i in (1, 2):
            self.to_plane(i, a).wait_recv()
        total = self.mine(0, 0, a)[...].astype(F32)
        total = total + self.column(0, a)[...].astype(F32) + self.column(1, a)[...].astype(F32)

        @pl.when(in_middle(self.z))
        def _():
            self.mirrored(a).wait_recv()
            self.column(4, a)[...] = (total + self.column(2, a)[...].astype(F32)).astype(BF)

        @pl.when(jnp.logical_not(in_middle(self.z)))
        def _():
            self.column(4, a)[...] = total.astype(BF)

        self.last(a).start()

    def put(self, a, out, semaphore):
        self.last(a).wait_send()
        self.last(1 - a if self.deep else a).wait_recv()
        here, there = self.y, 1 - self.y
        own, other = self.column(4, a), self.column(5, a)
        if self.deep:
            own[...] = (own[...].astype(F32) + other[...].astype(F32)).astype(BF)
            pairs = [((there if a else here), own)]
        else:
            pairs = [(here, own), (there, other)]
        copies = [pltpu.make_async_copy(v, out.at[h], semaphore.at[self.t, a + n]) for n, (h, v) in enumerate(pairs)]
        for copy in copies:
            copy.start()
        return copies

    def finish(self):
        for i in range(4):
            if self.deep:
                if i:
                    self.diagonal(i).wait_send()
                self.over_x(i, 0).wait_send()
                if i == 0:
                    self.over_x(i, 1).wait_send()
            else:
                self.diagonal(i).wait_send()
                self.early(i).wait_send()
                self.late(i).wait_send()
            if i:
                for a in self.halves():
                    self.to_plane(i, a).wait_send()


def slope_of(head):
    return jnp.exp2(jnp.full((1, 1), head + 1, jnp.int32).astype(F32) * (-8.0 / HEADS))


def normalise(h):
    centered = h - jnp.mean(h, -1, keepdims=True)
    inverse = lax.rsqrt(jnp.mean(centered * centered, -1, keepdims=True) + 1e-05)
    return centered * inverse, inverse


def norm_back(d_scaled, scaled, inverse):
    mean1 = jnp.mean(d_scaled, -1, keepdims=True)
    mean2 = jnp.mean(d_scaled * scaled, -1, keepdims=True)
    return inverse * (d_scaled - mean1 - scaled * mean2)


def column_sum(v):
    return jnp.sum(v, axis=0, keepdims=True)


def cdf(gate):
    return 0.5 * (1.0 + lax.erf(gate * 0.7071067811865476))


VECTORS = (
    (0, 96, 0), (96, 48, 2), (144, 48, 3), (192, 48, 4), (240, 384, 8), (624, 48, 5), (672, 48, 6), (720, 48, 7),
)


def spread_vectors(shards, k):
    lane = lax.broadcasted_iota(jnp.int32, (16, 768), 1)
    line = lax.broadcasted_iota(jnp.int32, (16, 768), 0)
    wide = jnp.broadcast_to(shards, (16, 768))
    rows = jnp.zeros((16, 768), F32)
    for start, n, row in VECTORS:
        per = 768 // n
        shift = ((k % per) * n - start + 768) % 768
        here = (lane // n == k % per) & (line == row + k // per)
        rows = jnp.where(here, pltpu.roll(wide, shift, 1), rows)
    return rows


(
    OWN, ALONG, SECOND, THIRD, FOURTH, ARRIVED, DIST, ROWS, QKV, ATTEND, NORM, LOAD, FEED, DOWN, MIDDLE,
    D_DOWN, CHUNK, D_NORM, D_OUT, D_CTX, D_ATTEND, D_QKV, D_TOK, ROW, R_FIRST, R_SECOND, R_THIRD, R_FOURTH, R_ALONG, R_FIFTH, R_PUT,
) = range(31)

ORDER = (
    (ALONG, 2, 2), (ALONG, 2, 3), (OWN, 2), (OWN, 0), (ALONG, 0, 2), (ALONG, 2, 1), (OWN, 4), (ALONG, 1, 2),
    (ALONG, 1, 1), (ALONG, 3, 1), (SECOND, 2, 1), (ALONG, 0, 3), (THIRD, 0, 0), (THIRD, 2, 0), (SECOND, 2, 2),
    (ALONG, 0, 1), (OWN, 3), (OWN, 5), (ALONG, 3, 2), (SECOND, 0, 2), (OWN, 1), (THIRD, 4, 0), (ALONG, 1, 3),
    (ALONG, 4, 2), (THIRD, 3, 0), (THIRD, 2, 2), (SECOND, 1, 1), (FOURTH, 3, 0), (ALONG, 3, 3), (SECOND, 0, 3),
    (SECOND, 3, 1), (THIRD, 0, 2), (SECOND, 1, 2), (ALONG, 4, 3), (SECOND, 0, 1), (FOURTH, 0, 0), (SECOND, 1, 3),
    (FOURTH, 4, 0), (FOURTH, 2, 2), (ALONG, 4, 1), (DIST,), (THIRD, 2, 1), (THIRD, 1, 2), (FOURTH, 2, 0),
    (THIRD, 1, 0), (SECOND, 3, 2), (SECOND, 4, 1), (ARRIVED, 3, 0), (SECOND, 2, 3), (THIRD, 5, 0), (THIRD, 1, 3),
    (FOURTH, 2, 1), (FOURTH, 1, 2), (FOURTH, 1, 0), (THIRD, 1, 1), (THIRD, 0, 3), (SECOND, 4, 2), (THIRD, 0, 1),
    (ALONG, 5, 1), (ALONG, 5, 2), (ARRIVED, 0, 0), (SECOND, 3, 3), (FOURTH, 0, 2), (FOURTH, 0, 1), (FOURTH, 1, 1),
    (ARRIVED, 4, 0), (THIRD, 4, 2), (FOURTH, 0, 3), (ARRIVED, 0, 2), (THIRD, 4, 1), (ARRIVED, 0, 3),
    (ARRIVED, 1, 0), (THIRD, 3, 1), (ARRIVED, 0, 1), (FOURTH, 1, 3), (THIRD, 3, 3), (ARRIVED, 1, 1),
    (FOURTH, 4, 2), (ROWS,), (ARRIVED, 1, 3), (SECOND, 4, 3), (ARRIVED, 1, 2), (QKV, 0), (QKV, 1), (THIRD, 3, 2),
    (FOURTH, 3, 1), (QKV, 2), (THIRD, 4, 3), (ATTEND, 0), (ALONG, 5, 3), (SECOND, 5, 2), (THIRD, 2, 3),
    (FOURTH, 4, 1), (FOURTH, 3, 3), (ARRIVED, 2, 0), (ATTEND, 1), (ARRIVED, 3, 1), (ATTEND, 2), (FOURTH, 4, 3),
    (SECOND, 5, 1), (FOURTH, 5, 0), (THIRD, 5, 2), (ATTEND, 3), (ARRIVED, 2, 1), (ARRIVED, 3, 3), (ARRIVED, 2, 2),
    (ARRIVED, 4, 3), (FOURTH, 2, 3), (FOURTH, 3, 2), (ATTEND, 4), (ARRIVED, 4, 1), (LOAD, 0), (ATTEND, 5),
    (ARRIVED, 2, 3), (SECOND, 5, 3), (LOAD, 1), (ARRIVED, 4, 2), (THIRD, 5, 1), (NORM,), (ARRIVED, 3, 2),
    (FEED, 0), (ARRIVED, 5, 0), (LOAD, 2), (FOURTH, 5, 2), (FEED, 1), (LOAD, 3), (ARRIVED, 5, 2), (THIRD, 5, 3),
    (FEED, 2), (FOURTH, 5, 1), (FEED, 3), (DOWN, 0), (ARRIVED, 5, 1), (FOURTH, 5, 3), (DOWN, 2), (DOWN, 1),
    (ARRIVED, 5, 3), (DOWN, 3), (MIDDLE,), (D_DOWN, 0), (R_FIRST, 0, 0), (D_DOWN, 3), (D_DOWN, 2), (R_FIRST, 0, 3),
    (R_SECOND, 0, 0), (D_DOWN, 1), (R_FIRST, 0, 1), (R_SECOND, 0, 3), (R_FIRST, 0, 2), (CHUNK, 0),
    (R_SECOND, 0, 1), (CHUNK, 1), (R_FIRST, 1, 3), (R_SECOND, 0, 2), (CHUNK, 2), (R_SECOND, 1, 3), (R_THIRD, 0, 3),
    (R_ALONG, 1, 3, 1), (R_THIRD, 0, 2), (R_THIRD, 0, 1), (CHUNK, 3), (R_FIRST, 1, 2), (R_FIRST, 1, 1),
    (R_FIRST, 1, 0), (R_THIRD, 1, 3), (R_SECOND, 1, 2), (R_ALONG, 1, 2, 1), (D_NORM,), (R_SECOND, 1, 1), (D_OUT,),
    (R_SECOND, 1, 0), (D_CTX,), (R_FOURTH, 1, 3), (R_FOURTH, 0, 3), (R_ALONG, 0, 3, 0), (R_FIRST, 2, 2),
    (R_ALONG, 1, 1, 1), (D_ATTEND, 0), (D_ATTEND, 1), (D_ATTEND, 2), (R_FOURTH, 0, 2), (R_THIRD, 0, 0),
    (R_ALONG, 1, 3, 0), (D_ATTEND, 3), (R_FIRST, 2, 1), (R_FOURTH, 0, 1), (R_FIRST, 2, 3), (D_ATTEND, 4),
    (R_SECOND, 2, 1), (D_ATTEND, 5), (R_SECOND, 2, 3), (D_QKV, 0), (ROW, 0), (R_FIRST, 2, 0), (R_FOURTH, 0, 0),
    (R_FOURTH, 1, 0), (ROW, 1), (R_THIRD, 1, 2), (D_QKV, 1), (R_ALONG, 0, 2, 0), (R_FIFTH, 1, 1),
    (R_ALONG, 0, 1, 0), (D_QKV, 2), (R_THIRD, 2, 1), (R_FIRST, 3, 3), (R_FIRST, 3, 2), (R_THIRD, 2, 3),
    (R_FOURTH, 2, 3), (R_FOURTH, 1, 2), (ROW, 2), (R_THIRD, 1, 1), (R_SECOND, 3, 3), (R_ALONG, 1, 2, 0),
    (R_FIRST, 3, 1), (R_FIFTH, 0, 0), (R_FOURTH, 1, 1), (R_THIRD, 3, 3), (R_ALONG, 1, 1, 0), (R_SECOND, 3, 2),
    (R_THIRD, 3, 2), (R_SECOND, 3, 1), (D_TOK,), (R_FIRST, 3, 0), (ROW, 3), (R_FOURTH, 3, 3), (R_THIRD, 3, 1),
    (R_SECOND, 2, 2), (R_FIFTH, 1, 0), (R_ALONG, 3, 3, 0), (R_FOURTH, 3, 1), (R_SECOND, 2, 0), (R_FOURTH, 3, 2),
    (R_SECOND, 3, 0), (R_PUT, 0, 0), (R_FOURTH, 2, 1), (R_ALONG, 2, 3, 0), (R_THIRD, 2, 2), (R_THIRD, 2, 0),
    (R_ALONG, 3, 2, 0), (R_ALONG, 3, 1, 0), (R_PUT, 1, 0), (R_THIRD, 3, 0), (R_FOURTH, 2, 2), (R_FOURTH, 2, 0),
    (R_PUT, 1, 1), (ROW, 4), (R_ALONG, 2, 1, 0), (R_ALONG, 2, 2, 0), (R_FOURTH, 3, 0), (R_FIFTH, 3, 0),
    (R_FIFTH, 2, 0), (R_PUT, 3, 0), (R_PUT, 2, 0),
)

GATHER_DEEP = (False, False, False, False, True, True)
REDUCE_DEEP = (False, True, False, False)
DOWN_ORDER = tuple(step[1] for step in ORDER if step[0] == D_DOWN)
SHARD_ROWS = (192, 384, 48, 144)


def run_in_order(order, steps):
    for name, *place in order:
        steps[name](*place)


def unit_starts(per_deep, per_flat):
    starts, total = [], 0
    for rows, deep in zip(SHARD_ROWS, REDUCE_DEEP):
        starts.append(total)
        total += rows * (per_deep if deep else per_flat)
    return starts, total


SIDE_STARTS, SIDE_ROWS = unit_starts(5, 8)
CROSS_STARTS, CROSS_ROWS = unit_starts(3, 4)
COLUMN_STARTS, COLUMN_ROWS = unit_starts(12, 6)


def layer_kernel(
    tok, cot, valid, vectors, s_qkv, s_out, s_ff, s_down,
    o_out, o_tok, o_qkv, o_outw, o_ff, o_down, o_rows, w_ff, probs, gu,
    w_bias, w_qkv, w_out, w_down, s_bias, v_rows, v_qkv, v_ctx, v_probs, v_scaled1, v_inv1, v_nl, v_gu, v_ffw,
    v_dn, v_db, v_nlt, v_over, full_a, full_b, both, across, sides, columns, v_sum, v_sums,
    g_sends, g_recvs, locals_, r_sends, r_recvs, row_sends, row_recvs, stages, saves, puts,
):
    y, z, x, c = whereabouts()
    length = tok.shape[0]
    lane = lax.broadcasted_iota(jnp.int32, (1, 128), 1)


    def stage(kind, src, dst, slot):
        return pltpu.make_async_copy(src, dst, stages.at[kind, slot])

    def chunk_of(n):
        return 2 * ((z + 1) % 2 if n < 2 else z % 2) + n % 2

    def ff_rows(n, m):
        return w_ff.at[pl.ds(pl.multiple_of((4 * m + chunk_of(n)) * 1536, 1536), 1536), :]

    def ff_slot(n, m):
        row = (n % 2) * 3072 + m * 1536
        return full_a.at[row : row + 1536, :]

    def ff_stages(n):
        return [stage(m, ff_rows(n, m), ff_slot(n, m), n % 2) for m in (0, 1)]

    def ff_stages_back(n):
        return [stage(m, ff_rows(n, m), v_ffw.at[m], 0) for m in (0, 1)]

    def gu_stages(n):
        return [stage(2 + m, gu.at[m, chunk_of(n)], v_gu.at[n % 2, m], n % 2) for m in (0, 1)]

    def gu_saves(n):
        return [stage(4 + m, v_gu.at[n % 2, m], gu.at[m, chunk_of(n)], n % 2) for m in (0, 1)]

    def side_by_side(ref):
        return jnp.concatenate([ref[:768, :], ref[768:, :]], 1)

    def probs_stage(pair):
        return stage(6, probs.at[pl.ds(2 * pair, 2)], v_probs.at[pair % 2], pair % 2)

    def probs_save(pair):
        return stage(7, v_probs.at[pair % 2], probs.at[pl.ds(2 * pair, 2)], pair % 2)

    def hidden_at(j):
        return pl.ds(pl.multiple_of(j * length, 16), length)


    g = [
        Gather(0, s_bias, w_bias, 16, 16, 0, False, GATHER_DEEP[0], g_sends, g_recvs, locals_),
        Gather(1, s_qkv, w_qkv, 144, 144, 0, False, GATHER_DEEP[1], g_sends, g_recvs, locals_),
        Gather(2, s_out, w_out, 48, 48, 0, False, GATHER_DEEP[2], g_sends, g_recvs, locals_),
        Gather(3, s_ff, w_ff, 384, 768, 0, True, GATHER_DEEP[3], g_sends, g_recvs, locals_),
        Gather(4, s_ff, w_ff, 384, 768, 384, True, GATHER_DEEP[4], g_sends, g_recvs, locals_),
        Gather(5, s_down, w_down, 192, 192, 0, False, GATHER_DEEP[5], g_sends, g_recvs, locals_),
    ]

    def begin_along(t, i):
        for a in g[t].halves():
            if i < 3:
                g[t].to_plane(i, a).start()
            else:

                @pl.when(in_middle(z))
                def _():
                    g[t].to_plane(3, a).start()

    def dist():
        j = lax.broadcasted_iota(jnp.int32, (length, length), 0)
        i = lax.broadcasted_iota(jnp.int32, (length, length), 1)
        v_scaled1[:, :length] = jnp.where(j < valid[0], jnp.abs(i - j).astype(F32), 1e33)

    def rows():
        total = w_bias[0:16, :].astype(F32)
        for k in range(1, 16):
            total = total + w_bias[16 * k : 16 * k + 16, :].astype(F32)
        v_rows[...] = total

    def project(n):
        part = dot(tok[...], w_qkv[768 * n : 768 * n + 768, :], 1, 1)
        if n == 0:
            part = (part + v_rows[0:1, :]).astype(BF).astype(F32) * 0.125
        if n == 2:
            part = part + v_rows[1:2, :]
        v_qkv[:, 768 * n : 768 * n + 768] = part.astype(BF)

    def attend(pair):
        col = 128 * pair
        if pair > 1:
            probs_save(pair - 2).wait()
        q_pair = v_qkv[:, col : col + 128]
        k_pair = v_qkv[:, 768 + col : 768 + col + 128]
        v_pair = v_qkv[:, 1536 + col : 1536 + col + 128]
        results = []
        for hh in range(2):
            mine = (lane < 64) if hh == 0 else (lane >= 64)
            scores = dot(k_pair, jnp.where(mine, q_pair, jnp.zeros((), BF)), 1, 1)
            scores = scores - slope_of(2 * pair + hh) * v_scaled1[:, :length]
            expo = jnp.exp(scores - jnp.max(scores, axis=0, keepdims=True)).astype(BF)
            v_probs[pair % 2, hh] = expo
            results.append(dot(expo, jnp.where(mine, v_pair, jnp.ones((), BF)), 0, 0))
        inverse = 1.0 / pltpu.roll(jnp.where(lane < 64, results[1], results[0]), 64, 1)
        v_over[:, col : col + 128] = inverse.astype(v_over.dtype)
        v_ctx[:, col : col + 128] = (jnp.where(lane < 64, results[0], results[1]) * inverse).astype(BF)
        probs_save(pair).start()

    def first_norm():
        h1 = dot(v_ctx[...], w_out[...], 1, 0) + v_rows[2:3, :] + tok[...].astype(F32)
        scaled1, inverse1 = normalise(h1)
        v_scaled1[...] = scaled1
        v_inv1[...] = jnp.broadcast_to(inverse1, v_inv1.shape)
        normed = scaled1 * v_rows[3:4, :] + v_rows[4:5, :]
        v_dn[...] = normed + v_rows[5:6, :]
        v_nl[...] = normed.astype(BF)
        v_nlt[...] = normed.astype(BF).T

    def load(n):
        for copy in ff_stages(n):
            copy.start()

    load_cot = pltpu.make_async_copy(cot, v_nl, saves.at[2])

    def feed(n):
        s = n % 2
        j = chunk_of(n)
        if n > 1:
            for copy in gu_saves(n - 2):
                copy.wait()
        for copy in ff_stages(n):
            copy.wait()
        gate = dot(v_nl[...], side_by_side(ff_slot(n, 0)), 1, 0) + v_rows[pl.ds(8 + j, 1), :]
        up = dot(v_nl[...], side_by_side(ff_slot(n, 1)), 1, 0) + v_rows[pl.ds(12 + j, 1), :]
        below = cdf(gate)
        density = jnp.exp(-0.5 * gate * gate) * 0.3989422804014327
        active = gate * below
        v_gu[s, 0] = active.astype(BF)
        v_gu[s, 1] = (up * (below + gate * density)).astype(BF)
        hidden = (active * up).astype(BF)
        full_b[hidden_at(2 * j), :] = hidden[:, :384]
        full_b[hidden_at(2 * j + 1), :] = hidden[:, 384:]
        for copy in gu_saves(n):
            copy.start()
        if n == 3:
            load_cot.start()

    def down(i):
        j = plane_at(z, i)
        hidden = jnp.concatenate([full_b[hidden_at(2 * j), :], full_b[hidden_at(2 * j + 1), :]], 1)
        v_dn[...] += dot(hidden, w_down[pl.ds(pl.multiple_of(j * 768, 768), 768), :], 1, 0)

    save_out = pltpu.make_async_copy(v_nl, o_out, saves.at[0])
    save_tok = pltpu.make_async_copy(v_ctx, o_tok, saves.at[1])

    def second_norm():
        for n in (2, 3):
            for copy in gu_saves(n):
                copy.wait()
        for n in (0, 1):
            for copy in gu_stages(n):
                copy.start()
        scaled2, inverse2 = normalise(v_dn[...])
        load_cot.wait()
        grad = v_nl[...].astype(F32)
        d_h2 = norm_back(grad * v_rows[6:7, :], scaled2, inverse2)
        v_dn[...] = d_h2
        v_db[...] = d_h2.astype(BF)
        v_nl[...] = (scaled2 * v_rows[6:7, :] + v_rows[7:8, :]).astype(BF)
        save_out.start()
        v_sum[5:6, :] = column_sum(d_h2.astype(BF).astype(F32))
        v_sum[6:7, :] = column_sum(grad * scaled2)
        v_sum[7:8, :] = column_sum(grad)


    def at_down(plane, x_, c_, h):
        return h * 3072 + index(plane, x_, c_) * 192

    def at_ff(plane, x_, c_, h):
        return (plane // 2) * 3072 + index(0, x_, c_) * 768 + h * 384

    def at_out(plane, x_, c_, h):
        return h * 768 + index(plane, x_, c_) * 48

    def at_qkv(plane, x_, c_, h):
        return 1536 + h * 2304 + index(plane, x_, c_) * 144

    def reduce_of(t, at, full):
        return Reduce(
            t, sum(SHARD_ROWS[:t]), SHARD_ROWS[t], REDUCE_DEEP[t],
            (SIDE_STARTS[t], CROSS_STARTS[t], COLUMN_STARTS[t]),
            at, full, both, across, sides, columns, r_sends, r_recvs,
        )

    r_down = reduce_of(0, at_down, full_a)
    r_ff1 = reduce_of(1, at_ff, full_b)
    r_ff2 = reduce_of(1, at_ff, full_a)
    r_out = reduce_of(2, at_out, full_b)
    r_qkv = reduce_of(3, at_qkv, full_b)

    def reducer(t, i):
        return (r_down, r_ff1 if i % 2 else r_ff2, r_out, r_qkv)[t]

    def d_down(i):
        for s in range(2):
            j = 2 * plane_at(z, i) + s
            part = dot(full_b[hidden_at(j), :], v_db[...], 0, 0)
            row = pl.multiple_of(j * 384, 384)
            full_a[pl.ds(row, 384), :] = part[:, :384].astype(BF)
            full_a[pl.ds(3072 + row, 384), :] = part[:, 384:].astype(BF)

    def chunk(n):
        s = n % 2
        j = chunk_of(n)
        if n == 0:
            for pair in (4, 5):
                probs_save(pair).wait()
            probs_stage(0).start()
            probs_stage(1).start()
        for copy in ff_stages_back(n):
            copy.start()
        for copy in gu_stages(n):
            copy.wait()
        d_hid = dot(v_db[...], w_down[pl.ds(pl.multiple_of(j * 768, 768), 768), :], 1, 1)
        d_up = (d_hid * v_gu[s, 0].astype(F32)).astype(BF)
        d_gate = (d_hid * v_gu[s, 1].astype(F32)).astype(BF)
        full = full_b if n < 2 else full_a
        for m, d in enumerate((d_gate, d_up)):
            part = dot(v_nlt[...], d, 1, 0).astype(BF)
            row = 3072 * m + 1536 * (n % 2)
            full[row : row + 768, :] = part[:, :384]
            full[row + 768 : row + 1536, :] = part[:, 384:]
            v_sum[pl.ds(8 + 4 * m + j, 1), :] = column_sum(d.astype(F32))
        for copy in ff_stages_back(n):
            copy.wait()
        back = dot(d_gate, side_by_side(v_ffw.at[0]), 1, 1) + dot(d_up, side_by_side(v_ffw.at[1]), 1, 1)
        v_dn[...] += back
        if n < 2:
            for copy in gu_stages(n + 2):
                copy.start()

    def first_norm_back():
        d_normed = v_dn[...]
        scaled = v_scaled1[...]
        v_sum[3:4, :] = column_sum(d_normed * scaled)
        v_sum[4:5, :] = column_sum(d_normed)
        d_h1 = norm_back(d_normed * v_rows[3:4, :], scaled, v_inv1[:, 0:1])
        v_dn[...] = d_h1
        v_db[...] = d_h1.astype(BF)
        v_sum[2:3, :] = column_sum(d_h1.astype(BF).astype(F32))

    def d_out():
        part = dot(v_ctx[...], v_db[...], 0, 0)
        full_b[0:768, :] = part[:, :384].astype(BF)
        full_b[768:1536, :] = part[:, 384:].astype(BF)

    v_dctx = v_nl

    def d_context():
        save_out.wait()
        v_dctx[...] = (dot(v_db[...], w_out[...], 1, 1) * v_over[...].astype(F32)).astype(BF)

    def attend_back(pair):
        col = 128 * pair
        probs_stage(pair).wait()
        q_pair = v_qkv[:, col : col + 128]
        k_pair = v_qkv[:, 768 + col : 768 + col + 128]
        v_pair = v_qkv[:, 1536 + col : 1536 + col + 128]
        d_pair = v_dctx[:, col : col + 128]
        product = d_pair.astype(F32) * v_ctx[:, col : col + 128].astype(F32)
        high = product.astype(BF)
        low = (product - high.astype(F32)).astype(BF)
        d_q, d_k, d_v = [], [], []
        for hh in range(2):
            mine = (lane < 64) if hh == 0 else (lane >= 64)
            head = jnp.broadcast_to(mine.astype(BF), (16, 128))
            inner = (dot(head, high, 1, 1) + dot(head, low, 1, 1))[0:1, :]
            d_head = jnp.where(mine, d_pair, jnp.zeros((), BF))
            d_probs = dot(v_pair, d_head, 1, 1)
            expo = v_probs[pair % 2, hh]
            d_scores = (expo.astype(F32) * (d_probs - inner)).astype(BF)
            d_v.append(dot(expo, d_head, 1, 0))
            d_k.append(dot(d_scores, jnp.where(mine, q_pair, jnp.zeros((), BF)), 1, 0))
            d_q.append(dot(k_pair, d_scores, 0, 0))
        upper = lax.broadcasted_iota(jnp.int32, (128, 1), 0) < 64
        v_qkv[:, col : col + 128] = (jnp.where(upper, d_q[0], d_q[1]) * 0.125).astype(BF).T
        v_qkv[:, 768 + col : 768 + col + 128] = (d_k[0] + d_k[1]).astype(BF)
        v_qkv[:, 1536 + col : 1536 + col + 128] = (d_v[0] + d_v[1]).astype(BF)
        if pair < 4:
            probs_stage(pair + 2).start()
        if pair == 5:
            v_sum[0:1, :] = column_sum(v_qkv[:, 0:768].astype(F32))
            v_sum[1:2, :] = column_sum(v_qkv[:, 1536:2304].astype(F32))

    def d_qkv_weight(n):
        part = dot(v_qkv[:, 768 * n : 768 * n + 768], tok[...], 0, 0)
        full_b[1536 + 768 * n : 2304 + 768 * n, :] = part[:, :384].astype(BF)
        full_b[3840 + 768 * n : 4608 + 768 * n, :] = part[:, 384:].astype(BF)

    def d_tokens():
        v_ctx[...] = (dot(v_qkv[...], w_qkv[...], 1, 0) + v_dn[...]).astype(BF)
        save_tok.start()

    def row_copy(n):
        device = (
            (y, index(z, x, 1 - c)), (y, index(z, 1 - x, c)), (1 - y, index(z, x, c)),
            *[(y, index(plane_at(z, i), x, c)) for i in (1, 2, 3)],
        )[n]
        return pltpu.make_async_remote_copy(
            src_ref=v_sum,
            dst_ref=v_sums.at[n],
            send_sem=row_sends.at[n],
            recv_sem=row_recvs.at[n],
            device_id=device,
            device_id_type=MESH,
        )

    def row_step(n):
        if 1 <= n <= 3:
            row_copy(n - 1).wait()
            v_sum[...] = v_sum[...] + v_sums[n - 1]
        if n < 3:
            row_copy(n).start()
        if n == 3:
            for m in (3, 4, 5):
                row_copy(m).start()
        if n == 4:
            for m in (3, 4, 5):
                row_copy(m).wait()
            o_rows[...] = v_sum[...] + v_sums[3] + v_sums[4] + v_sums[5]

    outs = (o_down, o_ff, o_outw, o_qkv)
    placed = []

    s_bias[...] = spread_vectors(vectors[...], index(z, x, c)).astype(BF)
    greet()
    run_in_order(
        ORDER,
        {
            OWN: lambda t: g[t].begin_plane(),
            ALONG: begin_along,
            SECOND: lambda t, i: g[t].second(i),
            THIRD: lambda t, i: g[t].third(i),
            FOURTH: lambda t, i: g[t].fourth(i),
            ARRIVED: lambda t, i: g[t].arrived(i),
            DIST: dist,
            ROWS: rows,
            QKV: project,
            ATTEND: attend,
            NORM: first_norm,
            LOAD: load,
            FEED: feed,
            DOWN: down,
            MIDDLE: second_norm,
            D_DOWN: d_down,
            CHUNK: chunk,
            D_NORM: first_norm_back,
            D_OUT: d_out,
            D_CTX: d_context,
            D_ATTEND: attend_back,
            D_QKV: d_qkv_weight,
            D_TOK: d_tokens,
            ROW: row_step,
            R_FIRST: lambda t, i: reducer(t, i).first(i),
            R_SECOND: lambda t, i: reducer(t, i).second(i),
            R_THIRD: lambda t, i: reducer(t, i).third(i),
            R_FOURTH: lambda t, i: reducer(t, i).fourth(i),
            R_ALONG: lambda t, i, a: reducer(t, i).along(i, a),
            R_FIFTH: lambda t, a: reducer(t, 0).fifth(a),
            R_PUT: lambda t, a: placed.extend(reducer(t, 0).put(a, outs[t], puts)),
        },
    )
    save_tok.wait()
    for copy in placed:
        copy.wait()
    for t in range(6):
        g[t].finish()
    for t in range(4):
        reducer(t, 0).finish()


def finish_kernel(tok, qkv, out, ff, down, rows, fwd, *outs):
    o_fwd, o_tok, o_qkv, o_qv, o_out, o_outb, o_g1, o_s1, o_ff, o_ffb, o_down, o_downb, o_g2, o_s2 = outs
    k = lax.axis_index("fsdp")
    o_fwd[...] = fwd[...]
    o_tok[...] = tok[...]
    for h in (0, 1):
        o_qkv[:, 384 * h : 384 * h + 384] = qkv[h].astype(F32)
        o_out[:, 384 * h : 384 * h + 384] = out[h].astype(F32)
        o_down[:, 384 * h : 384 * h + 384] = down[h].astype(F32)
        o_ff[384 * h : 384 * h + 384, :] = ff[h].astype(F32)
    by_vector = (o_qv, o_outb, o_g1, o_s1, o_ffb, o_downb, o_g2, o_s2)
    for ref, (_, n, row) in zip(by_vector, VECTORS):
        per = 768 // n
        line = rows[pl.ds(row + k // per, 1), :]
        moved = pltpu.roll(jnp.broadcast_to(line, (8, 768)), ((768 - (k % per) * n) % 768), 1)
        ref[...] = moved[0:1, 0:n]


def fused_on_device(
    tokens,
    qkv_weight,
    qv_bias,
    out_weight,
    out_bias,
    norm1_gain,
    norm1_shift,
    ff_weight,
    ff_bias,
    down_weight,
    down_bias,
    norm2_gain,
    norm2_shift,
    pair_length,
    cotangent,
):
    length, width = tokens.shape
    vectors = jnp.concatenate(
        [qv_bias, out_bias, norm1_gain, norm1_shift, ff_bias, down_bias, norm2_gain, norm2_shift]
    )
    vectors = vectors.astype(F32).reshape(1, width)
    in_vmem = pl.BlockSpec(memory_space=pltpu.VMEM)
    in_smem = pl.BlockSpec(memory_space=pltpu.SMEM)
    anywhere = pl.BlockSpec(memory_space=pl.ANY)
    struct = jax.ShapeDtypeStruct
    vmem = pltpu.VMEM
    dma = pltpu.SemaphoreType.DMA
    output, d_tokens, d_qkv, d_out, d_ff, d_down, d_rows = pl.pallas_call(
        layer_kernel,
        name="layer",
        out_shape=[
            struct((length, width), BF),
            struct((length, width), BF),
            struct((2, 144, 384), BF),
            struct((2, 48, 384), BF),
            struct((2, 384, 384), BF),
            struct((2, 192, 384), BF),
            struct((16, width), F32),
            struct((12288, 384), BF),
            struct((HEADS, length, length), BF),
            struct((2, 4, length, 768), BF),
        ],
        in_specs=[in_vmem, anywhere, in_smem, in_vmem] + [anywhere] * 4,
        out_specs=[anywhere] * 6 + [in_vmem] + [anywhere] * 3,
        scratch_shapes=[
            vmem((256, width), BF),
            vmem((2304, width), BF),
            vmem((width, width), BF),
            vmem((3072, width), BF),
            vmem((16, width), BF),
            vmem((16, width), F32),
            vmem((length, 2304), BF),
            vmem((length, width), BF),
            vmem((2, 2, length, length), BF),
            vmem((length, width), F32),
            vmem((length, 128), F32),
            vmem((length, width), BF),
            vmem((2, 2, length, 768), BF),
            vmem((2, 1536, 384), BF),
            vmem((length, width), F32),
            vmem((length, width), BF),
            vmem((width, length), BF),
            vmem((length, width), BF),
            vmem((6144, 384), BF),
            vmem((6144, 384), BF),
            vmem((768 * 16, 384), BF),
            vmem((CROSS_ROWS, 384), BF),
            vmem((SIDE_ROWS, 384), BF),
            vmem((COLUMN_ROWS, 384), BF),
            vmem((16, width), F32),
            vmem((6, 16, width), F32),
            dma((6, Gather.SLOTS)),
            dma((6, Gather.SLOTS)),
            dma((6,)),
            dma((4, Reduce.SLOTS)),
            dma((4, Reduce.SLOTS)),
            dma((6,)),
            dma((6,)),
            dma((8, 2)),
            dma((3,)),
            dma((4, 2)),
        ],
        compiler_params=pltpu.CompilerParams(
            collective_id=0, has_side_effects=True, vmem_limit_bytes=63 * 2**20
        ),
    )(tokens, cotangent, pair_length, vectors, qkv_weight.T, out_weight, ff_weight, down_weight)[:7]

    def vector(n):
        return struct((1, n), F32)

    full = [struct(s, F32) for s in ((144, width), (48, width), (768, 384), (192, width))]
    results = pl.pallas_call(
        finish_kernel,
        name="finish",
        out_shape=[
            struct((length, width), BF), struct((length, width), BF), full[0], vector(96), full[1], vector(48),
            vector(48), vector(48), full[2], vector(384), full[3], vector(48), vector(48), vector(48),
        ],
        in_specs=[in_vmem] * 7,
        out_specs=[in_vmem] * 14,
    )(d_tokens, d_qkv, d_out, d_ff, d_down, d_rows, output)
    results = [r[0] if r.shape[0] == 1 else r for r in results]
    results[2] = results[2].T
    return tuple(results)


def solution(mesh):
    in_specs = (
        P(("rep", "fsdp"), None),
        P(None, "fsdp"),
        P("fsdp"),
        P("fsdp", None),
        P("fsdp"),
        P("fsdp"),
        P("fsdp"),
        P(None, "fsdp"),
        P("fsdp"),
        P("fsdp", None),
        P("fsdp"),
        P("fsdp"),
        P("fsdp"),
        P(("rep", "fsdp")),
        P(("rep", "fsdp"), None),
    )
    out_specs = (
        P(("rep", "fsdp"), None),
        P(("rep", "fsdp"), None),
        P(None, "fsdp"),
        P("fsdp"),
        P("fsdp", None),
        P("fsdp"),
        P("fsdp"),
        P("fsdp"),
        P(None, "fsdp"),
        P("fsdp"),
        P("fsdp", None),
        P("fsdp"),
        P("fsdp"),
        P("fsdp"),
    )
    planes = mesh.shape["rep"] == 2 and mesh.shape["fsdp"] == 16
    return jax.shard_map(
        fused_on_device if planes else plain_on_device, mesh=mesh, in_specs=in_specs, out_specs=out_specs, check_vma=False
    )
```

```python
import jax
import jax.numpy as jnp
from jax import lax
from jax.experimental import pallas as pl
from jax.experimental.pallas import tpu as pltpu
from jax.sharding import PartitionSpec as P

HEADS = 12
MESH = pl.DeviceIdType.MESH
BF = jnp.bfloat16
F32 = jnp.float32


def layer_norm(h, gain, shift):
    mean = jnp.mean(h, -1, keepdims=True)
    centered = h - mean
    spread = jnp.mean(centered * centered, -1, keepdims=True)
    return centered * lax.rsqrt(spread + 1e-05) * gain + shift


def inner_rows(left, right):
    return lax.dot_general(
        left, right, (((0,), (0,)), ((), ())), preferred_element_type=jnp.float32
    )


def times_transposed(left, right):
    return lax.dot_general(
        left, right, (((1,), (1,)), ((), ())), preferred_element_type=jnp.float32
    )


def score_block(query, keys, slope, valid):
    length = query.shape[0]
    place = jnp.arange(length, dtype=jnp.float32)
    scores = times_transposed(query, keys) * 0.125 - slope * jnp.abs(
        place[:, None] - place[None, :]
    )
    allowed = jnp.arange(length, dtype=jnp.int32) < valid
    return jnp.where(allowed[None, :], scores, -1e30)


def head_slopes():
    return 2.0 ** (-8.0 * jnp.arange(1, HEADS + 1, dtype=jnp.float32) / HEADS)


def forward(tokens, attention, feedforward, valid):
    qkv_weight, qv_bias, out_weight, out_bias, gain1, shift1 = attention
    ff_weight, ff_bias, down_weight, down_bias, gain2, shift2 = feedforward
    length, width = tokens.shape
    bias_f = qv_bias.astype(jnp.float32)
    full_bias = jnp.concatenate([bias_f[:width], jnp.zeros((width,), jnp.float32), bias_f[width:]])
    qkv = (jnp.dot(tokens, qkv_weight, preferred_element_type=jnp.float32) + full_bias).astype(
        jnp.bfloat16
    )
    per_head = qkv.reshape(length, 3, HEADS, width // HEADS).transpose(1, 2, 0, 3)

    def attend(item):
        query, keys, values, slope = item
        scores = score_block(query, keys, slope, valid)
        top = jnp.max(scores, -1, keepdims=True)
        expo = jnp.exp(scores - top)
        total = jnp.sum(expo, -1, keepdims=True)
        probs = (expo / total).astype(jnp.bfloat16)
        return (
            jnp.dot(probs, values, preferred_element_type=jnp.float32),
            top[:, 0] + jnp.log(total[:, 0]),
        )

    context, log_total = lax.map(attend, (per_head[0], per_head[1], per_head[2], head_slopes()))
    context = context.transpose(1, 0, 2).reshape(length, width).astype(jnp.bfloat16)
    attended = jnp.dot(context, out_weight, preferred_element_type=jnp.float32) + out_bias.astype(
        jnp.float32
    )
    residual1 = tokens.astype(jnp.float32) + attended
    normed = layer_norm(residual1, gain1.astype(jnp.float32), shift1.astype(jnp.float32))
    normed_low = normed.astype(jnp.bfloat16)
    gate_up = jnp.dot(normed_low, ff_weight, preferred_element_type=jnp.float32) + ff_bias.astype(
        jnp.float32
    )
    half = gate_up.shape[1] // 2
    hidden = (jax.nn.gelu(gate_up[:, :half], approximate=False) * gate_up[:, half:]).astype(
        jnp.bfloat16
    )
    residual2 = (
        normed
        + jnp.dot(hidden, down_weight, preferred_element_type=jnp.float32)
        + down_bias.astype(jnp.float32)
    )
    return (per_head, log_total, context, residual1, normed_low, gate_up, hidden, residual2)


def gelu_product(gate, up):
    return jax.nn.gelu(gate, approximate=False) * up


def plain_on_device(
    tokens,
    qkv_weight,
    qv_bias,
    out_weight,
    out_bias,
    norm1_gain,
    norm1_shift,
    ff_weight,
    ff_bias,
    down_weight,
    down_bias,
    norm2_gain,
    norm2_shift,
    pair_length,
    cotangent,
):
    valid = pair_length[0]
    attention = (
        lax.all_gather(qkv_weight, "fsdp", axis=1, tiled=True),
        lax.all_gather(qv_bias, "fsdp", axis=0, tiled=True),
        lax.all_gather(out_weight, "fsdp", axis=0, tiled=True),
        lax.all_gather(out_bias, "fsdp", axis=0, tiled=True),
        lax.all_gather(norm1_gain, "fsdp", axis=0, tiled=True),
        lax.all_gather(norm1_shift, "fsdp", axis=0, tiled=True),
    )
    feedforward = (
        lax.all_gather(ff_weight, "fsdp", axis=1, tiled=True),
        lax.all_gather(ff_bias, "fsdp", axis=0, tiled=True),
        lax.all_gather(down_weight, "fsdp", axis=0, tiled=True),
        lax.all_gather(down_bias, "fsdp", axis=0, tiled=True),
        lax.all_gather(norm2_gain, "fsdp", axis=0, tiled=True),
        lax.all_gather(norm2_shift, "fsdp", axis=0, tiled=True),
    )
    stored = forward(tokens, attention, feedforward, valid)
    gain2 = feedforward[4].astype(jnp.float32)
    shift2 = feedforward[5].astype(jnp.float32)
    output = layer_norm(stored[7], gain2, shift2).astype(jnp.bfloat16)
    per_head, log_total, context, residual1, normed_low, gate_up, hidden, residual2 = stored
    full_qkv, bias_unused, full_out, out_unused, gain1, shift1 = attention
    full_ff, ff_unused, full_down, down_unused, gain_unused, shift_unused = feedforward
    length, width = tokens.shape
    unused_out, back_second = jax.vjp(layer_norm, residual2, gain2, shift2)
    d_res2, d_gain2, d_shift2 = back_second(cotangent.astype(jnp.float32))
    d_branch = d_res2.astype(jnp.bfloat16)
    d_down = inner_rows(hidden, d_branch)
    d_down_bias = jnp.sum(d_branch.astype(jnp.float32), 0)
    d_hidden = times_transposed(d_branch, full_down).astype(jnp.bfloat16)
    half = gate_up.shape[1] // 2
    unused_prod, back_gelu = jax.vjp(gelu_product, gate_up[:, :half], gate_up[:, half:])
    d_gate, d_up = back_gelu(d_hidden.astype(jnp.float32))
    d_gate_up = jnp.concatenate([d_gate, d_up], 1).astype(jnp.bfloat16)
    d_ff = inner_rows(normed_low, d_gate_up)
    d_ff_bias = jnp.sum(d_gate_up.astype(jnp.float32), 0)
    d_normed = times_transposed(d_gate_up, full_ff) + d_res2
    unused_norm, back_first = jax.vjp(
        layer_norm, residual1, gain1.astype(jnp.float32), shift1.astype(jnp.float32)
    )
    d_res1, d_gain1, d_shift1 = back_first(d_normed)
    ff_terms = (d_ff, d_ff_bias, d_down, d_down_bias, d_gain2, d_shift2)
    ff_grads = (
        lax.psum_scatter(ff_terms[0], "fsdp", scatter_dimension=1, tiled=True),
        lax.psum_scatter(ff_terms[1], "fsdp", scatter_dimension=0, tiled=True),
        lax.psum_scatter(ff_terms[2], "fsdp", scatter_dimension=0, tiled=True),
        lax.psum_scatter(ff_terms[3], "fsdp", scatter_dimension=0, tiled=True),
        lax.psum_scatter(ff_terms[4], "fsdp", scatter_dimension=0, tiled=True),
        lax.psum_scatter(ff_terms[5], "fsdp", scatter_dimension=0, tiled=True),
    )
    ff_grads = (
        lax.psum(ff_grads[0].astype(jnp.bfloat16), "rep").astype(jnp.float32),
        lax.psum(ff_grads[1].astype(jnp.bfloat16), "rep").astype(jnp.float32),
        lax.psum(ff_grads[2].astype(jnp.bfloat16), "rep").astype(jnp.float32),
        lax.psum(ff_grads[3].astype(jnp.bfloat16), "rep").astype(jnp.float32),
        lax.psum(ff_grads[4].astype(jnp.bfloat16), "rep").astype(jnp.float32),
        lax.psum(ff_grads[5].astype(jnp.bfloat16), "rep").astype(jnp.float32),
    )
    d_attended = d_res1.astype(jnp.bfloat16)
    d_out = inner_rows(context, d_attended)
    d_out_bias = jnp.sum(d_attended.astype(jnp.float32), 0)
    d_context = times_transposed(d_attended, full_out).astype(jnp.bfloat16)
    d_context = d_context.reshape(length, HEADS, width // HEADS).transpose(1, 0, 2)

    def attend_back(item):
        query, keys, values, grad_context, total_log, slope = item
        scores = score_block(query, keys, slope, valid)
        probs = jnp.exp(scores - total_log[:, None])
        probs_low = probs.astype(jnp.bfloat16)
        d_probs = times_transposed(grad_context, values)
        d_scores = (probs * (d_probs - jnp.sum(probs * d_probs, -1, keepdims=True))).astype(
            jnp.bfloat16
        )
        d_query = jnp.dot(d_scores, keys, preferred_element_type=jnp.float32) * 0.125
        d_keys = inner_rows(d_scores, query) * 0.125
        d_values = inner_rows(probs_low, grad_context)
        return (d_query, d_keys, d_values)

    d_query, d_keys, d_values = lax.map(
        attend_back, (per_head[0], per_head[1], per_head[2], d_context, log_total, head_slopes())
    )
    d_qkv = (
        jnp.stack([d_query, d_keys, d_values])
        .transpose(2, 0, 1, 3)
        .reshape(length, 3 * width)
        .astype(jnp.bfloat16)
    )
    d_qkv_w = inner_rows(tokens, d_qkv)
    column_sums = jnp.sum(d_qkv.astype(jnp.float32), 0)
    d_qv = jnp.concatenate([column_sums[:width], column_sums[2 * width :]])
    d_tokens = (times_transposed(d_qkv, full_qkv) + d_res1).astype(jnp.bfloat16)
    at_terms = (d_qkv_w, d_qv, d_out, d_out_bias, d_gain1, d_shift1)
    at_grads = (
        lax.psum_scatter(at_terms[0], "fsdp", scatter_dimension=1, tiled=True),
        lax.psum_scatter(at_terms[1], "fsdp", scatter_dimension=0, tiled=True),
        lax.psum_scatter(at_terms[2], "fsdp", scatter_dimension=0, tiled=True),
        lax.psum_scatter(at_terms[3], "fsdp", scatter_dimension=0, tiled=True),
        lax.psum_scatter(at_terms[4], "fsdp", scatter_dimension=0, tiled=True),
        lax.psum_scatter(at_terms[5], "fsdp", scatter_dimension=0, tiled=True),
    )
    at_grads = (
        lax.psum(at_grads[0].astype(jnp.bfloat16), "rep").astype(jnp.float32),
        lax.psum(at_grads[1].astype(jnp.bfloat16), "rep").astype(jnp.float32),
        lax.psum(at_grads[2].astype(jnp.bfloat16), "rep").astype(jnp.float32),
        lax.psum(at_grads[3].astype(jnp.bfloat16), "rep").astype(jnp.float32),
        lax.psum(at_grads[4].astype(jnp.bfloat16), "rep").astype(jnp.float32),
        lax.psum(at_grads[5].astype(jnp.bfloat16), "rep").astype(jnp.float32),
    )
    return (
        output,
        d_tokens,
        at_grads[0],
        at_grads[1],
        at_grads[2],
        at_grads[3],
        at_grads[4],
        at_grads[5],
        ff_grads[0],
        ff_grads[1],
        ff_grads[2],
        ff_grads[3],
        ff_grads[4],
        ff_grads[5],
    )


def dot(left, right, left_dim, right_dim):
    return lax.dot_general(
        left, right, (((left_dim,), (right_dim,)), ((), ())), preferred_element_type=F32
    )


def whereabouts():
    y = lax.axis_index("rep")
    k = lax.axis_index("fsdp")
    return y, k // 4, (k // 2) % 2, k % 2


def index(z, x, c):
    return z * 4 + x * 2 + c


def plane_at(z, i):
    return (z, z + 1 - 2 * (z % 2), (z + 2) % 4, 3 - z)[i]


def in_middle(z):
    return (z == 1) | (z == 2)


def greet():
    y, z, x, c = whereabouts()
    friends = [(y, index(z, x, 1 - c)), (y, index(z, 1 - x, c)), (1 - y, index(z, x, c))]
    friends += [(y, index(plane_at(z, i), x, c)) for i in (1, 2, 3)]
    barrier = pltpu.get_barrier_semaphore()
    for friend in friends:
        pl.semaphore_signal(barrier, inc=1, device_id=friend, device_id_type=MESH)
    pl.semaphore_wait(barrier, len(friends))


class Gather:
    Z, X, Y, D, C = 0, 8, 12, 16, 20
    SLOTS = 28

    def __init__(self, t, src, dst, rows, pitch, start, by_row, deep, sends, recvs, locals_):
        self.t, self.src, self.dst, self.rows, self.by_row, self.deep = t, src, dst, rows, by_row, deep
        self.pitch, self.start = pitch, start
        self.sends, self.recvs, self.locals_ = sends, recvs, locals_
        self.y, self.z, self.x, self.c = whereabouts()

    def plane(self, i):
        return plane_at(self.z, i)

    def half(self, ref, base, h):
        if self.by_row:
            n = self.rows // 2
            return ref.at[pl.ds(pl.multiple_of(base + h * n, 16), n), :]
        n = ref.shape[1] // 2
        return ref.at[pl.ds(base, self.rows), pl.ds(pl.multiple_of(h * n, 128), n)]

    def part(self, k, h):
        return self.half(self.dst, pl.multiple_of(k * self.pitch + self.start, 16), h)

    def shard(self, k):
        return self.dst.at[pl.ds(pl.multiple_of(k * self.pitch + self.start, 16), self.rows), :]

    def whole(self):
        return self.src.at[pl.ds(self.start, self.rows), :]

    def copy(self, slot, src, dst, device, arrival=None):
        return pltpu.make_async_remote_copy(
            src_ref=src,
            dst_ref=dst,
            send_sem=self.sends.at[self.t, slot],
            recv_sem=self.recvs.at[self.t, slot if arrival is None else arrival],
            device_id=device,
            device_id_type=MESH,
        )

    def halves(self):
        return (0, 1) if self.deep else (0,)

    def to_plane(self, i, a):
        h = 1 - self.y if a else self.y
        k = index(self.z, self.x, self.c)
        device = (self.y, index(self.plane(i), self.x, self.c))
        return self.copy(self.Z + 2 * i + a, self.half(self.src, self.start, h), self.part(k, h), device)

    def relay(self, a):
        h = 1 - self.y if a else self.y
        k = index(self.plane(2), self.x, self.c)
        device = (self.y, index(self.plane(1), self.x, self.c))
        return self.copy(self.Z + a, self.part(k, h), self.part(k, h), device, self.Z + 6 + a)

    def to_x(self, i):
        k = index(self.plane(i), self.x, self.c)
        src = self.half(self.src, self.start, self.y) if i == 0 else self.part(k, self.y)
        return self.copy(
            self.X + i, src, self.part(k, self.y), (self.y, index(self.z, 1 - self.x, self.c))
        )

    def to_y(self, i):
        k = index(self.plane(i), self.x, self.c)
        part = self.part(k, self.y)
        return self.copy(self.Y + i, part, part, (1 - self.y, index(self.z, self.x, self.c)))

    def onward(self, i):
        c = 0 if i == 0 or self.deep else self.c
        k = index(self.plane(i), (1 - self.x) * (1 - c) + self.x * c, self.c)
        part = self.part(k, self.y * (1 - c) + (1 - self.y) * c)
        x = self.x * (1 - c) + (1 - self.x) * c
        y = self.y * c + (1 - self.y) * (1 - c)
        return self.copy(self.D + i, part, part, (y, index(self.z, x, self.c)))

    def to_core(self, i, home):
        k = index(self.plane(i), self.x if home else 1 - self.x, self.c)
        src = self.whole() if home and i == 0 else self.shard(k)
        device = (self.y, index(self.z, self.x, 1 - self.c))
        return self.copy(self.C + i + (0 if home else 4), src, self.shard(k), device)

    def own(self):
        return pltpu.make_async_copy(
            self.whole(), self.shard(index(self.z, self.x, self.c)), self.locals_.at[self.t]
        )

    def begin(self):
        for a in self.halves():
            for i in (2, 1):
                self.to_plane(i, a).start()

            @pl.when(in_middle(self.z))
            def _():
                self.to_plane(3, a).start()

    def begin_plane(self):
        self.to_x(0).start()
        self.to_core(0, True).start()
        self.own().start()

    def second(self, i):
        if i == 0:
            return
        for a in self.halves():
            self.to_plane(i, a).wait_recv()
            if i == 2:

                @pl.when(in_middle(self.z))
                def _():
                    self.relay(a).start()

            if a == 0:
                self.to_x(i).start()
                if not self.deep:
                    self.to_y(i).start()
        if self.deep:
            self.to_core(i, True).start()

    def third(self, i):
        if i and not self.deep:
            self.to_y(i).wait_recv()
            self.to_core(i, True).start()
        self.to_x(i).wait_recv()
        self.onward(i).start()

    def fourth(self, i):
        self.onward(i).wait_recv()
        self.to_core(i, False).start()

    def arrived(self, i):
        self.to_core(i, True).wait_recv()
        self.to_core(i, False).wait_recv()
        if i == 0:
            self.own().wait()

    def finish(self):
        for a in self.halves():
            for i in (1, 2):
                self.to_plane(i, a).wait_send()

            @pl.when(in_middle(self.z))
            def _():
                self.to_plane(3, a).wait_send()
                self.relay(a).wait_send()

        for i in range(4):
            self.to_x(i).wait_send()
            if i and not self.deep:
                self.to_y(i).wait_send()
            self.onward(i).wait_send()
            self.to_core(i, True).wait_send()
            self.to_core(i, False).wait_send()


class Reduce:
    CORE, DIAGONAL, EARLY, LATE, PLANE, ARRIVE, LAST, SLOTS = 0, 4, 5, 6, 7, 36, 38, 40

    def __init__(self, t, base, rows, deep, starts, at, full, both, across, sides, columns, sends, recvs):
        self.t, self.base, self.rows, self.deep, self.at = t, base, rows, deep, at
        self.full, self.both, self.across, self.sides, self.columns = full, both, across, sides, columns
        self.starts, self.sends, self.recvs = starts, sends, recvs
        self.y, self.z, self.x, self.c = whereabouts()

    def copy(self, slot, src, dst, device, arrival=None):
        return pltpu.make_async_remote_copy(
            src_ref=src,
            dst_ref=dst,
            send_sem=self.sends.at[self.t, slot],
            recv_sem=self.recvs.at[self.t, slot if arrival is None else arrival],
            device_id=device,
            device_id_type=MESH,
        )

    def rows_of(self, ref, row):
        return ref.at[pl.ds(pl.multiple_of(row, 16), self.rows), :]

    def unit(self, i, away_x, c, h):
        x = 1 - self.x if away_x else self.x
        return self.rows_of(self.full, self.at(plane_at(self.z, i), x, c, h))

    def mine(self, i, away_x, away_h):
        n = i * 4 + away_x * 2 + away_h
        return self.rows_of(self.both, self.base * 16 + n * self.rows)

    def side(self, i, s):
        n = (i + s if i == 0 else i + 1) if self.deep else i * 2 + s
        return self.rows_of(self.sides, self.starts[0] + n * self.rows)

    def cross(self, i):
        return self.rows_of(self.across, self.starts[1] + (i - 1 if self.deep else i) * self.rows)

    def column(self, n, a):
        return self.rows_of(self.columns, self.starts[2] + (2 * n + a if self.deep else n) * self.rows)

    def halves(self):
        return (0, 1) if self.deep else (0,)

    def way(self, i):
        return 0 if self.deep else (1 if i == 0 else self.c)

    def neighbour(self, over_x):
        return (
            self.y * over_x + (1 - self.y) * (1 - over_x),
            index(self.z, (1 - self.x) * over_x + self.x * (1 - over_x), self.c),
        )

    def to_core(self, i, n):
        device = (self.y, index(self.z, self.x, 1 - self.c))
        h = 1 - self.y if n % 2 else self.y
        src = self.unit(i, n // 2, 1 - self.c, h)
        return self.copy(i * 9 + n, src, self.mine(i, n // 2, n % 2), device)

    def diagonal(self, i):
        device = self.neighbour(self.way(i))
        return self.copy(i * 9 + self.DIAGONAL, self.mine(i, 1, 1), self.cross(i), device)

    def early(self, i):
        w = self.way(i)
        return self.copy(i * 9 + self.EARLY, self.mine(i, w, 1 - w), self.side(i, 0), self.neighbour(w))

    def late(self, i):
        w = self.way(i)
        return self.copy(i * 9 + self.LATE, self.mine(i, 1 - w, w), self.side(i, 1), self.neighbour(1 - w))

    def over_x(self, i, a):
        slot = i * 9 + (self.LATE if a else self.EARLY)
        return self.copy(slot, self.mine(i, 1, a), self.side(i, a), self.neighbour(1))

    def to_plane(self, i, a):
        slot = i * 9 + self.PLANE + a
        src = self.mine(i, 0, a)
        if i < 3:
            device = (self.y, index(plane_at(self.z, i), self.x, self.c))
            return self.copy(slot, src, self.column(i - 1, a), device)
        near, far = plane_at(self.z, 1), plane_at(self.z, 3)
        middle = (self.z % 3 + 1) // 2
        plane = far * middle + near * (1 - middle)
        arrival = slot * middle + (self.ARRIVE + a) * (1 - middle)
        return self.copy(
            slot, src, self.column(3 - middle, a), (self.y, index(plane, self.x, self.c)), arrival
        )

    def handed(self, a):
        slot = 3 * 9 + self.PLANE + a
        device = (self.y, index(plane_at(self.z, 1), self.x, self.c))
        return self.copy(slot, self.mine(3, 0, a), self.column(3, a), device, self.ARRIVE + a)

    def mirrored(self, a):
        slot = 3 * 9 + self.PLANE + a
        device = (self.y, index(plane_at(self.z, 3), self.x, self.c))
        return self.copy(slot, self.mine(3, 0, a), self.column(2, a), device)

    def last(self, a):
        device = (1 - self.y, index(self.z, self.x, self.c))
        b = 1 - a if self.deep else a
        return self.copy(self.LAST + a, self.column(4, a), self.column(5, b), device, self.LAST + b)

    def first(self, i):
        for n in (3, 2, 1, 0):
            self.to_core(i, n).start()

    def second(self, i):
        for n in (3, 2, 1, 0):
            self.to_core(i, n).wait()
            h = 1 - self.y if n % 2 else self.y
            part = self.mine(i, n // 2, n % 2)
            part[...] = part[...] + self.unit(i, n // 2, self.c, h)[...]
            if self.deep and i == 0:
                if n > 1:
                    self.over_x(i, n - 2).start()
            elif n == 3:
                self.diagonal(i).start()
        if not self.deep:
            self.early(i).start()

    def third(self, i):
        if self.deep and i == 0:
            return
        w = self.way(i)
        self.diagonal(i).wait_recv()
        part = self.mine(i, 1 - w, w)
        part[...] = part[...] + self.cross(i)[...]
        if self.deep:
            self.over_x(i, 0).start()
        else:
            self.late(i).start()

    def fourth(self, i):
        if self.deep:
            for a in (0, 1) if i == 0 else (0,):
                self.over_x(i, a).wait_recv()
                part = self.mine(i, 0, a)
                part[...] = part[...] + self.side(i, a)[...]
            return
        self.early(i).wait_recv()
        self.late(i).wait_recv()
        part = self.mine(i, 0, 0)
        total = part[...].astype(F32) + self.side(i, 0)[...].astype(F32)
        part[...] = (total + self.side(i, 1)[...].astype(F32)).astype(BF)

    def along(self, i, a):
        if i == 2:

            @pl.when(in_middle(self.z))
            def _():
                self.handed(a).wait_recv()
                part = self.mine(2, 0, a)
                part[...] = part[...] + self.column(3, a)[...]

        self.to_plane(i, a).start()

    def fifth(self, a):
        for i in (1, 2):
            self.to_plane(i, a).wait_recv()
        total = self.mine(0, 0, a)[...].astype(F32)
        total = total + self.column(0, a)[...].astype(F32) + self.column(1, a)[...].astype(F32)

        @pl.when(in_middle(self.z))
        def _():
            self.mirrored(a).wait_recv()
            self.column(4, a)[...] = (total + self.column(2, a)[...].astype(F32)).astype(BF)

        @pl.when(jnp.logical_not(in_middle(self.z)))
        def _():
            self.column(4, a)[...] = total.astype(BF)

        self.last(a).start()

    def put(self, a, out, semaphore):
        self.last(a).wait_send()
        self.last(1 - a if self.deep else a).wait_recv()
        here, there = self.y, 1 - self.y
        own, other = self.column(4, a), self.column(5, a)
        if self.deep:
            own[...] = (own[...].astype(F32) + other[...].astype(F32)).astype(BF)
            pairs = [((there if a else here), own)]
        else:
            pairs = [(here, own), (there, other)]
        copies = [pltpu.make_async_copy(v, out.at[h], semaphore.at[self.t, a + n]) for n, (h, v) in enumerate(pairs)]
        for copy in copies:
            copy.start()
        return copies

    def finish(self):
        for i in range(4):
            if self.deep:
                if i:
                    self.diagonal(i).wait_send()
                self.over_x(i, 0).wait_send()
                if i == 0:
                    self.over_x(i, 1).wait_send()
            else:
                self.diagonal(i).wait_send()
                self.early(i).wait_send()
                self.late(i).wait_send()
            if i:
                for a in self.halves():
                    self.to_plane(i, a).wait_send()


def slope_of(head):
    return jnp.exp2(jnp.full((1, 1), head + 1, jnp.int32).astype(F32) * (-8.0 / HEADS))


def normalise(h):
    centered = h - jnp.mean(h, -1, keepdims=True)
    inverse = lax.rsqrt(jnp.mean(centered * centered, -1, keepdims=True) + 1e-05)
    return centered * inverse, inverse


def norm_back(d_scaled, scaled, inverse):
    mean1 = jnp.mean(d_scaled, -1, keepdims=True)
    mean2 = jnp.mean(d_scaled * scaled, -1, keepdims=True)
    return inverse * (d_scaled - mean1 - scaled * mean2)


def column_sum(v):
    return jnp.sum(v, axis=0, keepdims=True)


def cdf(gate):
    return 0.5 * (1.0 + lax.erf(gate * 0.7071067811865476))


VECTORS = (
    (0, 96, 0), (96, 48, 2), (144, 48, 3), (192, 48, 4), (240, 384, 8), (624, 48, 5), (672, 48, 6), (720, 48, 7),
)


def spread_vectors(shards, k):
    lane = lax.broadcasted_iota(jnp.int32, (16, 768), 1)
    line = lax.broadcasted_iota(jnp.int32, (16, 768), 0)
    wide = jnp.broadcast_to(shards, (16, 768))
    rows = jnp.zeros((16, 768), F32)
    for start, n, row in VECTORS:
        per = 768 // n
        shift = ((k % per) * n - start + 768) % 768
        here = (lane // n == k % per) & (line == row + k // per)
        rows = jnp.where(here, pltpu.roll(wide, shift, 1), rows)
    return rows


(
    OWN, ALONG, SECOND, THIRD, FOURTH, ARRIVED, DIST, ROWS, QKV, ATTEND, NORM, LOAD, FEED, DOWN, MIDDLE,
    D_DOWN, CHUNK, D_NORM, D_OUT, D_CTX, D_ATTEND, D_QKV, D_TOK, ROW, R_FIRST, R_SECOND, R_THIRD, R_FOURTH, R_ALONG, R_FIFTH, R_PUT,
) = range(31)

ORDER = (
    (OWN, 0), (ALONG, 1, 2), (ALONG, 2, 1), (OWN, 1), (ALONG, 0, 2), (ALONG, 2, 2), (ALONG, 2, 3), (OWN, 4),
    (ALONG, 3, 1), (THIRD, 0, 0), (OWN, 2), (ALONG, 0, 1), (ALONG, 1, 1), (THIRD, 1, 0), (ALONG, 0, 3), (OWN, 5),
    (SECOND, 2, 1), (THIRD, 4, 0), (ALONG, 1, 3), (SECOND, 0, 2), (SECOND, 1, 2), (FOURTH, 0, 0), (SECOND, 0, 1),
    (ALONG, 3, 2), (SECOND, 1, 1), (OWN, 3), (ARRIVED, 0, 0), (SECOND, 1, 3), (ALONG, 3, 3), (ALONG, 4, 1),
    (ALONG, 4, 2), (THIRD, 5, 0), (THIRD, 2, 0), (SECOND, 3, 2), (SECOND, 0, 3), (THIRD, 2, 1), (THIRD, 1, 3),
    (FOURTH, 4, 0), (DIST,), (SECOND, 3, 1), (THIRD, 1, 1), (SECOND, 3, 3), (FOURTH, 1, 0), (FOURTH, 2, 0),
    (THIRD, 0, 1), (THIRD, 0, 2), (SECOND, 2, 2), (ALONG, 4, 3), (FOURTH, 1, 3), (ARRIVED, 1, 0), (THIRD, 1, 2),
    (THIRD, 0, 3), (ALONG, 5, 1), (SECOND, 2, 3), (FOURTH, 2, 1), (FOURTH, 5, 0), (SECOND, 4, 1), (FOURTH, 0, 1),
    (THIRD, 3, 1), (THIRD, 3, 2), (SECOND, 4, 2), (FOURTH, 1, 1), (ARRIVED, 2, 0), (THIRD, 2, 2), (ALONG, 5, 2),
    (FOURTH, 0, 3), (FOURTH, 0, 2), (ARRIVED, 0, 1), (FOURTH, 1, 2), (THIRD, 2, 3), (ARRIVED, 0, 2), (THIRD, 4, 1),
    (ARRIVED, 0, 3), (FOURTH, 3, 2), (ARRIVED, 1, 2), (ROWS,), (THIRD, 3, 3), (ARRIVED, 1, 3), (FOURTH, 2, 2),
    (ARRIVED, 1, 1), (FOURTH, 4, 1), (ALONG, 5, 3), (THIRD, 4, 2), (QKV, 0), (QKV, 1), (THIRD, 3, 0),
    (SECOND, 4, 3), (QKV, 2), (FOURTH, 2, 3), (ARRIVED, 2, 2), (ATTEND, 0), (SECOND, 5, 1), (THIRD, 4, 3),
    (SECOND, 5, 2), (ATTEND, 1), (FOURTH, 3, 1), (FOURTH, 4, 2), (ARRIVED, 4, 1), (ATTEND, 2), (ARRIVED, 2, 3),
    (ATTEND, 3), (ARRIVED, 2, 1), (FOURTH, 4, 3), (FOURTH, 3, 3), (ARRIVED, 4, 0), (THIRD, 5, 1), (ATTEND, 4),
    (SECOND, 5, 3), (ARRIVED, 3, 1), (ATTEND, 5), (THIRD, 5, 2), (FOURTH, 3, 0), (ARRIVED, 3, 3), (ARRIVED, 4, 3),
    (LOAD, 0), (ARRIVED, 5, 0), (FOURTH, 5, 1), (LOAD, 1), (ARRIVED, 4, 2), (NORM,), (ARRIVED, 3, 2),
    (THIRD, 5, 3), (FEED, 0), (ARRIVED, 3, 0), (LOAD, 2), (FEED, 1), (LOAD, 3), (FEED, 2), (ARRIVED, 5, 1),
    (FOURTH, 5, 2), (FOURTH, 5, 3), (FEED, 3), (DOWN, 1), (DOWN, 0), (ARRIVED, 5, 3), (DOWN, 3), (ARRIVED, 5, 2),
    (DOWN, 2), (MIDDLE,), (D_DOWN, 3), (R_FIRST, 0, 3), (D_DOWN, 1), (R_FIRST, 0, 1), (D_DOWN, 0), (D_DOWN, 2),
    (R_FIRST, 0, 2), (R_FIRST, 0, 0), (R_SECOND, 0, 3), (R_SECOND, 0, 1), (CHUNK, 0), (R_SECOND, 0, 2), (CHUNK, 1),
    (R_FIRST, 1, 3), (R_SECOND, 0, 0), (R_THIRD, 0, 3), (CHUNK, 2), (R_SECOND, 1, 3), (R_ALONG, 1, 3, 1),
    (R_THIRD, 0, 2), (R_FIRST, 1, 1), (CHUNK, 3), (D_NORM,), (R_FIRST, 1, 2), (R_THIRD, 0, 1), (R_FOURTH, 0, 3),
    (R_SECOND, 1, 1), (R_ALONG, 0, 3, 0), (R_THIRD, 1, 3), (D_OUT,), (R_FIRST, 1, 0), (R_SECOND, 1, 2), (D_CTX,),
    (R_FIRST, 2, 0), (R_FIRST, 2, 2), (R_ALONG, 1, 2, 1), (R_THIRD, 0, 0), (R_SECOND, 1, 0), (R_FOURTH, 0, 2),
    (D_ATTEND, 0), (D_ATTEND, 1), (R_FIRST, 2, 3), (R_SECOND, 2, 2), (R_SECOND, 2, 3), (R_ALONG, 1, 1, 1),
    (D_ATTEND, 2), (R_FOURTH, 1, 3), (R_ALONG, 0, 2, 0), (R_FIRST, 2, 1), (D_ATTEND, 3), (D_ATTEND, 4),
    (D_ATTEND, 5), (R_FOURTH, 0, 1), (R_ALONG, 1, 3, 0), (ROW, 0), (R_SECOND, 2, 1), (R_FOURTH, 1, 0), (D_QKV, 0),
    (R_THIRD, 1, 2), (D_QKV, 1), (R_THIRD, 1, 1), (ROW, 1), (R_THIRD, 2, 3), (R_THIRD, 2, 1), (D_QKV, 2),
    (R_FIRST, 3, 3), (R_ALONG, 0, 1, 0), (R_FIFTH, 1, 1), (R_FIRST, 3, 2), (R_FOURTH, 1, 2), (R_SECOND, 3, 3),
    (R_SECOND, 2, 0), (R_ALONG, 1, 2, 0), (R_FIRST, 3, 1), (D_TOK,), (R_FOURTH, 0, 0), (R_SECOND, 3, 2),
    (R_FOURTH, 1, 1), (ROW, 2), (R_FIFTH, 0, 0), (R_FOURTH, 2, 3), (R_THIRD, 2, 2), (R_ALONG, 2, 3, 0),
    (R_THIRD, 3, 3), (R_ALONG, 1, 1, 0), (R_SECOND, 3, 1), (R_THIRD, 2, 0), (R_FOURTH, 2, 2), (R_FOURTH, 2, 1),
    (R_ALONG, 2, 2, 0), (R_FIRST, 3, 0), (R_FOURTH, 3, 3), (R_PUT, 0, 0), (R_THIRD, 3, 2), (R_ALONG, 3, 3, 0),
    (R_THIRD, 3, 1), (ROW, 3), (R_FIFTH, 1, 0), (R_SECOND, 3, 0), (R_ALONG, 2, 1, 0), (R_FOURTH, 3, 2),
    (R_FOURTH, 3, 1), (R_FOURTH, 2, 0), (R_ALONG, 3, 2, 0), (R_ALONG, 3, 1, 0), (R_THIRD, 3, 0), (R_FIFTH, 2, 0),
    (R_PUT, 1, 1), (R_FOURTH, 3, 0), (R_FIFTH, 3, 0), (R_PUT, 2, 0), (ROW, 4), (R_PUT, 1, 0), (R_PUT, 3, 0),
)

GATHER_DEEP = (False, False, False, False, True, True)
REDUCE_DEEP = (False, True, False, False)
DOWN_ORDER = tuple(step[1] for step in ORDER if step[0] == D_DOWN)
SHARD_ROWS = (192, 384, 48, 144)


def run_in_order(order, steps):
    for name, *place in order:
        steps[name](*place)


def unit_starts(per_deep, per_flat):
    starts, total = [], 0
    for rows, deep in zip(SHARD_ROWS, REDUCE_DEEP):
        starts.append(total)
        total += rows * (per_deep if deep else per_flat)
    return starts, total


SIDE_STARTS, SIDE_ROWS = unit_starts(5, 8)
CROSS_STARTS, CROSS_ROWS = unit_starts(3, 4)
COLUMN_STARTS, COLUMN_ROWS = unit_starts(12, 6)


def layer_kernel(
    tok, cot, valid, vectors, s_qkv, s_out, s_ff, s_down,
    o_out, o_tok, o_qkv, o_outw, o_ff, o_down, o_rows, w_ff, probs, gu,
    w_bias, w_qkv, w_out, w_down, s_bias, v_rows, v_qkv, v_ctx, v_probs, v_scaled1, v_inv1, v_nl, v_gu, v_ffw,
    v_dn, v_db, v_nlt, v_over, full_a, full_b, both, across, sides, columns, v_sum, v_sums,
    g_sends, g_recvs, locals_, r_sends, r_recvs, row_sends, row_recvs, stages, saves, puts,
):
    y, z, x, c = whereabouts()
    length = tok.shape[0]
    lane = lax.broadcasted_iota(jnp.int32, (1, 128), 1)


    def stage(kind, src, dst, slot):
        return pltpu.make_async_copy(src, dst, stages.at[kind, slot])

    def chunk_of(n):
        return 2 * ((z + 1) % 2 if n < 2 else z % 2) + n % 2

    def ff_rows(n, m):
        return w_ff.at[pl.ds(pl.multiple_of((4 * m + chunk_of(n)) * 1536, 1536), 1536), :]

    def ff_slot(n, m):
        row = (n % 2) * 3072 + m * 1536
        return full_a.at[row : row + 1536, :]

    def ff_stages(n):
        return [stage(m, ff_rows(n, m), ff_slot(n, m), n % 2) for m in (0, 1)]

    def ff_stages_back(n):
        return [stage(m, ff_rows(n, m), v_ffw.at[m], 0) for m in (0, 1)]

    def gu_stages(n):
        return [stage(2 + m, gu.at[m, chunk_of(n)], v_gu.at[n % 2, m], n % 2) for m in (0, 1)]

    def gu_saves(n):
        return [stage(4 + m, v_gu.at[n % 2, m], gu.at[m, chunk_of(n)], n % 2) for m in (0, 1)]

    def side_by_side(ref):
        return jnp.concatenate([ref[:768, :], ref[768:, :]], 1)

    def probs_stage(pair):
        return stage(6, probs.at[pl.ds(2 * pair, 2)], v_probs.at[pair % 2], pair % 2)

    def probs_save(pair):
        return stage(7, v_probs.at[pair % 2], probs.at[pl.ds(2 * pair, 2)], pair % 2)

    def hidden_at(j):
        return pl.ds(pl.multiple_of(j * length, 16), length)


    g = [
        Gather(0, s_bias, w_bias, 16, 16, 0, False, GATHER_DEEP[0], g_sends, g_recvs, locals_),
        Gather(1, s_qkv, w_qkv, 144, 144, 0, False, GATHER_DEEP[1], g_sends, g_recvs, locals_),
        Gather(2, s_out, w_out, 48, 48, 0, False, GATHER_DEEP[2], g_sends, g_recvs, locals_),
        Gather(3, s_ff, w_ff, 384, 768, 0, True, GATHER_DEEP[3], g_sends, g_recvs, locals_),
        Gather(4, s_ff, w_ff, 384, 768, 384, True, GATHER_DEEP[4], g_sends, g_recvs, locals_),
        Gather(5, s_down, w_down, 192, 192, 0, False, GATHER_DEEP[5], g_sends, g_recvs, locals_),
    ]

    def begin_along(t, i):
        for a in g[t].halves():
            if i < 3:
                g[t].to_plane(i, a).start()
            else:

                @pl.when(in_middle(z))
                def _():
                    g[t].to_plane(3, a).start()

    def dist():
        j = lax.broadcasted_iota(jnp.int32, (length, length), 0)
        i = lax.broadcasted_iota(jnp.int32, (length, length), 1)
        v_scaled1[:, :length] = jnp.where(j < valid[0], jnp.abs(i - j).astype(F32), 1e33)

    def rows():
        total = w_bias[0:16, :].astype(F32)
        for k in range(1, 16):
            total = total + w_bias[16 * k : 16 * k + 16, :].astype(F32)
        v_rows[...] = total

    def project(n):
        part = dot(tok[...], w_qkv[768 * n : 768 * n + 768, :], 1, 1)
        if n == 0:
            part = (part + v_rows[0:1, :]).astype(BF).astype(F32) * 0.125
        if n == 2:
            part = part + v_rows[1:2, :]
        v_qkv[:, 768 * n : 768 * n + 768] = part.astype(BF)

    def attend(pair):
        col = 128 * pair
        if pair > 1:
            probs_save(pair - 2).wait()
        q_pair = v_qkv[:, col : col + 128]
        k_pair = v_qkv[:, 768 + col : 768 + col + 128]
        v_pair = v_qkv[:, 1536 + col : 1536 + col + 128]
        results = []
        for hh in range(2):
            mine = (lane < 64) if hh == 0 else (lane >= 64)
            scores = dot(k_pair, jnp.where(mine, q_pair, jnp.zeros((), BF)), 1, 1)
            scores = scores - slope_of(2 * pair + hh) * v_scaled1[:, :length]
            expo = jnp.exp(scores - jnp.max(scores, axis=0, keepdims=True)).astype(BF)
            v_probs[pair % 2, hh] = expo
            results.append(dot(expo, jnp.where(mine, v_pair, jnp.ones((), BF)), 0, 0))
        inverse = 1.0 / pltpu.roll(jnp.where(lane < 64, results[1], results[0]), 64, 1)
        v_over[:, col : col + 128] = inverse.astype(v_over.dtype)
        v_ctx[:, col : col + 128] = (jnp.where(lane < 64, results[0], results[1]) * inverse).astype(BF)
        probs_save(pair).start()

    def first_norm():
        h1 = dot(v_ctx[...], w_out[...], 1, 0) + v_rows[2:3, :] + tok[...].astype(F32)
        scaled1, inverse1 = normalise(h1)
        v_scaled1[...] = scaled1
        v_inv1[...] = jnp.broadcast_to(inverse1, v_inv1.shape)
        normed = scaled1 * v_rows[3:4, :] + v_rows[4:5, :]
        v_dn[...] = normed + v_rows[5:6, :]
        v_nl[...] = normed.astype(BF)
        v_nlt[...] = normed.astype(BF).T

    def load(n):
        for copy in ff_stages(n):
            copy.start()

    load_cot = pltpu.make_async_copy(cot, v_nl, saves.at[2])

    def feed(n):
        s = n % 2
        j = chunk_of(n)
        if n > 1:
            for copy in gu_saves(n - 2):
                copy.wait()
        for copy in ff_stages(n):
            copy.wait()
        gate = dot(v_nl[...], side_by_side(ff_slot(n, 0)), 1, 0) + v_rows[pl.ds(8 + j, 1), :]
        up = dot(v_nl[...], side_by_side(ff_slot(n, 1)), 1, 0) + v_rows[pl.ds(12 + j, 1), :]
        below = cdf(gate)
        density = jnp.exp(-0.5 * gate * gate) * 0.3989422804014327
        active = gate * below
        v_gu[s, 0] = active.astype(BF)
        v_gu[s, 1] = (up * (below + gate * density)).astype(BF)
        hidden = (active * up).astype(BF)
        full_b[hidden_at(2 * j), :] = hidden[:, :384]
        full_b[hidden_at(2 * j + 1), :] = hidden[:, 384:]
        for copy in gu_saves(n):
            copy.start()
        if n == 3:
            load_cot.start()

    def down(i):
        j = plane_at(z, i)
        hidden = jnp.concatenate([full_b[hidden_at(2 * j), :], full_b[hidden_at(2 * j + 1), :]], 1)
        v_dn[...] += dot(hidden, w_down[pl.ds(pl.multiple_of(j * 768, 768), 768), :], 1, 0)

    save_out = pltpu.make_async_copy(v_nl, o_out, saves.at[0])
    save_tok = pltpu.make_async_copy(v_ctx, o_tok, saves.at[1])

    def second_norm():
        for n in (2, 3):
            for copy in gu_saves(n):
                copy.wait()
        for n in (0, 1):
            for copy in gu_stages(n):
                copy.start()
        scaled2, inverse2 = normalise(v_dn[...])
        load_cot.wait()
        grad = v_nl[...].astype(F32)
        d_h2 = norm_back(grad * v_rows[6:7, :], scaled2, inverse2)
        v_dn[...] = d_h2
        v_db[...] = d_h2.astype(BF)
        v_nl[...] = (scaled2 * v_rows[6:7, :] + v_rows[7:8, :]).astype(BF)
        save_out.start()
        v_sum[5:6, :] = column_sum(d_h2.astype(BF).astype(F32))
        v_sum[6:7, :] = column_sum(grad * scaled2)
        v_sum[7:8, :] = column_sum(grad)


    def at_down(plane, x_, c_, h):
        return h * 3072 + index(plane, x_, c_) * 192

    def at_ff(plane, x_, c_, h):
        return (plane // 2) * 3072 + index(0, x_, c_) * 768 + h * 384

    def at_out(plane, x_, c_, h):
        return h * 768 + index(plane, x_, c_) * 48

    def at_qkv(plane, x_, c_, h):
        return 1536 + h * 2304 + index(plane, x_, c_) * 144

    def reduce_of(t, at, full):
        return Reduce(
            t, sum(SHARD_ROWS[:t]), SHARD_ROWS[t], REDUCE_DEEP[t],
            (SIDE_STARTS[t], CROSS_STARTS[t], COLUMN_STARTS[t]),
            at, full, both, across, sides, columns, r_sends, r_recvs,
        )

    r_down = reduce_of(0, at_down, full_a)
    r_ff1 = reduce_of(1, at_ff, full_b)
    r_ff2 = reduce_of(1, at_ff, full_a)
    r_out = reduce_of(2, at_out, full_b)
    r_qkv = reduce_of(3, at_qkv, full_b)

    def reducer(t, i):
        return (r_down, r_ff1 if i % 2 else r_ff2, r_out, r_qkv)[t]

    def d_down(i):
        for s in range(2):
            j = 2 * plane_at(z, i) + s
            part = dot(full_b[hidden_at(j), :], v_db[...], 0, 0)
            row = pl.multiple_of(j * 384, 384)
            full_a[pl.ds(row, 384), :] = part[:, :384].astype(BF)
            full_a[pl.ds(3072 + row, 384), :] = part[:, 384:].astype(BF)

    def chunk(n):
        s = n % 2
        j = chunk_of(n)
        if n == 0:
            for pair in (4, 5):
                probs_save(pair).wait()
            probs_stage(0).start()
            probs_stage(1).start()
        for copy in ff_stages_back(n):
            copy.start()
        for copy in gu_stages(n):
            copy.wait()
        d_hid = dot(v_db[...], w_down[pl.ds(pl.multiple_of(j * 768, 768), 768), :], 1, 1)
        d_up = (d_hid * v_gu[s, 0].astype(F32)).astype(BF)
        d_gate = (d_hid * v_gu[s, 1].astype(F32)).astype(BF)
        full = full_b if n < 2 else full_a
        for m, d in enumerate((d_gate, d_up)):
            part = dot(v_nlt[...], d, 1, 0).astype(BF)
            row = 3072 * m + 1536 * (n % 2)
            full[row : row + 768, :] = part[:, :384]
            full[row + 768 : row + 1536, :] = part[:, 384:]
            v_sum[pl.ds(8 + 4 * m + j, 1), :] = column_sum(d.astype(F32))
        for copy in ff_stages_back(n):
            copy.wait()
        back = dot(d_gate, side_by_side(v_ffw.at[0]), 1, 1) + dot(d_up, side_by_side(v_ffw.at[1]), 1, 1)
        v_dn[...] += back
        if n < 2:
            for copy in gu_stages(n + 2):
                copy.start()

    def first_norm_back():
        d_normed = v_dn[...]
        scaled = v_scaled1[...]
        v_sum[3:4, :] = column_sum(d_normed * scaled)
        v_sum[4:5, :] = column_sum(d_normed)
        d_h1 = norm_back(d_normed * v_rows[3:4, :], scaled, v_inv1[:, 0:1])
        v_dn[...] = d_h1
        v_db[...] = d_h1.astype(BF)
        v_sum[2:3, :] = column_sum(d_h1.astype(BF).astype(F32))

    def d_out():
        part = dot(v_ctx[...], v_db[...], 0, 0)
        full_b[0:768, :] = part[:, :384].astype(BF)
        full_b[768:1536, :] = part[:, 384:].astype(BF)

    v_dctx = v_nl

    def d_context():
        save_out.wait()
        v_dctx[...] = (dot(v_db[...], w_out[...], 1, 1) * v_over[...].astype(F32)).astype(BF)

    def attend_back(pair):
        col = 128 * pair
        probs_stage(pair).wait()
        q_pair = v_qkv[:, col : col + 128]
        k_pair = v_qkv[:, 768 + col : 768 + col + 128]
        v_pair = v_qkv[:, 1536 + col : 1536 + col + 128]
        d_pair = v_dctx[:, col : col + 128]
        product = d_pair.astype(F32) * v_ctx[:, col : col + 128].astype(F32)
        high = product.astype(BF)
        low = (product - high.astype(F32)).astype(BF)
        d_q, d_k, d_v = [], [], []
        for hh in range(2):
            mine = (lane < 64) if hh == 0 else (lane >= 64)
            head = jnp.broadcast_to(mine.astype(BF), (16, 128))
            inner = (dot(head, high, 1, 1) + dot(head, low, 1, 1))[0:1, :]
            d_head = jnp.where(mine, d_pair, jnp.zeros((), BF))
            d_probs = dot(v_pair, d_head, 1, 1)
            expo = v_probs[pair % 2, hh]
            d_scores = (expo.astype(F32) * (d_probs - inner)).astype(BF)
            d_v.append(dot(expo, d_head, 1, 0))
            d_k.append(dot(d_scores, jnp.where(mine, q_pair, jnp.zeros((), BF)), 1, 0))
            d_q.append(dot(k_pair, d_scores, 0, 0))
        upper = lax.broadcasted_iota(jnp.int32, (128, 1), 0) < 64
        v_qkv[:, col : col + 128] = (jnp.where(upper, d_q[0], d_q[1]) * 0.125).astype(BF).T
        v_qkv[:, 768 + col : 768 + col + 128] = (d_k[0] + d_k[1]).astype(BF)
        v_qkv[:, 1536 + col : 1536 + col + 128] = (d_v[0] + d_v[1]).astype(BF)
        if pair < 4:
            probs_stage(pair + 2).start()
        if pair == 5:
            v_sum[0:1, :] = column_sum(v_qkv[:, 0:768].astype(F32))
            v_sum[1:2, :] = column_sum(v_qkv[:, 1536:2304].astype(F32))

    def d_qkv_weight(n):
        part = dot(v_qkv[:, 768 * n : 768 * n + 768], tok[...], 0, 0)
        full_b[1536 + 768 * n : 2304 + 768 * n, :] = part[:, :384].astype(BF)
        full_b[3840 + 768 * n : 4608 + 768 * n, :] = part[:, 384:].astype(BF)

    def d_tokens():
        v_ctx[...] = (dot(v_qkv[...], w_qkv[...], 1, 0) + v_dn[...]).astype(BF)
        save_tok.start()

    def row_copy(n):
        device = (
            (y, index(z, x, 1 - c)), (y, index(z, 1 - x, c)), (1 - y, index(z, x, c)),
            *[(y, index(plane_at(z, i), x, c)) for i in (1, 2, 3)],
        )[n]
        return pltpu.make_async_remote_copy(
            src_ref=v_sum,
            dst_ref=v_sums.at[n],
            send_sem=row_sends.at[n],
            recv_sem=row_recvs.at[n],
            device_id=device,
            device_id_type=MESH,
        )

    def row_step(n):
        if 1 <= n <= 3:
            row_copy(n - 1).wait()
            v_sum[...] = v_sum[...] + v_sums[n - 1]
        if n < 3:
            row_copy(n).start()
        if n == 3:
            for m in (3, 4, 5):
                row_copy(m).start()
        if n == 4:
            for m in (3, 4, 5):
                row_copy(m).wait()
            o_rows[...] = v_sum[...] + v_sums[3] + v_sums[4] + v_sums[5]

    outs = (o_down, o_ff, o_outw, o_qkv)
    placed = []

    s_bias[...] = spread_vectors(vectors[...], index(z, x, c)).astype(BF)
    greet()
    run_in_order(
        ORDER,
        {
            OWN: lambda t: g[t].begin_plane(),
            ALONG: begin_along,
            SECOND: lambda t, i: g[t].second(i),
            THIRD: lambda t, i: g[t].third(i),
            FOURTH: lambda t, i: g[t].fourth(i),
            ARRIVED: lambda t, i: g[t].arrived(i),
            DIST: dist,
            ROWS: rows,
            QKV: project,
            ATTEND: attend,
            NORM: first_norm,
            LOAD: load,
            FEED: feed,
            DOWN: down,
            MIDDLE: second_norm,
            D_DOWN: d_down,
            CHUNK: chunk,
            D_NORM: first_norm_back,
            D_OUT: d_out,
            D_CTX: d_context,
            D_ATTEND: attend_back,
            D_QKV: d_qkv_weight,
            D_TOK: d_tokens,
            ROW: row_step,
            R_FIRST: lambda t, i: reducer(t, i).first(i),
            R_SECOND: lambda t, i: reducer(t, i).second(i),
            R_THIRD: lambda t, i: reducer(t, i).third(i),
            R_FOURTH: lambda t, i: reducer(t, i).fourth(i),
            R_ALONG: lambda t, i, a: reducer(t, i).along(i, a),
            R_FIFTH: lambda t, a: reducer(t, 0).fifth(a),
            R_PUT: lambda t, a: placed.extend(reducer(t, 0).put(a, outs[t], puts)),
        },
    )
    save_tok.wait()
    for copy in placed:
        copy.wait()
    for t in range(6):
        g[t].finish()
    for t in range(4):
        reducer(t, 0).finish()


def finish_kernel(tok, qkv, out, ff, down, rows, fwd, *outs):
    o_fwd, o_tok, o_qkv, o_qv, o_out, o_outb, o_g1, o_s1, o_ff, o_ffb, o_down, o_downb, o_g2, o_s2 = outs
    k = lax.axis_index("fsdp")
    o_fwd[...] = fwd[...]
    o_tok[...] = tok[...]
    for h in (0, 1):
        o_qkv[:, 384 * h : 384 * h + 384] = qkv[h].astype(F32)
        o_out[:, 384 * h : 384 * h + 384] = out[h].astype(F32)
        o_down[:, 384 * h : 384 * h + 384] = down[h].astype(F32)
        o_ff[384 * h : 384 * h + 384, :] = ff[h].astype(F32)
    by_vector = (o_qv, o_outb, o_g1, o_s1, o_ffb, o_downb, o_g2, o_s2)
    for ref, (_, n, row) in zip(by_vector, VECTORS):
        per = 768 // n
        line = rows[pl.ds(row + k // per, 1), :]
        moved = pltpu.roll(jnp.broadcast_to(line, (8, 768)), ((768 - (k % per) * n) % 768), 1)
        ref[...] = moved[0, 0:n]


def fused_on_device(
    tokens,
    qkv_weight,
    qv_bias,
    out_weight,
    out_bias,
    norm1_gain,
    norm1_shift,
    ff_weight,
    ff_bias,
    down_weight,
    down_bias,
    norm2_gain,
    norm2_shift,
    pair_length,
    cotangent,
):
    length, width = tokens.shape
    vectors = jnp.concatenate(
        [qv_bias, out_bias, norm1_gain, norm1_shift, ff_bias, down_bias, norm2_gain, norm2_shift]
    )
    vectors = vectors.astype(F32).reshape(1, width)
    in_vmem = pl.BlockSpec(memory_space=pltpu.VMEM)
    in_smem = pl.BlockSpec(memory_space=pltpu.SMEM)
    anywhere = pl.BlockSpec(memory_space=pl.ANY)
    struct = jax.ShapeDtypeStruct
    vmem = pltpu.VMEM
    dma = pltpu.SemaphoreType.DMA
    output, d_tokens, d_qkv, d_out, d_ff, d_down, d_rows = pl.pallas_call(
        layer_kernel,
        name="layer",
        out_shape=[
            struct((length, width), BF),
            struct((length, width), BF),
            struct((2, 144, 384), BF),
            struct((2, 48, 384), BF),
            struct((2, 384, 384), BF),
            struct((2, 192, 384), BF),
            struct((16, width), F32),
            struct((12288, 384), BF),
            struct((HEADS, length, length), BF),
            struct((2, 4, length, 768), BF),
        ],
        in_specs=[in_vmem, anywhere, in_smem, in_vmem] + [anywhere] * 4,
        out_specs=[anywhere] * 6 + [in_vmem] + [anywhere] * 3,
        scratch_shapes=[
            vmem((256, width), BF),
            vmem((2304, width), BF),
            vmem((width, width), BF),
            vmem((3072, width), BF),
            vmem((16, width), BF),
            vmem((16, width), F32),
            vmem((length, 2304), BF),
            vmem((length, width), BF),
            vmem((2, 2, length, length), BF),
            vmem((length, width), F32),
            vmem((length, 128), F32),
            vmem((length, width), BF),
            vmem((2, 2, length, 768), BF),
            vmem((2, 1536, 384), BF),
            vmem((length, width), F32),
            vmem((length, width), BF),
            vmem((width, length), BF),
            vmem((length, width), BF),
            vmem((6144, 384), BF),
            vmem((6144, 384), BF),
            vmem((768 * 16, 384), BF),
            vmem((CROSS_ROWS, 384), BF),
            vmem((SIDE_ROWS, 384), BF),
            vmem((COLUMN_ROWS, 384), BF),
            vmem((16, width), F32),
            vmem((6, 16, width), F32),
            dma((6, Gather.SLOTS)),
            dma((6, Gather.SLOTS)),
            dma((6,)),
            dma((4, Reduce.SLOTS)),
            dma((4, Reduce.SLOTS)),
            dma((6,)),
            dma((6,)),
            dma((8, 2)),
            dma((3,)),
            dma((4, 2)),
        ],
        compiler_params=pltpu.CompilerParams(
            collective_id=0, has_side_effects=True, vmem_limit_bytes=63 * 2**20
        ),
    )(tokens, cotangent, pair_length, vectors, qkv_weight.T, out_weight, ff_weight, down_weight)[:7]

    def vector(n):
        return struct((n,), F32)

    full = [struct(s, F32) for s in ((144, width), (48, width), (768, 384), (192, width))]
    results = pl.pallas_call(
        finish_kernel,
        name="finish",
        out_shape=[
            struct((length, width), BF), struct((length, width), BF), full[0], vector(96), full[1], vector(48),
            vector(48), vector(48), full[2], vector(384), full[3], vector(48), vector(48), vector(48),
        ],
        in_specs=[in_vmem] * 7,
        out_specs=[in_vmem] * 14,
    )(d_tokens, d_qkv, d_out, d_ff, d_down, d_rows, output)
    results = list(results)
    results[2] = results[2].T
    return tuple(results)


def solution(mesh):
    in_specs = (
        P(("rep", "fsdp"), None),
        P(None, "fsdp"),
        P("fsdp"),
        P("fsdp", None),
        P("fsdp"),
        P("fsdp"),
        P("fsdp"),
        P(None, "fsdp"),
        P("fsdp"),
        P("fsdp", None),
        P("fsdp"),
        P("fsdp"),
        P("fsdp"),
        P(("rep", "fsdp")),
        P(("rep", "fsdp"), None),
    )
    out_specs = (
        P(("rep", "fsdp"), None),
        P(("rep", "fsdp"), None),
        P(None, "fsdp"),
        P("fsdp"),
        P("fsdp", None),
        P("fsdp"),
        P("fsdp"),
        P("fsdp"),
        P(None, "fsdp"),
        P("fsdp"),
        P("fsdp", None),
        P("fsdp"),
        P("fsdp"),
        P("fsdp"),
    )
    planes = mesh.shape["rep"] == 2 and mesh.shape["fsdp"] == 16
    return jax.shard_map(
        fused_on_device if planes else plain_on_device, mesh=mesh, in_specs=in_specs, out_specs=out_specs, check_vma=False
    )
```

```python
import jax
import jax.numpy as jnp
from jax import lax
from jax.experimental import pallas as pl
from jax.experimental.pallas import tpu as pltpu
from jax.sharding import PartitionSpec as P

HEADS = 12
MESH = pl.DeviceIdType.MESH
BF = jnp.bfloat16
F32 = jnp.float32


def layer_norm(h, gain, shift):
    mean = jnp.mean(h, -1, keepdims=True)
    centered = h - mean
    spread = jnp.mean(centered * centered, -1, keepdims=True)
    return centered * lax.rsqrt(spread + 1e-05) * gain + shift


def inner_rows(left, right):
    return lax.dot_general(
        left, right, (((0,), (0,)), ((), ())), preferred_element_type=jnp.float32
    )


def times_transposed(left, right):
    return lax.dot_general(
        left, right, (((1,), (1,)), ((), ())), preferred_element_type=jnp.float32
    )


def score_block(query, keys, slope, valid):
    length = query.shape[0]
    place = jnp.arange(length, dtype=jnp.float32)
    scores = times_transposed(query, keys) * 0.125 - slope * jnp.abs(
        place[:, None] - place[None, :]
    )
    allowed = jnp.arange(length, dtype=jnp.int32) < valid
    return jnp.where(allowed[None, :], scores, -1e30)


def head_slopes():
    return 2.0 ** (-8.0 * jnp.arange(1, HEADS + 1, dtype=jnp.float32) / HEADS)


def forward(tokens, attention, feedforward, valid):
    qkv_weight, qv_bias, out_weight, out_bias, gain1, shift1 = attention
    ff_weight, ff_bias, down_weight, down_bias, gain2, shift2 = feedforward
    length, width = tokens.shape
    bias_f = qv_bias.astype(jnp.float32)
    full_bias = jnp.concatenate([bias_f[:width], jnp.zeros((width,), jnp.float32), bias_f[width:]])
    qkv = (jnp.dot(tokens, qkv_weight, preferred_element_type=jnp.float32) + full_bias).astype(
        jnp.bfloat16
    )
    per_head = qkv.reshape(length, 3, HEADS, width // HEADS).transpose(1, 2, 0, 3)

    def attend(item):
        query, keys, values, slope = item
        scores = score_block(query, keys, slope, valid)
        top = jnp.max(scores, -1, keepdims=True)
        expo = jnp.exp(scores - top)
        total = jnp.sum(expo, -1, keepdims=True)
        probs = (expo / total).astype(jnp.bfloat16)
        return (
            jnp.dot(probs, values, preferred_element_type=jnp.float32),
            top[:, 0] + jnp.log(total[:, 0]),
        )

    context, log_total = lax.map(attend, (per_head[0], per_head[1], per_head[2], head_slopes()))
    context = context.transpose(1, 0, 2).reshape(length, width).astype(jnp.bfloat16)
    attended = jnp.dot(context, out_weight, preferred_element_type=jnp.float32) + out_bias.astype(
        jnp.float32
    )
    residual1 = tokens.astype(jnp.float32) + attended
    normed = layer_norm(residual1, gain1.astype(jnp.float32), shift1.astype(jnp.float32))
    normed_low = normed.astype(jnp.bfloat16)
    gate_up = jnp.dot(normed_low, ff_weight, preferred_element_type=jnp.float32) + ff_bias.astype(
        jnp.float32
    )
    half = gate_up.shape[1] // 2
    hidden = (jax.nn.gelu(gate_up[:, :half], approximate=False) * gate_up[:, half:]).astype(
        jnp.bfloat16
    )
    residual2 = (
        normed
        + jnp.dot(hidden, down_weight, preferred_element_type=jnp.float32)
        + down_bias.astype(jnp.float32)
    )
    return (per_head, log_total, context, residual1, normed_low, gate_up, hidden, residual2)


def gelu_product(gate, up):
    return jax.nn.gelu(gate, approximate=False) * up


def plain_on_device(
    tokens,
    qkv_weight,
    qv_bias,
    out_weight,
    out_bias,
    norm1_gain,
    norm1_shift,
    ff_weight,
    ff_bias,
    down_weight,
    down_bias,
    norm2_gain,
    norm2_shift,
    pair_length,
    cotangent,
):
    valid = pair_length[0]
    attention = (
        lax.all_gather(qkv_weight, "fsdp", axis=1, tiled=True),
        lax.all_gather(qv_bias, "fsdp", axis=0, tiled=True),
        lax.all_gather(out_weight, "fsdp", axis=0, tiled=True),
        lax.all_gather(out_bias, "fsdp", axis=0, tiled=True),
        lax.all_gather(norm1_gain, "fsdp", axis=0, tiled=True),
        lax.all_gather(norm1_shift, "fsdp", axis=0, tiled=True),
    )
    feedforward = (
        lax.all_gather(ff_weight, "fsdp", axis=1, tiled=True),
        lax.all_gather(ff_bias, "fsdp", axis=0, tiled=True),
        lax.all_gather(down_weight, "fsdp", axis=0, tiled=True),
        lax.all_gather(down_bias, "fsdp", axis=0, tiled=True),
        lax.all_gather(norm2_gain, "fsdp", axis=0, tiled=True),
        lax.all_gather(norm2_shift, "fsdp", axis=0, tiled=True),
    )
    stored = forward(tokens, attention, feedforward, valid)
    gain2 = feedforward[4].astype(jnp.float32)
    shift2 = feedforward[5].astype(jnp.float32)
    output = layer_norm(stored[7], gain2, shift2).astype(jnp.bfloat16)
    per_head, log_total, context, residual1, normed_low, gate_up, hidden, residual2 = stored
    full_qkv, bias_unused, full_out, out_unused, gain1, shift1 = attention
    full_ff, ff_unused, full_down, down_unused, gain_unused, shift_unused = feedforward
    length, width = tokens.shape
    unused_out, back_second = jax.vjp(layer_norm, residual2, gain2, shift2)
    d_res2, d_gain2, d_shift2 = back_second(cotangent.astype(jnp.float32))
    d_branch = d_res2.astype(jnp.bfloat16)
    d_down = inner_rows(hidden, d_branch)
    d_down_bias = jnp.sum(d_branch.astype(jnp.float32), 0)
    d_hidden = times_transposed(d_branch, full_down).astype(jnp.bfloat16)
    half = gate_up.shape[1] // 2
    unused_prod, back_gelu = jax.vjp(gelu_product, gate_up[:, :half], gate_up[:, half:])
    d_gate, d_up = back_gelu(d_hidden.astype(jnp.float32))
    d_gate_up = jnp.concatenate([d_gate, d_up], 1).astype(jnp.bfloat16)
    d_ff = inner_rows(normed_low, d_gate_up)
    d_ff_bias = jnp.sum(d_gate_up.astype(jnp.float32), 0)
    d_normed = times_transposed(d_gate_up, full_ff) + d_res2
    unused_norm, back_first = jax.vjp(
        layer_norm, residual1, gain1.astype(jnp.float32), shift1.astype(jnp.float32)
    )
    d_res1, d_gain1, d_shift1 = back_first(d_normed)
    ff_terms = (d_ff, d_ff_bias, d_down, d_down_bias, d_gain2, d_shift2)
    ff_grads = (
        lax.psum_scatter(ff_terms[0], "fsdp", scatter_dimension=1, tiled=True),
        lax.psum_scatter(ff_terms[1], "fsdp", scatter_dimension=0, tiled=True),
        lax.psum_scatter(ff_terms[2], "fsdp", scatter_dimension=0, tiled=True),
        lax.psum_scatter(ff_terms[3], "fsdp", scatter_dimension=0, tiled=True),
        lax.psum_scatter(ff_terms[4], "fsdp", scatter_dimension=0, tiled=True),
        lax.psum_scatter(ff_terms[5], "fsdp", scatter_dimension=0, tiled=True),
    )
    ff_grads = (
        lax.psum(ff_grads[0].astype(jnp.bfloat16), "rep").astype(jnp.float32),
        lax.psum(ff_grads[1].astype(jnp.bfloat16), "rep").astype(jnp.float32),
        lax.psum(ff_grads[2].astype(jnp.bfloat16), "rep").astype(jnp.float32),
        lax.psum(ff_grads[3].astype(jnp.bfloat16), "rep").astype(jnp.float32),
        lax.psum(ff_grads[4].astype(jnp.bfloat16), "rep").astype(jnp.float32),
        lax.psum(ff_grads[5].astype(jnp.bfloat16), "rep").astype(jnp.float32),
    )
    d_attended = d_res1.astype(jnp.bfloat16)
    d_out = inner_rows(context, d_attended)
    d_out_bias = jnp.sum(d_attended.astype(jnp.float32), 0)
    d_context = times_transposed(d_attended, full_out).astype(jnp.bfloat16)
    d_context = d_context.reshape(length, HEADS, width // HEADS).transpose(1, 0, 2)

    def attend_back(item):
        query, keys, values, grad_context, total_log, slope = item
        scores = score_block(query, keys, slope, valid)
        probs = jnp.exp(scores - total_log[:, None])
        probs_low = probs.astype(jnp.bfloat16)
        d_probs = times_transposed(grad_context, values)
        d_scores = (probs * (d_probs - jnp.sum(probs * d_probs, -1, keepdims=True))).astype(
            jnp.bfloat16
        )
        d_query = jnp.dot(d_scores, keys, preferred_element_type=jnp.float32) * 0.125
        d_keys = inner_rows(d_scores, query) * 0.125
        d_values = inner_rows(probs_low, grad_context)
        return (d_query, d_keys, d_values)

    d_query, d_keys, d_values = lax.map(
        attend_back, (per_head[0], per_head[1], per_head[2], d_context, log_total, head_slopes())
    )
    d_qkv = (
        jnp.stack([d_query, d_keys, d_values])
        .transpose(2, 0, 1, 3)
        .reshape(length, 3 * width)
        .astype(jnp.bfloat16)
    )
    d_qkv_w = inner_rows(tokens, d_qkv)
    column_sums = jnp.sum(d_qkv.astype(jnp.float32), 0)
    d_qv = jnp.concatenate([column_sums[:width], column_sums[2 * width :]])
    d_tokens = (times_transposed(d_qkv, full_qkv) + d_res1).astype(jnp.bfloat16)
    at_terms = (d_qkv_w, d_qv, d_out, d_out_bias, d_gain1, d_shift1)
    at_grads = (
        lax.psum_scatter(at_terms[0], "fsdp", scatter_dimension=1, tiled=True),
        lax.psum_scatter(at_terms[1], "fsdp", scatter_dimension=0, tiled=True),
        lax.psum_scatter(at_terms[2], "fsdp", scatter_dimension=0, tiled=True),
        lax.psum_scatter(at_terms[3], "fsdp", scatter_dimension=0, tiled=True),
        lax.psum_scatter(at_terms[4], "fsdp", scatter_dimension=0, tiled=True),
        lax.psum_scatter(at_terms[5], "fsdp", scatter_dimension=0, tiled=True),
    )
    at_grads = (
        lax.psum(at_grads[0].astype(jnp.bfloat16), "rep").astype(jnp.float32),
        lax.psum(at_grads[1].astype(jnp.bfloat16), "rep").astype(jnp.float32),
        lax.psum(at_grads[2].astype(jnp.bfloat16), "rep").astype(jnp.float32),
        lax.psum(at_grads[3].astype(jnp.bfloat16), "rep").astype(jnp.float32),
        lax.psum(at_grads[4].astype(jnp.bfloat16), "rep").astype(jnp.float32),
        lax.psum(at_grads[5].astype(jnp.bfloat16), "rep").astype(jnp.float32),
    )
    return (
        output,
        d_tokens,
        at_grads[0],
        at_grads[1],
        at_grads[2],
        at_grads[3],
        at_grads[4],
        at_grads[5],
        ff_grads[0],
        ff_grads[1],
        ff_grads[2],
        ff_grads[3],
        ff_grads[4],
        ff_grads[5],
    )


def dot(left, right, left_dim, right_dim):
    return lax.dot_general(
        left, right, (((left_dim,), (right_dim,)), ((), ())), preferred_element_type=F32
    )


def whereabouts():
    y = lax.axis_index("rep")
    k = lax.axis_index("fsdp")
    return y, k // 4, (k // 2) % 2, k % 2


def index(z, x, c):
    return z * 4 + x * 2 + c


def plane_at(z, i):
    return (z, z + 1 - 2 * (z % 2), (z + 2) % 4, 3 - z)[i]


def in_middle(z):
    return (z == 1) | (z == 2)


def greet(barrier):
    y, z, x, c = whereabouts()
    friends = [(y, index(z, x, 1 - c)), (y, index(z, 1 - x, c)), (1 - y, index(z, x, c))]
    friends += [(y, index(plane_at(z, i), x, c)) for i in (1, 2, 3)]
    for friend in friends:
        pl.semaphore_signal(barrier, inc=1, device_id=friend, device_id_type=MESH)
    return len(friends)


class Gather:
    Z, X, Y, D, C = 0, 8, 12, 16, 20
    SLOTS = 28

    def __init__(self, t, src, dst, rows, pitch, start, by_row, deep, sends, recvs, locals_):
        self.t, self.src, self.dst, self.rows, self.by_row, self.deep = t, src, dst, rows, by_row, deep
        self.pitch, self.start = pitch, start
        self.sends, self.recvs, self.locals_ = sends, recvs, locals_
        self.y, self.z, self.x, self.c = whereabouts()

    def plane(self, i):
        return plane_at(self.z, i)

    def half(self, ref, base, h):
        if self.by_row:
            n = self.rows // 2
            return ref.at[pl.ds(pl.multiple_of(base + h * n, 16), n), :]
        n = ref.shape[1] // 2
        return ref.at[pl.ds(base, self.rows), pl.ds(pl.multiple_of(h * n, 128), n)]

    def part(self, k, h):
        return self.half(self.dst, pl.multiple_of(k * self.pitch + self.start, 16), h)

    def shard(self, k):
        return self.dst.at[pl.ds(pl.multiple_of(k * self.pitch + self.start, 16), self.rows), :]

    def whole(self):
        return self.src.at[pl.ds(self.start, self.rows), :]

    def copy(self, slot, src, dst, device, arrival=None):
        return pltpu.make_async_remote_copy(
            src_ref=src,
            dst_ref=dst,
            send_sem=self.sends.at[self.t, slot],
            recv_sem=self.recvs.at[self.t, slot if arrival is None else arrival],
            device_id=device,
            device_id_type=MESH,
        )

    def halves(self):
        return (0, 1) if self.deep else (0,)

    def to_plane(self, i, a):
        h = 1 - self.y if a else self.y
        k = index(self.z, self.x, self.c)
        device = (self.y, index(self.plane(i), self.x, self.c))
        return self.copy(self.Z + 2 * i + a, self.half(self.src, self.start, h), self.part(k, h), device)

    def relay(self, a):
        h = 1 - self.y if a else self.y
        k = index(self.plane(2), self.x, self.c)
        device = (self.y, index(self.plane(1), self.x, self.c))
        return self.copy(self.Z + a, self.part(k, h), self.part(k, h), device, self.Z + 6 + a)

    def to_x(self, i):
        k = index(self.plane(i), self.x, self.c)
        src = self.half(self.src, self.start, self.y) if i == 0 else self.part(k, self.y)
        return self.copy(
            self.X + i, src, self.part(k, self.y), (self.y, index(self.z, 1 - self.x, self.c))
        )

    def to_y(self, i):
        k = index(self.plane(i), self.x, self.c)
        part = self.part(k, self.y)
        return self.copy(self.Y + i, part, part, (1 - self.y, index(self.z, self.x, self.c)))

    def onward(self, i):
        c = 0 if i == 0 or self.deep else self.c
        k = index(self.plane(i), (1 - self.x) * (1 - c) + self.x * c, self.c)
        part = self.part(k, self.y * (1 - c) + (1 - self.y) * c)
        x = self.x * (1 - c) + (1 - self.x) * c
        y = self.y * c + (1 - self.y) * (1 - c)
        return self.copy(self.D + i, part, part, (y, index(self.z, x, self.c)))

    def to_core(self, i, home):
        k = index(self.plane(i), self.x if home else 1 - self.x, self.c)
        src = self.whole() if home and i == 0 else self.shard(k)
        device = (self.y, index(self.z, self.x, 1 - self.c))
        return self.copy(self.C + i + (0 if home else 4), src, self.shard(k), device)

    def own(self):
        return pltpu.make_async_copy(
            self.whole(), self.shard(index(self.z, self.x, self.c)), self.locals_.at[self.t]
        )

    def begin(self):
        for a in self.halves():
            for i in (2, 1):
                self.to_plane(i, a).start()

            @pl.when(in_middle(self.z))
            def _():
                self.to_plane(3, a).start()

    def begin_plane(self):
        self.to_x(0).start()
        self.to_core(0, True).start()
        self.own().start()

    def second(self, i):
        if i == 0:
            return
        for a in self.halves():
            self.to_plane(i, a).wait_recv()
            if i == 2:

                @pl.when(in_middle(self.z))
                def _():
                    self.relay(a).start()

            if a == 0:
                self.to_x(i).start()
                if not self.deep:
                    self.to_y(i).start()
        if self.deep:
            self.to_core(i, True).start()

    def third(self, i):
        if i and not self.deep:
            self.to_y(i).wait_recv()
            self.to_core(i, True).start()
        self.to_x(i).wait_recv()
        self.onward(i).start()

    def fourth(self, i):
        self.onward(i).wait_recv()
        self.to_core(i, False).start()

    def arrived(self, i):
        self.to_core(i, True).wait_recv()
        self.to_core(i, False).wait_recv()
        if i == 0:
            self.own().wait()

    def finish(self):
        for a in self.halves():
            for i in (1, 2):
                self.to_plane(i, a).wait_send()

            @pl.when(in_middle(self.z))
            def _():
                self.to_plane(3, a).wait_send()
                self.relay(a).wait_send()

        for i in range(4):
            self.to_x(i).wait_send()
            if i and not self.deep:
                self.to_y(i).wait_send()
            self.onward(i).wait_send()
            self.to_core(i, True).wait_send()
            self.to_core(i, False).wait_send()


class Reduce:
    CORE, DIAGONAL, EARLY, LATE, PLANE, ARRIVE, LAST, SLOTS = 0, 4, 5, 6, 7, 36, 38, 40

    def __init__(self, t, base, rows, deep, starts, at, full, both, across, sides, columns, sends, recvs):
        self.t, self.base, self.rows, self.deep, self.at = t, base, rows, deep, at
        self.full, self.both, self.across, self.sides, self.columns = full, both, across, sides, columns
        self.starts, self.sends, self.recvs = starts, sends, recvs
        self.y, self.z, self.x, self.c = whereabouts()

    def copy(self, slot, src, dst, device, arrival=None):
        return pltpu.make_async_remote_copy(
            src_ref=src,
            dst_ref=dst,
            send_sem=self.sends.at[self.t, slot],
            recv_sem=self.recvs.at[self.t, slot if arrival is None else arrival],
            device_id=device,
            device_id_type=MESH,
        )

    def rows_of(self, ref, row):
        return ref.at[pl.ds(pl.multiple_of(row, 16), self.rows), :]

    def unit(self, i, away_x, c, h):
        x = 1 - self.x if away_x else self.x
        return self.rows_of(self.full, self.at(plane_at(self.z, i), x, c, h))

    def mine(self, i, away_x, away_h):
        n = i * 4 + away_x * 2 + away_h
        return self.rows_of(self.both, self.base * 16 + n * self.rows)

    def side(self, i, s):
        n = (i + s if i == 0 else i + 1) if self.deep else i * 2 + s
        return self.rows_of(self.sides, self.starts[0] + n * self.rows)

    def cross(self, i):
        return self.rows_of(self.across, self.starts[1] + (i - 1 if self.deep else i) * self.rows)

    def column(self, n, a):
        return self.rows_of(self.columns, self.starts[2] + (2 * n + a if self.deep else n) * self.rows)

    def halves(self):
        return (0, 1) if self.deep else (0,)

    def way(self, i):
        return 0 if self.deep else (1 if i == 0 else self.c)

    def neighbour(self, over_x):
        return (
            self.y * over_x + (1 - self.y) * (1 - over_x),
            index(self.z, (1 - self.x) * over_x + self.x * (1 - over_x), self.c),
        )

    def to_core(self, i, n):
        device = (self.y, index(self.z, self.x, 1 - self.c))
        h = 1 - self.y if n % 2 else self.y
        src = self.unit(i, n // 2, 1 - self.c, h)
        return self.copy(i * 9 + n, src, self.mine(i, n // 2, n % 2), device)

    def diagonal(self, i):
        device = self.neighbour(self.way(i))
        return self.copy(i * 9 + self.DIAGONAL, self.mine(i, 1, 1), self.cross(i), device)

    def early(self, i):
        w = self.way(i)
        return self.copy(i * 9 + self.EARLY, self.mine(i, w, 1 - w), self.side(i, 0), self.neighbour(w))

    def late(self, i):
        w = self.way(i)
        return self.copy(i * 9 + self.LATE, self.mine(i, 1 - w, w), self.side(i, 1), self.neighbour(1 - w))

    def over_x(self, i, a):
        slot = i * 9 + (self.LATE if a else self.EARLY)
        return self.copy(slot, self.mine(i, 1, a), self.side(i, a), self.neighbour(1))

    def to_plane(self, i, a):
        slot = i * 9 + self.PLANE + a
        src = self.mine(i, 0, a)
        if i < 3:
            device = (self.y, index(plane_at(self.z, i), self.x, self.c))
            return self.copy(slot, src, self.column(i - 1, a), device)
        near, far = plane_at(self.z, 1), plane_at(self.z, 3)
        middle = (self.z % 3 + 1) // 2
        plane = far * middle + near * (1 - middle)
        arrival = slot * middle + (self.ARRIVE + a) * (1 - middle)
        return self.copy(
            slot, src, self.column(3 - middle, a), (self.y, index(plane, self.x, self.c)), arrival
        )

    def handed(self, a):
        slot = 3 * 9 + self.PLANE + a
        device = (self.y, index(plane_at(self.z, 1), self.x, self.c))
        return self.copy(slot, self.mine(3, 0, a), self.column(3, a), device, self.ARRIVE + a)

    def mirrored(self, a):
        slot = 3 * 9 + self.PLANE + a
        device = (self.y, index(plane_at(self.z, 3), self.x, self.c))
        return self.copy(slot, self.mine(3, 0, a), self.column(2, a), device)

    def last(self, a):
        device = (1 - self.y, index(self.z, self.x, self.c))
        b = 1 - a if self.deep else a
        return self.copy(self.LAST + a, self.column(4, a), self.column(5, b), device, self.LAST + b)

    def first(self, i):
        for n in (3, 2, 1, 0):
            self.to_core(i, n).start()

    def second(self, i):
        for n in (3, 2, 1, 0):
            self.to_core(i, n).wait()
            h = 1 - self.y if n % 2 else self.y
            part = self.mine(i, n // 2, n % 2)
            part[...] = part[...] + self.unit(i, n // 2, self.c, h)[...]
            if self.deep and i == 0:
                if n > 1:
                    self.over_x(i, n - 2).start()
            elif n == 3:
                self.diagonal(i).start()
        if not self.deep:
            self.early(i).start()

    def third(self, i):
        if self.deep and i == 0:
            return
        w = self.way(i)
        self.diagonal(i).wait_recv()
        part = self.mine(i, 1 - w, w)
        part[...] = part[...] + self.cross(i)[...]
        if self.deep:
            self.over_x(i, 0).start()
        else:
            self.late(i).start()

    def fourth(self, i):
        if self.deep:
            for a in (0, 1) if i == 0 else (0,):
                self.over_x(i, a).wait_recv()
                part = self.mine(i, 0, a)
                part[...] = part[...] + self.side(i, a)[...]
            return
        self.early(i).wait_recv()
        self.late(i).wait_recv()
        part = self.mine(i, 0, 0)
        total = part[...].astype(F32) + self.side(i, 0)[...].astype(F32)
        part[...] = (total + self.side(i, 1)[...].astype(F32)).astype(BF)

    def along(self, i, a):
        if i == 2:

            @pl.when(in_middle(self.z))
            def _():
                self.handed(a).wait_recv()
                part = self.mine(2, 0, a)
                part[...] = part[...] + self.column(3, a)[...]

        self.to_plane(i, a).start()

    def fifth(self, a):
        for i in (1, 2):
            self.to_plane(i, a).wait_recv()
        total = self.mine(0, 0, a)[...].astype(F32)
        total = total + self.column(0, a)[...].astype(F32) + self.column(1, a)[...].astype(F32)

        @pl.when(in_middle(self.z))
        def _():
            self.mirrored(a).wait_recv()
            self.column(4, a)[...] = (total + self.column(2, a)[...].astype(F32)).astype(BF)

        @pl.when(jnp.logical_not(in_middle(self.z)))
        def _():
            self.column(4, a)[...] = total.astype(BF)

        self.last(a).start()

    def put(self, a, out, semaphore):
        self.last(a).wait_send()
        self.last(1 - a if self.deep else a).wait_recv()
        here, there = self.y, 1 - self.y
        own, other = self.column(4, a), self.column(5, a)
        if self.deep:
            own[...] = (own[...].astype(F32) + other[...].astype(F32)).astype(BF)
            pairs = [((there if a else here), own)]
        else:
            pairs = [(here, own), (there, other)]
        copies = [pltpu.make_async_copy(v, out.at[h], semaphore.at[self.t, a + n]) for n, (h, v) in enumerate(pairs)]
        for copy in copies:
            copy.start()
        return copies

    def finish(self):
        for i in range(4):
            if self.deep:
                if i:
                    self.diagonal(i).wait_send()
                self.over_x(i, 0).wait_send()
                if i == 0:
                    self.over_x(i, 1).wait_send()
            else:
                self.diagonal(i).wait_send()
                self.early(i).wait_send()
                self.late(i).wait_send()
            if i:
                for a in self.halves():
                    self.to_plane(i, a).wait_send()


def slope_of(head):
    return jnp.exp2(jnp.full((1, 1), head + 1, jnp.int32).astype(F32) * (-8.0 / HEADS))


def normalise(h):
    centered = h - jnp.mean(h, -1, keepdims=True)
    inverse = lax.rsqrt(jnp.mean(centered * centered, -1, keepdims=True) + 1e-05)
    return centered * inverse, inverse


def norm_back(d_scaled, scaled, inverse):
    mean1 = jnp.mean(d_scaled, -1, keepdims=True)
    mean2 = jnp.mean(d_scaled * scaled, -1, keepdims=True)
    return inverse * (d_scaled - mean1 - scaled * mean2)


def column_sum(v):
    return jnp.sum(v, axis=0, keepdims=True)


def cdf(gate):
    return 0.5 * (1.0 + lax.erf(gate * 0.7071067811865476))


VECTORS = (
    (0, 96, 0), (96, 48, 2), (144, 48, 3), (192, 48, 4), (240, 384, 8), (624, 48, 5), (672, 48, 6), (720, 48, 7),
)


def spread_vectors(shards, k):
    lane = lax.broadcasted_iota(jnp.int32, (16, 768), 1)
    line = lax.broadcasted_iota(jnp.int32, (16, 768), 0)
    wide = jnp.broadcast_to(shards, (16, 768))
    rows = jnp.zeros((16, 768), F32)
    for start, n, row in VECTORS:
        per = 768 // n
        shift = ((k % per) * n - start + 768) % 768
        here = (lane // n == k % per) & (line == row + k // per)
        rows = jnp.where(here, pltpu.roll(wide, shift, 1), rows)
    return rows


(
    OWN, ALONG, SECOND, THIRD, FOURTH, ARRIVED, DIST, ROWS, QKV, ATTEND, NORM, LOAD, FEED, DOWN, MIDDLE,
    D_DOWN, CHUNK, D_NORM, D_OUT, D_CTX, D_ATTEND, D_QKV, D_TOK, ROW, R_FIRST, R_SECOND, R_THIRD, R_FOURTH, R_ALONG, R_FIFTH, R_PUT,
) = range(31)

ORDER = (
    (OWN, 0), (ALONG, 1, 2), (ALONG, 2, 1), (OWN, 1), (ALONG, 0, 2), (ALONG, 2, 2), (ALONG, 2, 3), (OWN, 4),
    (ALONG, 3, 1), (THIRD, 0, 0), (OWN, 2), (ALONG, 0, 1), (ALONG, 1, 1), (THIRD, 1, 0), (ALONG, 0, 3), (OWN, 5),
    (SECOND, 2, 1), (THIRD, 4, 0), (ALONG, 1, 3), (SECOND, 0, 2), (SECOND, 1, 2), (FOURTH, 0, 0), (SECOND, 0, 1),
    (ALONG, 3, 2), (SECOND, 1, 1), (OWN, 3), (ARRIVED, 0, 0), (SECOND, 1, 3), (ALONG, 3, 3), (ALONG, 4, 1),
    (ALONG, 4, 2), (THIRD, 5, 0), (THIRD, 2, 0), (SECOND, 3, 2), (SECOND, 0, 3), (THIRD, 2, 1), (THIRD, 1, 3),
    (FOURTH, 4, 0), (DIST,), (SECOND, 3, 1), (THIRD, 1, 1), (SECOND, 3, 3), (FOURTH, 1, 0), (FOURTH, 2, 0),
    (THIRD, 0, 1), (THIRD, 0, 2), (SECOND, 2, 2), (ALONG, 4, 3), (FOURTH, 1, 3), (ARRIVED, 1, 0), (THIRD, 1, 2),
    (THIRD, 0, 3), (ALONG, 5, 1), (SECOND, 2, 3), (FOURTH, 2, 1), (FOURTH, 5, 0), (SECOND, 4, 1), (FOURTH, 0, 1),
    (THIRD, 3, 1), (THIRD, 3, 2), (SECOND, 4, 2), (FOURTH, 1, 1), (ARRIVED, 2, 0), (THIRD, 2, 2), (ALONG, 5, 2),
    (FOURTH, 0, 3), (FOURTH, 0, 2), (ARRIVED, 0, 1), (FOURTH, 1, 2), (THIRD, 2, 3), (ARRIVED, 0, 2), (THIRD, 4, 1),
    (ARRIVED, 0, 3), (FOURTH, 3, 2), (ARRIVED, 1, 2), (ROWS,), (THIRD, 3, 3), (ARRIVED, 1, 3), (FOURTH, 2, 2),
    (ARRIVED, 1, 1), (FOURTH, 4, 1), (ALONG, 5, 3), (THIRD, 4, 2), (QKV, 0), (QKV, 1), (THIRD, 3, 0),
    (SECOND, 4, 3), (QKV, 2), (FOURTH, 2, 3), (ARRIVED, 2, 2), (ATTEND, 0), (SECOND, 5, 1), (THIRD, 4, 3),
    (SECOND, 5, 2), (ATTEND, 1), (FOURTH, 3, 1), (FOURTH, 4, 2), (ARRIVED, 4, 1), (ATTEND, 2), (ARRIVED, 2, 3),
    (ATTEND, 3), (ARRIVED, 2, 1), (FOURTH, 4, 3), (FOURTH, 3, 3), (ARRIVED, 4, 0), (THIRD, 5, 1), (ATTEND, 4),
    (SECOND, 5, 3), (ARRIVED, 3, 1), (ATTEND, 5), (THIRD, 5, 2), (FOURTH, 3, 0), (ARRIVED, 3, 3), (ARRIVED, 4, 3),
    (LOAD, 0), (ARRIVED, 5, 0), (FOURTH, 5, 1), (LOAD, 1), (ARRIVED, 4, 2), (NORM,), (ARRIVED, 3, 2),
    (THIRD, 5, 3), (FEED, 0), (ARRIVED, 3, 0), (LOAD, 2), (FEED, 1), (LOAD, 3), (FEED, 2), (ARRIVED, 5, 1),
    (FOURTH, 5, 2), (FOURTH, 5, 3), (FEED, 3), (DOWN, 1), (DOWN, 0), (ARRIVED, 5, 3), (DOWN, 3), (ARRIVED, 5, 2),
    (DOWN, 2), (MIDDLE,), (D_DOWN, 3), (R_FIRST, 0, 3), (D_DOWN, 1), (R_FIRST, 0, 1), (D_DOWN, 0), (D_DOWN, 2),
    (R_FIRST, 0, 2), (R_FIRST, 0, 0), (R_SECOND, 0, 3), (R_SECOND, 0, 1), (CHUNK, 0), (R_SECOND, 0, 2), (CHUNK, 1),
    (R_FIRST, 1, 3), (R_SECOND, 0, 0), (R_THIRD, 0, 3), (CHUNK, 2), (R_SECOND, 1, 3), (R_ALONG, 1, 3, 1),
    (R_THIRD, 0, 2), (R_FIRST, 1, 1), (CHUNK, 3), (D_NORM,), (R_FIRST, 1, 2), (R_THIRD, 0, 1), (R_FOURTH, 0, 3),
    (R_SECOND, 1, 1), (R_ALONG, 0, 3, 0), (R_THIRD, 1, 3), (D_OUT,), (R_FIRST, 1, 0), (R_SECOND, 1, 2), (D_CTX,),
    (R_FIRST, 2, 0), (R_FIRST, 2, 2), (R_ALONG, 1, 2, 1), (R_THIRD, 0, 0), (R_SECOND, 1, 0), (R_FOURTH, 0, 2),
    (D_ATTEND, 0), (D_ATTEND, 1), (R_FIRST, 2, 3), (R_SECOND, 2, 2), (R_SECOND, 2, 3), (R_ALONG, 1, 1, 1),
    (D_ATTEND, 2), (R_FOURTH, 1, 3), (R_ALONG, 0, 2, 0), (R_FIRST, 2, 1), (D_ATTEND, 3), (D_ATTEND, 4),
    (D_ATTEND, 5), (R_FOURTH, 0, 1), (R_ALONG, 1, 3, 0), (ROW, 0), (R_SECOND, 2, 1), (R_FOURTH, 1, 0), (D_QKV, 0),
    (R_THIRD, 1, 2), (D_QKV, 1), (R_THIRD, 1, 1), (ROW, 1), (R_THIRD, 2, 3), (R_THIRD, 2, 1), (D_QKV, 2),
    (R_FIRST, 3, 3), (R_ALONG, 0, 1, 0), (R_FIFTH, 1, 1), (R_FIRST, 3, 2), (R_FOURTH, 1, 2), (R_SECOND, 3, 3),
    (R_SECOND, 2, 0), (R_ALONG, 1, 2, 0), (R_FIRST, 3, 1), (D_TOK,), (R_FOURTH, 0, 0), (R_SECOND, 3, 2),
    (R_FOURTH, 1, 1), (ROW, 2), (R_FIFTH, 0, 0), (R_FOURTH, 2, 3), (R_THIRD, 2, 2), (R_ALONG, 2, 3, 0),
    (R_THIRD, 3, 3), (R_ALONG, 1, 1, 0), (R_SECOND, 3, 1), (R_THIRD, 2, 0), (R_FOURTH, 2, 2), (R_FOURTH, 2, 1),
    (R_ALONG, 2, 2, 0), (R_FIRST, 3, 0), (R_FOURTH, 3, 3), (R_PUT, 0, 0), (R_THIRD, 3, 2), (R_ALONG, 3, 3, 0),
    (R_THIRD, 3, 1), (ROW, 3), (R_FIFTH, 1, 0), (R_SECOND, 3, 0), (R_ALONG, 2, 1, 0), (R_FOURTH, 3, 2),
    (R_FOURTH, 3, 1), (R_FOURTH, 2, 0), (R_ALONG, 3, 2, 0), (R_ALONG, 3, 1, 0), (R_THIRD, 3, 0), (R_FIFTH, 2, 0),
    (R_PUT, 1, 1), (R_FOURTH, 3, 0), (R_FIFTH, 3, 0), (R_PUT, 2, 0), (ROW, 4), (R_PUT, 1, 0), (R_PUT, 3, 0),
)

GATHER_DEEP = (False, False, False, False, True, True)
REDUCE_DEEP = (False, True, False, False)
DOWN_ORDER = tuple(step[1] for step in ORDER if step[0] == D_DOWN)
SHARD_ROWS = (192, 384, 48, 144)


def run_in_order(order, steps):
    for name, *place in order:
        steps[name](*place)


def unit_starts(per_deep, per_flat):
    starts, total = [], 0
    for rows, deep in zip(SHARD_ROWS, REDUCE_DEEP):
        starts.append(total)
        total += rows * (per_deep if deep else per_flat)
    return starts, total


SIDE_STARTS, SIDE_ROWS = unit_starts(5, 8)
CROSS_STARTS, CROSS_ROWS = unit_starts(3, 4)
COLUMN_STARTS, COLUMN_ROWS = unit_starts(12, 6)


def layer_kernel(
    tok, cot, valid, vectors, s_qkv, s_out, s_ff, s_down,
    o_out, o_tok, o_qkv, o_outw, o_ff, o_down, o_rows, w_ff, probs, gu,
    w_bias, w_qkv, w_out, w_down, s_bias, v_rows, v_qkv, v_ctx, v_probs, v_scaled1, v_inv1, v_nl, v_gu, v_ffw,
    v_dn, v_db, v_nlt, v_over, full_a, full_b, both, across, sides, columns, v_sum, v_sums,
    g_sends, g_recvs, locals_, r_sends, r_recvs, row_sends, row_recvs, stages, saves, puts,
):
    y, z, x, c = whereabouts()
    length = tok.shape[0]
    lane = lax.broadcasted_iota(jnp.int32, (1, 128), 1)


    def stage(kind, src, dst, slot):
        return pltpu.make_async_copy(src, dst, stages.at[kind, slot])

    def chunk_of(n):
        return 2 * ((z + 1) % 2 if n < 2 else z % 2) + n % 2

    def ff_rows(n, m):
        return w_ff.at[pl.ds(pl.multiple_of((4 * m + chunk_of(n)) * 1536, 1536), 1536), :]

    def ff_slot(n, m):
        row = (n % 2) * 3072 + m * 1536
        return full_a.at[row : row + 1536, :]

    def ff_stages(n):
        return [stage(m, ff_rows(n, m), ff_slot(n, m), n % 2) for m in (0, 1)]

    def ff_stages_back(n):
        return [stage(m, ff_rows(n, m), v_ffw.at[m], 0) for m in (0, 1)]

    def gu_stages(n):
        return [stage(2 + m, gu.at[m, chunk_of(n)], v_gu.at[n % 2, m], n % 2) for m in (0, 1)]

    def gu_saves(n):
        return [stage(4 + m, v_gu.at[n % 2, m], gu.at[m, chunk_of(n)], n % 2) for m in (0, 1)]

    def side_by_side(ref):
        return jnp.concatenate([ref[:768, :], ref[768:, :]], 1)

    def probs_stage(pair):
        return stage(6, probs.at[pl.ds(2 * pair, 2)], v_probs.at[pair % 2], pair % 2)

    def probs_save(pair):
        return stage(7, v_probs.at[pair % 2], probs.at[pl.ds(2 * pair, 2)], pair % 2)

    def hidden_at(j):
        return pl.ds(pl.multiple_of(j * length, 16), length)


    g = [
        Gather(0, s_bias, w_bias, 16, 16, 0, False, GATHER_DEEP[0], g_sends, g_recvs, locals_),
        Gather(1, s_qkv, w_qkv, 144, 144, 0, False, GATHER_DEEP[1], g_sends, g_recvs, locals_),
        Gather(2, s_out, w_out, 48, 48, 0, False, GATHER_DEEP[2], g_sends, g_recvs, locals_),
        Gather(3, s_ff, w_ff, 384, 768, 0, True, GATHER_DEEP[3], g_sends, g_recvs, locals_),
        Gather(4, s_ff, w_ff, 384, 768, 384, True, GATHER_DEEP[4], g_sends, g_recvs, locals_),
        Gather(5, s_down, w_down, 192, 192, 0, False, GATHER_DEEP[5], g_sends, g_recvs, locals_),
    ]

    def begin_along(t, i):
        for a in g[t].halves():
            if i < 3:
                g[t].to_plane(i, a).start()
            else:

                @pl.when(in_middle(z))
                def _():
                    g[t].to_plane(3, a).start()

    def dist():
        j = lax.broadcasted_iota(jnp.int32, (length, length), 0)
        i = lax.broadcasted_iota(jnp.int32, (length, length), 1)
        v_scaled1[:, :length] = jnp.where(j < valid[0], jnp.abs(i - j).astype(F32), 1e33)

    def rows():
        total = w_bias[0:16, :].astype(F32)
        for k in range(1, 16):
            total = total + w_bias[16 * k : 16 * k + 16, :].astype(F32)
        v_rows[...] = total

    def project(n):
        part = dot(tok[...], w_qkv[768 * n : 768 * n + 768, :], 1, 1)
        if n == 0:
            part = (part + v_rows[0:1, :]).astype(BF).astype(F32) * 0.125
        if n == 2:
            part = part + v_rows[1:2, :]
        v_qkv[:, 768 * n : 768 * n + 768] = part.astype(BF)

    def attend(pair):
        col = 128 * pair
        if pair > 1:
            probs_save(pair - 2).wait()
        q_pair = v_qkv[:, col : col + 128]
        k_pair = v_qkv[:, 768 + col : 768 + col + 128]
        v_pair = v_qkv[:, 1536 + col : 1536 + col + 128]
        results = []
        for hh in range(2):
            mine = (lane < 64) if hh == 0 else (lane >= 64)
            scores = dot(k_pair, jnp.where(mine, q_pair, jnp.zeros((), BF)), 1, 1)
            scores = scores - slope_of(2 * pair + hh) * v_scaled1[:, :length]
            expo = jnp.exp(scores - jnp.max(scores, axis=0, keepdims=True)).astype(BF)
            v_probs[pair % 2, hh] = expo
            results.append(dot(expo, jnp.where(mine, v_pair, jnp.ones((), BF)), 0, 0))
        inverse = 1.0 / pltpu.roll(jnp.where(lane < 64, results[1], results[0]), 64, 1)
        v_over[:, col : col + 128] = inverse.astype(v_over.dtype)
        v_ctx[:, col : col + 128] = (jnp.where(lane < 64, results[0], results[1]) * inverse).astype(BF)
        probs_save(pair).start()

    def first_norm():
        h1 = dot(v_ctx[...], w_out[...], 1, 0) + v_rows[2:3, :] + tok[...].astype(F32)
        scaled1, inverse1 = normalise(h1)
        v_scaled1[...] = scaled1
        v_inv1[...] = jnp.broadcast_to(inverse1, v_inv1.shape)
        normed = scaled1 * v_rows[3:4, :] + v_rows[4:5, :]
        v_dn[...] = normed + v_rows[5:6, :]
        v_nl[...] = normed.astype(BF)
        v_nlt[...] = normed.astype(BF).T

    def load(n):
        for copy in ff_stages(n):
            copy.start()

    load_cot = pltpu.make_async_copy(cot, v_nl, saves.at[2])

    def feed(n):
        s = n % 2
        j = chunk_of(n)
        if n > 1:
            for copy in gu_saves(n - 2):
                copy.wait()
        for copy in ff_stages(n):
            copy.wait()
        gate = dot(v_nl[...], side_by_side(ff_slot(n, 0)), 1, 0) + v_rows[pl.ds(8 + j, 1), :]
        up = dot(v_nl[...], side_by_side(ff_slot(n, 1)), 1, 0) + v_rows[pl.ds(12 + j, 1), :]
        below = cdf(gate)
        density = jnp.exp(-0.5 * gate * gate) * 0.3989422804014327
        active = gate * below
        v_gu[s, 0] = active.astype(BF)
        v_gu[s, 1] = (up * (below + gate * density)).astype(BF)
        hidden = (active * up).astype(BF)
        full_b[hidden_at(2 * j), :] = hidden[:, :384]
        full_b[hidden_at(2 * j + 1), :] = hidden[:, 384:]
        for copy in gu_saves(n):
            copy.start()
        if n == 3:
            load_cot.start()

    def down(i):
        j = plane_at(z, i)
        hidden = jnp.concatenate([full_b[hidden_at(2 * j), :], full_b[hidden_at(2 * j + 1), :]], 1)
        v_dn[...] += dot(hidden, w_down[pl.ds(pl.multiple_of(j * 768, 768), 768), :], 1, 0)

    save_out = pltpu.make_async_copy(v_nl, o_out, saves.at[0])
    save_tok = pltpu.make_async_copy(v_ctx, o_tok, saves.at[1])

    def second_norm():
        for n in (2, 3):
            for copy in gu_saves(n):
                copy.wait()
        for n in (0, 1):
            for copy in gu_stages(n):
                copy.start()
        scaled2, inverse2 = normalise(v_dn[...])
        load_cot.wait()
        grad = v_nl[...].astype(F32)
        d_h2 = norm_back(grad * v_rows[6:7, :], scaled2, inverse2)
        v_dn[...] = d_h2
        v_db[...] = d_h2.astype(BF)
        v_nl[...] = (scaled2 * v_rows[6:7, :] + v_rows[7:8, :]).astype(BF)
        save_out.start()
        v_sum[5:6, :] = column_sum(d_h2.astype(BF).astype(F32))
        v_sum[6:7, :] = column_sum(grad * scaled2)
        v_sum[7:8, :] = column_sum(grad)


    def at_down(plane, x_, c_, h):
        return h * 3072 + index(plane, x_, c_) * 192

    def at_ff(plane, x_, c_, h):
        return (plane // 2) * 3072 + index(0, x_, c_) * 768 + h * 384

    def at_out(plane, x_, c_, h):
        return h * 768 + index(plane, x_, c_) * 48

    def at_qkv(plane, x_, c_, h):
        return 1536 + h * 2304 + index(plane, x_, c_) * 144

    def reduce_of(t, at, full):
        return Reduce(
            t, sum(SHARD_ROWS[:t]), SHARD_ROWS[t], REDUCE_DEEP[t],
            (SIDE_STARTS[t], CROSS_STARTS[t], COLUMN_STARTS[t]),
            at, full, both, across, sides, columns, r_sends, r_recvs,
        )

    r_down = reduce_of(0, at_down, full_a)
    r_ff1 = reduce_of(1, at_ff, full_b)
    r_ff2 = reduce_of(1, at_ff, full_a)
    r_out = reduce_of(2, at_out, full_b)
    r_qkv = reduce_of(3, at_qkv, full_b)

    def reducer(t, i):
        return (r_down, r_ff1 if i % 2 else r_ff2, r_out, r_qkv)[t]

    def d_down(i):
        for s in range(2):
            j = 2 * plane_at(z, i) + s
            part = dot(full_b[hidden_at(j), :], v_db[...], 0, 0)
            row = pl.multiple_of(j * 384, 384)
            full_a[pl.ds(row, 384), :] = part[:, :384].astype(BF)
            full_a[pl.ds(3072 + row, 384), :] = part[:, 384:].astype(BF)

    def chunk(n):
        s = n % 2
        j = chunk_of(n)
        if n == 0:
            for pair in (4, 5):
                probs_save(pair).wait()
            probs_stage(0).start()
            probs_stage(1).start()
        for copy in ff_stages_back(n):
            copy.start()
        for copy in gu_stages(n):
            copy.wait()
        d_hid = dot(v_db[...], w_down[pl.ds(pl.multiple_of(j * 768, 768), 768), :], 1, 1)
        d_up = (d_hid * v_gu[s, 0].astype(F32)).astype(BF)
        d_gate = (d_hid * v_gu[s, 1].astype(F32)).astype(BF)
        full = full_b if n < 2 else full_a
        for m, d in enumerate((d_gate, d_up)):
            part = dot(v_nlt[...], d, 1, 0).astype(BF)
            row = 3072 * m + 1536 * (n % 2)
            full[row : row + 768, :] = part[:, :384]
            full[row + 768 : row + 1536, :] = part[:, 384:]
            v_sum[pl.ds(8 + 4 * m + j, 1), :] = column_sum(d.astype(F32))
        for copy in ff_stages_back(n):
            copy.wait()
        back = dot(d_gate, side_by_side(v_ffw.at[0]), 1, 1) + dot(d_up, side_by_side(v_ffw.at[1]), 1, 1)
        v_dn[...] += back
        if n < 2:
            for copy in gu_stages(n + 2):
                copy.start()

    def first_norm_back():
        d_normed = v_dn[...]
        scaled = v_scaled1[...]
        v_sum[3:4, :] = column_sum(d_normed * scaled)
        v_sum[4:5, :] = column_sum(d_normed)
        d_h1 = norm_back(d_normed * v_rows[3:4, :], scaled, v_inv1[:, 0:1])
        v_dn[...] = d_h1
        v_db[...] = d_h1.astype(BF)
        v_sum[2:3, :] = column_sum(d_h1.astype(BF).astype(F32))

    def d_out():
        part = dot(v_ctx[...], v_db[...], 0, 0)
        full_b[0:768, :] = part[:, :384].astype(BF)
        full_b[768:1536, :] = part[:, 384:].astype(BF)

    v_dctx = v_nl

    def d_context():
        save_out.wait()
        v_dctx[...] = (dot(v_db[...], w_out[...], 1, 1) * v_over[...].astype(F32)).astype(BF)

    def attend_back(pair):
        col = 128 * pair
        probs_stage(pair).wait()
        q_pair = v_qkv[:, col : col + 128]
        k_pair = v_qkv[:, 768 + col : 768 + col + 128]
        v_pair = v_qkv[:, 1536 + col : 1536 + col + 128]
        d_pair = v_dctx[:, col : col + 128]
        product = d_pair.astype(F32) * v_ctx[:, col : col + 128].astype(F32)
        high = product.astype(BF)
        low = (product - high.astype(F32)).astype(BF)
        d_q, d_k, d_v = [], [], []
        for hh in range(2):
            mine = (lane < 64) if hh == 0 else (lane >= 64)
            head = jnp.broadcast_to(mine.astype(BF), (16, 128))
            inner = (dot(head, high, 1, 1) + dot(head, low, 1, 1))[0:1, :]
            d_head = jnp.where(mine, d_pair, jnp.zeros((), BF))
            d_probs = dot(v_pair, d_head, 1, 1)
            expo = v_probs[pair % 2, hh]
            d_scores = (expo.astype(F32) * (d_probs - inner)).astype(BF)
            d_v.append(dot(expo, d_head, 1, 0))
            d_k.append(dot(d_scores, jnp.where(mine, q_pair, jnp.zeros((), BF)), 1, 0))
            d_q.append(dot(k_pair, d_scores, 0, 0))
        upper = lax.broadcasted_iota(jnp.int32, (128, 1), 0) < 64
        v_qkv[:, col : col + 128] = (jnp.where(upper, d_q[0], d_q[1]) * 0.125).astype(BF).T
        v_qkv[:, 768 + col : 768 + col + 128] = (d_k[0] + d_k[1]).astype(BF)
        v_qkv[:, 1536 + col : 1536 + col + 128] = (d_v[0] + d_v[1]).astype(BF)
        if pair < 4:
            probs_stage(pair + 2).start()
        if pair == 5:
            v_sum[0:1, :] = column_sum(v_qkv[:, 0:768].astype(F32))
            v_sum[1:2, :] = column_sum(v_qkv[:, 1536:2304].astype(F32))

    def d_qkv_weight(n):
        part = dot(v_qkv[:, 768 * n : 768 * n + 768], tok[...], 0, 0)
        full_b[1536 + 768 * n : 2304 + 768 * n, :] = part[:, :384].astype(BF)
        full_b[3840 + 768 * n : 4608 + 768 * n, :] = part[:, 384:].astype(BF)

    def d_tokens():
        v_ctx[...] = (dot(v_qkv[...], w_qkv[...], 1, 0) + v_dn[...]).astype(BF)
        save_tok.start()

    def row_copy(n):
        device = (
            (y, index(z, x, 1 - c)), (y, index(z, 1 - x, c)), (1 - y, index(z, x, c)),
            *[(y, index(plane_at(z, i), x, c)) for i in (1, 2, 3)],
        )[n]
        return pltpu.make_async_remote_copy(
            src_ref=v_sum,
            dst_ref=v_sums.at[n],
            send_sem=row_sends.at[n],
            recv_sem=row_recvs.at[n],
            device_id=device,
            device_id_type=MESH,
        )

    def row_step(n):
        if 1 <= n <= 3:
            row_copy(n - 1).wait()
            v_sum[...] = v_sum[...] + v_sums[n - 1]
        if n < 3:
            row_copy(n).start()
        if n == 3:
            for m in (3, 4, 5):
                row_copy(m).start()
        if n == 4:
            for m in (3, 4, 5):
                row_copy(m).wait()
            o_rows[...] = v_sum[...] + v_sums[3] + v_sums[4] + v_sums[5]

    outs = (o_down, o_ff, o_outw, o_qkv)
    placed = []

    barrier = pltpu.get_barrier_semaphore()
    friends = greet(barrier)
    s_bias[...] = spread_vectors(vectors[...], index(z, x, c)).astype(BF)
    pl.semaphore_wait(barrier, friends)
    run_in_order(
        ORDER,
        {
            OWN: lambda t: g[t].begin_plane(),
            ALONG: begin_along,
            SECOND: lambda t, i: g[t].second(i),
            THIRD: lambda t, i: g[t].third(i),
            FOURTH: lambda t, i: g[t].fourth(i),
            ARRIVED: lambda t, i: g[t].arrived(i),
            DIST: dist,
            ROWS: rows,
            QKV: project,
            ATTEND: attend,
            NORM: first_norm,
            LOAD: load,
            FEED: feed,
            DOWN: down,
            MIDDLE: second_norm,
            D_DOWN: d_down,
            CHUNK: chunk,
            D_NORM: first_norm_back,
            D_OUT: d_out,
            D_CTX: d_context,
            D_ATTEND: attend_back,
            D_QKV: d_qkv_weight,
            D_TOK: d_tokens,
            ROW: row_step,
            R_FIRST: lambda t, i: reducer(t, i).first(i),
            R_SECOND: lambda t, i: reducer(t, i).second(i),
            R_THIRD: lambda t, i: reducer(t, i).third(i),
            R_FOURTH: lambda t, i: reducer(t, i).fourth(i),
            R_ALONG: lambda t, i, a: reducer(t, i).along(i, a),
            R_FIFTH: lambda t, a: reducer(t, 0).fifth(a),
            R_PUT: lambda t, a: placed.extend(reducer(t, 0).put(a, outs[t], puts)),
        },
    )
    save_tok.wait()
    for copy in placed:
        copy.wait()
    for t in range(6):
        g[t].finish()
    for t in range(4):
        reducer(t, 0).finish()


def finish_kernel(tok, qkv, out, ff, down, rows, fwd, *outs):
    o_fwd, o_tok, o_qkv, o_qv, o_out, o_outb, o_g1, o_s1, o_ff, o_ffb, o_down, o_downb, o_g2, o_s2 = outs
    k = lax.axis_index("fsdp")
    o_fwd[...] = fwd[...]
    o_tok[...] = tok[...]
    for h in (0, 1):
        o_qkv[:, 384 * h : 384 * h + 384] = qkv[h].astype(F32)
        o_out[:, 384 * h : 384 * h + 384] = out[h].astype(F32)
        o_down[:, 384 * h : 384 * h + 384] = down[h].astype(F32)
        o_ff[384 * h : 384 * h + 384, :] = ff[h].astype(F32)
    by_vector = (o_qv, o_outb, o_g1, o_s1, o_ffb, o_downb, o_g2, o_s2)
    for ref, (_, n, row) in zip(by_vector, VECTORS):
        per = 768 // n
        line = rows[pl.ds(row + k // per, 1), :]
        moved = pltpu.roll(jnp.broadcast_to(line, (8, 768)), ((768 - (k % per) * n) % 768), 1)
        ref[...] = moved[0, 0:n]


def fused_on_device(
    tokens,
    qkv_weight,
    qv_bias,
    out_weight,
    out_bias,
    norm1_gain,
    norm1_shift,
    ff_weight,
    ff_bias,
    down_weight,
    down_bias,
    norm2_gain,
    norm2_shift,
    pair_length,
    cotangent,
):
    length, width = tokens.shape
    parts = (qv_bias, out_bias, norm1_gain, norm1_shift, ff_bias, down_bias, norm2_gain, norm2_shift)
    vectors = jnp.zeros((width,), F32)
    for part, (start, n, _) in zip(parts, VECTORS):
        vectors = vectors + jnp.pad(part.astype(F32), (start, width - start - n))
    vectors = vectors.reshape(1, width)
    in_vmem = pl.BlockSpec(memory_space=pltpu.VMEM)
    in_smem = pl.BlockSpec(memory_space=pltpu.SMEM)
    anywhere = pl.BlockSpec(memory_space=pl.ANY)
    struct = jax.ShapeDtypeStruct
    vmem = pltpu.VMEM
    dma = pltpu.SemaphoreType.DMA
    output, d_tokens, d_qkv, d_out, d_ff, d_down, d_rows = pl.pallas_call(
        layer_kernel,
        name="layer",
        out_shape=[
            struct((length, width), BF),
            struct((length, width), BF),
            struct((2, 144, 384), BF),
            struct((2, 48, 384), BF),
            struct((2, 384, 384), BF),
            struct((2, 192, 384), BF),
            struct((16, width), F32),
            struct((12288, 384), BF),
            struct((HEADS, length, length), BF),
            struct((2, 4, length, 768), BF),
        ],
        in_specs=[in_vmem, anywhere, in_smem, in_vmem] + [anywhere] * 4,
        out_specs=[anywhere] * 6 + [in_vmem] + [anywhere] * 3,
        scratch_shapes=[
            vmem((256, width), BF),
            vmem((2304, width), BF),
            vmem((width, width), BF),
            vmem((3072, width), BF),
            vmem((16, width), BF),
            vmem((16, width), F32),
            vmem((length, 2304), BF),
            vmem((length, width), BF),
            vmem((2, 2, length, length), BF),
            vmem((length, width), F32),
            vmem((length, 128), F32),
            vmem((length, width), BF),
            vmem((2, 2, length, 768), BF),
            vmem((2, 1536, 384), BF),
            vmem((length, width), F32),
            vmem((length, width), BF),
            vmem((width, length), BF),
            vmem((length, width), BF),
            vmem((6144, 384), BF),
            vmem((6144, 384), BF),
            vmem((768 * 16, 384), BF),
            vmem((CROSS_ROWS, 384), BF),
            vmem((SIDE_ROWS, 384), BF),
            vmem((COLUMN_ROWS, 384), BF),
            vmem((16, width), F32),
            vmem((6, 16, width), F32),
            dma((6, Gather.SLOTS)),
            dma((6, Gather.SLOTS)),
            dma((6,)),
            dma((4, Reduce.SLOTS)),
            dma((4, Reduce.SLOTS)),
            dma((6,)),
            dma((6,)),
            dma((8, 2)),
            dma((3,)),
            dma((4, 2)),
        ],
        compiler_params=pltpu.CompilerParams(
            collective_id=0, has_side_effects=True, vmem_limit_bytes=63 * 2**20
        ),
    )(tokens, cotangent, pair_length, vectors, qkv_weight.T, out_weight, ff_weight, down_weight)[:7]

    def vector(n):
        return struct((n,), F32)

    full = [struct(s, F32) for s in ((144, width), (48, width), (768, 384), (192, width))]
    results = pl.pallas_call(
        finish_kernel,
        name="finish",
        out_shape=[
            struct((length, width), BF), struct((length, width), BF), full[0], vector(96), full[1], vector(48),
            vector(48), vector(48), full[2], vector(384), full[3], vector(48), vector(48), vector(48),
        ],
        in_specs=[in_vmem] * 7,
        out_specs=[in_vmem] * 14,
    )(d_tokens, d_qkv, d_out, d_ff, d_down, d_rows, output)
    results = list(results)
    results[2] = results[2].T
    return tuple(results)


def solution(mesh):
    in_specs = (
        P(("rep", "fsdp"), None),
        P(None, "fsdp"),
        P("fsdp"),
        P("fsdp", None),
        P("fsdp"),
        P("fsdp"),
        P("fsdp"),
        P(None, "fsdp"),
        P("fsdp"),
        P("fsdp", None),
        P("fsdp"),
        P("fsdp"),
        P("fsdp"),
        P(("rep", "fsdp")),
        P(("rep", "fsdp"), None),
    )
    out_specs = (
        P(("rep", "fsdp"), None),
        P(("rep", "fsdp"), None),
        P(None, "fsdp"),
        P("fsdp"),
        P("fsdp", None),
        P("fsdp"),
        P("fsdp"),
        P("fsdp"),
        P(None, "fsdp"),
        P("fsdp"),
        P("fsdp", None),
        P("fsdp"),
        P("fsdp"),
        P("fsdp"),
    )
    planes = mesh.shape["rep"] == 2 and mesh.shape["fsdp"] == 16
    return jax.shard_map(
        fused_on_device if planes else plain_on_device, mesh=mesh, in_specs=in_specs, out_specs=out_specs, check_vma=False
    )
```
